32 devices in a mesh: row: 4 (over y, x), col: 8 (over z, core).
Axes of the slice: x: 2, y: 2, z: 4, core: 2. Of those that a mesh axis runs over, the one named last changes fastest.
Arguments:
- residual: bfloat16 [256, 5120], P('row', 'col'), may hold values from -6 to 6
- attn_gain: float32 [5120], P('col'), may hold values from 0.1 to 1.9
- w_query: bfloat16 [5120, 5120], P('col', 'row'), may hold values from -0.078125 to 0.078125
- w_key: bfloat16 [5120, 1024], P('col', 'row'), may hold values from -0.078125 to 0.078125
- w_value: bfloat16 [5120, 1024], P('col', 'row'), may hold values from -0.078125 to 0.078125
- w_out: bfloat16 [5120, 5120], P('row', 'col'), may hold values from -0.078125 to 0.078125
- mlp_gain: float32 [5120], P('col'), may hold values from 0.1 to 1.9
- w_gate: bfloat16 [2, 5120, 13824], P(None, 'col', 'row'), may hold values from -0.078125 to 0.078125
- w_up: bfloat16 [2, 5120, 13824], P(None, 'col', 'row'), may hold values from -0.078125 to 0.078125
- w_down: bfloat16 [2, 13824, 5120], P(None, 'row', 'col'), may hold values from -0.0546875 to 0.0546875
- final_gain: float32 [5120], P('col'), may hold values from 0.1 to 1.9
- w_head: bfloat16 [5120, 81920], P(None, ('row', 'col')), may hold values from -32 to 32
- seq_lengths: int32 [8], replicated, may hold values from 1 to 64, 256 in all
- targets: int32 [256], replicated, may hold values from 0 to 81919
Outputs:
- seq_diff: float32 [8], replicated
The draws below stay inside these ranges and needn't reach their ends.
Inputs may be any that keep to these rules, and one draw needn't show every extreme that they name: `seq_lengths`: the lengths sum to 256 and the largest is exactly 64.
All inputs are finite; a program needn't handle non-finite values.
Results may differ from the reference program's by a relative error of at most 0.02.
Values may be sent and summed in bfloat16 or wider, within the bound.
No kernel may reach another device: no remote copies, remote signals or barrier semaphores. Data moves between devices by JAX's collectives and lax.ppermute only.
A program may use at most 128 MiB of HBM per device.

```python
import math
import jax
import jax.numpy as jnp
import numpy as np
from jax import lax

D = 5120
HEADS = 40
KV_HEADS = 8
HEAD_DIM = 128
FF = 13824
VOCAB = 81920
TOKENS = 256
SEQS = 8


def draw_w_head(key, part):
    base_key = jax.random.fold_in(key, 11)
    spread = 3.0 / math.sqrt(D)
    base = jnp.clip(jax.random.normal(base_key, (D, VOCAB), jnp.float32), -6.0, 6.0) * spread
    return base.astype(jnp.bfloat16)


def touch_ends(array, rng, smallest, largest):
    extent = array.shape
    place = [jax.random.randint(jax.random.fold_in(rng, axis), (), 0, extent[axis]) for axis in range(len(extent))]
    array = array.at[tuple(place)].set(smallest)
    longest = extent.index(max(extent))
    place[longest] = (place[longest] + 1) % extent[longest]
    return array.at[tuple(place)].set(largest)


def shard_levels(own_key, extent, pieces, smallest, largest):
    def one(position, parts):
        heights = jax.random.uniform(jax.random.fold_in(jax.random.fold_in(own_key, 6), position), (parts,), jnp.float32, smallest / len(pieces), largest / len(pieces))
        return jnp.repeat(jnp.exp(heights), extent[position] // parts).reshape((-1,) + (1,) * (len(extent) - position - 1))

    level = one(*pieces[0])
    for cut in pieces[1:]:
        level = level * one(*cut)
    return level


def skewed_wide(key, shape, count, skew):
    portions = [min(1 << octave, count + 1 - (1 << octave)) * (1 << 20) // math.isqrt((1 << octave) ** skew) + 1 for octave in range((count + 1).bit_length()) if 1 << octave <= count]
    scale = 1 + sum(portions) // (1 << 30)
    table = np.cumsum(np.array([max(1, weight // scale) for weight in portions]))
    ticket = jax.random.randint(jax.random.fold_in(key, 1), shape, 0, int(table[len(portions) - 1]))
    start = jnp.left_shift(1, jnp.searchsorted(jnp.asarray(table, jnp.int32), ticket, side="right").astype(jnp.int32))
    standing = start - 1 + jax.random.randint(jax.random.fold_in(key, 4), shape, 0, 1 << 30) % jnp.minimum(start, count + 1 - start)
    return jax.random.permutation(jax.random.fold_in(key, 2), count)[standing].astype(jnp.int32)


def length_profile(number_of, total, most, lean):
    weights = [(1 << 20) // math.isqrt(standing ** lean) + 1 for standing in range(2, number_of + 1)]
    spare, given = total - most - (number_of - 1), [1] * (number_of - 1)
    while spare > 0:
        free = [i for i in range(number_of - 1) if given[i] < most]
        whole, left = sum([weights[i] for i in free]), spare
        for i in free:
            addition = min(most - given[i], max(1, left * weights[i] // whole), spare)
            given[i] = given[i] + addition
            spare = spare - addition
    return np.array([most] + given)


def uneven_parts(own_key, amount, total, limit, slope):
    if amount == 2:
        one = jax.random.randint(own_key, (), max(1, total - limit), min(limit, total - 1) + 1)
        return jnp.stack([one, total - one])
    sizes = jnp.asarray(length_profile(amount, total, limit, slope), jnp.int32)
    pairs = (amount - 1) // 2
    giver, receiver = sizes[1:1 + 2 * pairs:2], sizes[2:2 + 2 * pairs:2]
    slack = jnp.minimum(giver - 1, limit - receiver)
    moved = jax.random.randint(jax.random.fold_in(own_key, 1), (pairs,), 0, 1 << 20) % (slack + 1)
    sizes = sizes.at[1:1 + 2 * pairs:2].set(giver - moved).at[2:2 + 2 * pairs:2].set(receiver + moved)
    return sizes[jax.random.permutation(jax.random.fold_in(own_key, 2), amount)]


def centred(stream_key, dims, width, most, shards=(), kind=jnp.bfloat16):
    drawn = jax.random.normal(stream_key, dims, jnp.float32) * width
    if len(shards) > 0:
        drawn = shard_levels(stream_key, dims, shards, -0.22, 0.18) * drawn
    return jnp.clip(drawn, min=-most, max=most).astype(kind)


def setup_inputs(seed: int = 0) -> dict:
    arg_keys = jax.random.split(jax.random.key(seed), 15)
    residual = centred(arg_keys[0], (TOKENS, D), 1.0, 6.0, ((0, 4), (1, 8)))
    attn_gain = jnp.clip(1.0 + 0.18 * jax.random.normal(arg_keys[1], (D,), jnp.float32), 0.1, 1.9)
    w_query = centred(arg_keys[2], (D, HEADS * HEAD_DIM), D ** -0.5, 0.078125, ((0, 8), (1, 4)))
    w_key = centred(arg_keys[3], (D, KV_HEADS * HEAD_DIM), D ** -0.5, 0.078125, ((0, 8), (1, 4)))
    w_value = centred(arg_keys[4], (D, KV_HEADS * HEAD_DIM), D ** -0.5, 0.078125, ((0, 8), (1, 4)))
    w_out = centred(arg_keys[5], (HEADS * HEAD_DIM, D), (HEADS * HEAD_DIM) ** -0.5, 0.078125, ((0, 4), (1, 8)))
    mlp_gain = jnp.clip(1.0 + 0.18 * jax.random.normal(arg_keys[6], (D,), jnp.float32), 0.1, 1.9)
    w_gate = centred(arg_keys[7], (2, D, FF), D ** -0.5, 0.078125, ((1, 8), (2, 4)))
    w_up = centred(arg_keys[8], (2, D, FF), D ** -0.5, 0.078125, ((1, 8), (2, 4)))
    w_down = centred(arg_keys[9], (2, FF, D), FF ** -0.5, 0.0546875, ((1, 4), (2, 8)))
    final_gain = jnp.clip(1.0 + 0.18 * jax.random.normal(arg_keys[10], (D,), jnp.float32), 0.1, 1.9)
    w_head = draw_w_head(jax.random.fold_in(arg_keys[14], 71), 0)
    seq_lengths = uneven_parts(arg_keys[12], SEQS, TOKENS, TOKENS // 4, 2).astype(jnp.int32)
    targets = touch_ends(skewed_wide(arg_keys[13], (TOKENS,), VOCAB, 2), jax.random.fold_in(arg_keys[13], 3), 0, VOCAB - 1).astype(jnp.int32)
    return dict(residual=residual, attn_gain=attn_gain, w_query=w_query, w_key=w_key, w_value=w_value, w_out=w_out, mlp_gain=mlp_gain, w_gate=w_gate, w_up=w_up, w_down=w_down, final_gain=final_gain, w_head=w_head, seq_lengths=seq_lengths, targets=targets)


EPSILON = 1e-06
ROPE_BASE = 1000000.0
MASKED = -1e+30

def normalize(features, gain_vector):
    mean_square = lax.optimization_barrier(jnp.mean(features * features, axis=-1, keepdims=True))
    return features * lax.rsqrt(mean_square + EPSILON) * gain_vector[None, :]

def sequence_layout(seq_lengths, token_index):
    ends_at = jnp.cumsum(seq_lengths).astype(jnp.int32)
    before = ends_at[None, :] <= token_index[:, None]
    segment = lax.optimization_barrier(jnp.sum(before.astype(jnp.int32), axis=1)).astype(jnp.int32)
    starts_at = lax.optimization_barrier(jnp.sum(jnp.where(before, seq_lengths[None, :], 0), axis=1)).astype(jnp.int32)
    return (segment, (token_index - starts_at).astype(jnp.float32))

def angles_for(positions, head_width):
    exponent = jnp.arange(head_width // 2, dtype=jnp.float32) * 2.0 / head_width
    frequency = ROPE_BASE ** (-exponent)
    return positions[:, None] * frequency[None, :]

def rotate(features, angles):
    half_width = features.shape[-1] // 2
    lower_half = features[..., :half_width]
    upper_half = features[..., half_width:]
    cosine = jnp.cos(angles)[:, None, :]
    sine_part = jnp.sin(angles)[:, None, :]
    return jnp.concatenate([lower_half * cosine - upper_half * sine_part, upper_half * cosine + lower_half * sine_part], axis=-1)

def reference(residual, attn_gain, w_query, w_key, w_value, w_out, mlp_gain, w_gate, w_up, w_down, final_gain, w_head, seq_lengths, targets):
    stream_in = residual.astype(jnp.float32)
    normed = normalize(stream_in, attn_gain).astype(jnp.bfloat16)
    token_index = jnp.arange(TOKENS, dtype=jnp.int32)
    segment, positions = sequence_layout(seq_lengths, token_index)
    angles = angles_for(positions, HEAD_DIM)
    queries = rotate(jnp.dot(normed, w_query, preferred_element_type=jnp.float32).reshape(TOKENS, HEADS, HEAD_DIM), angles).astype(jnp.bfloat16)
    keys_all = rotate(jnp.dot(normed, w_key, preferred_element_type=jnp.float32).reshape(TOKENS, KV_HEADS, HEAD_DIM), angles).astype(jnp.bfloat16)
    values_all = jnp.dot(normed, w_value, preferred_element_type=jnp.float32).astype(jnp.bfloat16).reshape(TOKENS, KV_HEADS, HEAD_DIM)
    group_size = HEADS // KV_HEADS
    grouped = queries.reshape(TOKENS, KV_HEADS, group_size, HEAD_DIM).transpose(1, 2, 0, 3)
    allowed = (segment[:, None] == segment[None, :]) & (token_index[None, :] <= token_index[:, None])

    def one_head(operands):
        query_block, key_block, value_block = operands
        scores = jnp.einsum('gqd,kd->gqk', query_block.astype(jnp.float32), key_block.astype(jnp.float32)) * HEAD_DIM ** (-0.5)
        scores = jnp.where(allowed[None], scores, MASKED)
        top_value = lax.optimization_barrier(jnp.max(scores, axis=-1, keepdims=True))
        weights = jnp.exp(scores - top_value)
        weights = (weights / lax.optimization_barrier(jnp.sum(weights, axis=-1, keepdims=True))).astype(jnp.bfloat16)
        return jnp.einsum('gqk,kd->gqd', weights.astype(jnp.float32), value_block.astype(jnp.float32))
    attended = lax.map(one_head, (grouped, keys_all.transpose(1, 0, 2), values_all.transpose(1, 0, 2)))
    attended = attended.astype(jnp.bfloat16).transpose(2, 0, 1, 3).reshape(TOKENS, HEADS * HEAD_DIM)
    projected = jnp.dot(attended, w_out, preferred_element_type=jnp.float32)
    stream = lax.optimization_barrier((stream_in + projected).astype(jnp.bfloat16))
    stream_f = stream.astype(jnp.float32)
    mlp_in = normalize(stream_f, mlp_gain).astype(jnp.bfloat16)
    logprobs = []
    for member in range(2):
        gate = jnp.dot(mlp_in, w_gate[member], preferred_element_type=jnp.float32)
        upward = jnp.dot(mlp_in, w_up[member], preferred_element_type=jnp.float32)
        hidden = (jax.nn.silu(gate) * upward).astype(jnp.bfloat16)
        output_f = stream_f + jnp.dot(hidden, w_down[member], preferred_element_type=jnp.float32)
        final_state = normalize(output_f, final_gain).astype(jnp.bfloat16)
        logits = jnp.dot(final_state, w_head, preferred_element_type=jnp.float32)
        top_value = lax.optimization_barrier(jnp.max(logits, axis=1))
        log_total = top_value + jnp.log(lax.optimization_barrier(jnp.sum(jnp.exp(logits - top_value[:, None]), axis=1)))
        picked = jnp.take_along_axis(logits, targets[:, None].astype(jnp.int32), axis=1)[:, 0]
        logprobs.append(picked - log_total)
    difference = logprobs[0] - logprobs[1]
    one_hot = (segment[:, None] == jnp.arange(SEQS, dtype=jnp.int32)[None, :]).astype(jnp.float32)
    seq_sums = jnp.dot(difference, one_hot, precision=lax.Precision.HIGHEST)
    return seq_sums / seq_lengths.astype(jnp.float32)
```

```python
import functools

import jax
import jax.numpy as jnp
from jax import lax
from jax.experimental import pallas as pl
from jax.experimental.pallas import tpu as pltpu
from jax.sharding import PartitionSpec as P

D = 5120
HEAD_DIM = 128
SEQS = 8
LONGEST = 64

EPSILON = 1e-06
ROPE_BASE = 1000000.0
MASKED = -1e30
BF16 = jnp.bfloat16
F32 = jnp.float32
MIB = 1 << 20

VMEM = pl.BlockSpec(memory_space=pltpu.VMEM)
SMEM = pl.BlockSpec(memory_space=pltpu.SMEM)


def params(mib):
    return pltpu.CompilerParams(vmem_limit_bytes=mib * MIB)


def cost(flops, byte_count):
    return pl.CostEstimate(flops=flops, bytes_accessed=byte_count, transcendentals=0)


def row_xor(x, mask):
    count = lax.axis_size("row")
    return lax.ppermute(x, "row", [(i, i ^ mask) for i in range(count)])


def col_xor(x, mask):
    count = lax.axis_size("col")
    return lax.ppermute(x, "col", [(i, i ^ mask) for i in range(count)])


def tree_sum(values):
    values = list(values)
    while len(values) > 1:
        values = [values[i] + values[i + 1] for i in range(0, len(values), 2)]
    return values[0]


def col_sum(x):
    return tree_sum([x] + [col_xor(x, j) for j in range(1, lax.axis_size("col"))])


def sequence_layout(seq_lengths, token_index):
    ends_at = jnp.cumsum(seq_lengths)
    before = ends_at[None, :] <= token_index[:, None]
    segment = jnp.sum(before.astype(jnp.int32), axis=1)
    starts_at = jnp.sum(jnp.where(before, seq_lengths[None, :], 0), axis=1)
    return (segment, (token_index - starts_at).astype(F32))


def assemble(offsets, blocks, gain, x_ref, unit):
    step = 0
    for block in blocks:
        for first in range(0, block.shape[0], unit):
            rows = block[first : first + unit, :].astype(F32) * gain[...]
            place = pl.multiple_of(offsets[step], unit)
            x_ref[pl.ds(place, unit), :] = rows.astype(BF16)
            step += 1


def qkv_kernel(unit, count, offsets, *refs):
    blocks, (gain, wq, wk, wv, keep, send, x_ref) = refs[:count], refs[count:]
    assemble(offsets, blocks, gain, x_ref, unit)
    half = keep.shape[0]
    x = x_ref[...]
    at = 0
    for w in (wq, wk, wv):
        width = w.shape[1]
        part = jnp.dot(x, w[...], preferred_element_type=F32).astype(BF16)
        keep[:, at : at + width] = part[:half]
        send[:, at : at + width] = part[half:]
        at += width


def core_add_kernel(keep, recv, *outs):
    rows = outs[0].shape[0]
    for i, out in enumerate(outs):
        a = keep[i * rows : (i + 1) * rows, :].astype(F32)
        b = recv[i * rows : (i + 1) * rows, :].astype(F32)
        out[...] = (a + b).astype(out.dtype)


def rope_kernel(rotated, count, *refs):
    parts, (scale, cosine, sine, out) = refs[:count], refs[count:]
    width = out.shape[1]
    for at in range(0, width, HEAD_DIM):
        total = parts[0][:, at : at + HEAD_DIM].astype(F32)
        for part in parts[1:]:
            total = total + part[:, at : at + HEAD_DIM].astype(F32)
        total = total * scale[...]
        if at < rotated:
            total = total * cosine[...] + pltpu.roll(total, HEAD_DIM // 2, 1) * sine[...]
        out[:, at : at + HEAD_DIM] = total.astype(BF16)


def attention_kernel(heads, kv_heads, count, block, places, row_places, *refs):
    pieces, rest = refs[:count], refs[count:]
    bias, w_out = rest[0], rest[1]
    outs, (qkv, attended) = rest[2:-2], rest[-2:]
    unit = pieces[0].shape[0]
    for i, piece in enumerate(pieces):
        qkv[pl.ds(pl.multiple_of(places[i], unit), unit), :] = piece[...]
    tokens = qkv.shape[0]
    group = heads // kv_heads
    window = min(tokens, block + LONGEST)
    row_unit = outs[0].shape[0]
    for start in range(0, tokens, block):
        first = max(0, start + block - window)
        mask = bias[start : start + block, :]
        mask = jnp.concatenate([mask] * group, axis=0)
        for g in range(kv_heads):
            q = jnp.concatenate(
                [
                    qkv[start : start + block, h * HEAD_DIM : (h + 1) * HEAD_DIM]
                    for h in range(g * group, (g + 1) * group)
                ],
                axis=0,
            )
            k_at = (heads + g) * HEAD_DIM
            v_at = (heads + kv_heads + g) * HEAD_DIM
            k = qkv[first : first + window, k_at : k_at + HEAD_DIM]
            v = qkv[first : first + window, v_at : v_at + HEAD_DIM]
            scores = lax.dot_general(
                q, k, (((1,), (1,)), ((), ())), preferred_element_type=F32
            ) * HEAD_DIM ** (-0.5)
            scores = scores + mask
            weights = jnp.exp(scores - jnp.max(scores, axis=1, keepdims=True))
            total = jnp.sum(weights, axis=1, keepdims=True)
            weights = (weights / total).astype(BF16)
            result = jnp.dot(weights, v, preferred_element_type=F32).astype(BF16)
            for h in range(group):
                at = (g * group + h) * HEAD_DIM
                for sub in range(0, block, row_unit):
                    place = pl.multiple_of(row_places[(start + sub) // row_unit], row_unit)
                    attended[pl.ds(place, row_unit), at : at + HEAD_DIM] = result[
                        h * block + sub : h * block + sub + row_unit
                    ]
    product = jnp.dot(attended[...], w_out[...], preferred_element_type=F32)
    for i, out in enumerate(outs):
        out[...] = product[i * row_unit : (i + 1) * row_unit].astype(out.dtype)


def arrange_kernel(unit, offsets, *refs):
    blocks, (gain, out) = refs[:-2], refs[-2:]
    assemble(offsets, blocks, gain, out, unit)


def gate_up_kernel(x, w_gate, w_up, keep, send):
    half = keep.shape[1]
    for i, w in enumerate((w_gate, w_up)):
        part = jnp.dot(x[...], w[0], preferred_element_type=F32).astype(BF16)
        keep[i] = part[:half]
        send[i] = part[half:]


def down_kernel(count, places, *refs):
    own, other, w_down = refs[:count], refs[count : 2 * count], refs[2 * count]
    outs, total = refs[2 * count + 1 : -1], refs[-1]
    at = 0
    for i in range(count):
        hidden = jnp.concatenate([own[i][...], other[i][...]], axis=0)
        width = hidden.shape[1]
        part = jnp.dot(hidden, w_down[0, at : at + width, :], preferred_element_type=F32)
        total[...] = part if i == 0 else total[...] + part
        at += width
    unit = outs[0].shape[0]
    for i, out in enumerate(outs):
        place = pl.multiple_of(places[i], unit)
        out[...] = total[pl.ds(place, unit), :].astype(out.dtype)


def head_kernel(rows, col_index, row_places, *refs):
    own, other = refs[:rows], refs[rows : 2 * rows]
    scale, target, w, out, lhs, top, total, picked = refs[2 * rows :]
    step = pl.program_id(0)
    blocks, unit = own[0].shape[0], own[0].shape[1]

    @pl.when(step == 0)
    def _():
        for core, arrays in enumerate((own, other)):
            for i, array in enumerate(arrays):
                place = pl.multiple_of(row_places[i], unit)
                for j in range(blocks):
                    feature = col_index[2 * j + core]
                    lhs[feature, pl.ds(place, unit), :] = array[j]
        top[...] = jnp.full_like(top, MASKED)
        total[...] = jnp.zeros_like(total)
        picked[...] = jnp.zeros_like(picked)

    depth = lhs.shape[2]
    logits = jnp.dot(lhs[0], w[:depth, :], preferred_element_type=F32)
    for i in range(1, lhs.shape[0]):
        logits += jnp.dot(
            lhs[i], w[i * depth : (i + 1) * depth, :], preferred_element_type=F32
        )
    logits = logits * scale[...]
    width = logits.shape[1]
    lane = lax.broadcasted_iota(jnp.int32, logits.shape, 1) + step * width
    hit = jnp.where(lane == target[...], logits, 0.0)
    picked[...] += jnp.sum(hit, axis=1, keepdims=True)
    new_top = jnp.maximum(top[...], jnp.max(logits, axis=1, keepdims=True))
    total[...] = total[...] * jnp.exp(top[...] - new_top) + jnp.sum(
        jnp.exp(logits - new_top), axis=1, keepdims=True
    )
    top[...] = new_top

    @pl.when(step == pl.num_programs(0) - 1)
    def _():
        place = lax.broadcasted_iota(jnp.int32, out.shape, 1)
        out[...] = jnp.where(
            place == 0, top[...], jnp.where(place == 1, total[...], picked[...])
        )


def chain_reduce(near, far, add_near, pairs_of):
    length = lax.axis_size("col") // 2
    middle = length // 2 - 1
    for hop in range(length - 1):
        if hop <= middle:
            received = lax.ppermute(far, "col", pairs_of(hop))
        else:
            received = lax.ppermute(near, "col", pairs_of(hop))
        if hop < middle:
            far = (far.astype(F32) + received.astype(F32)).astype(BF16)
        else:
            near = add_near(near, received, hop)
    return near


def per_device(
    residual,
    attn_gain,
    w_query,
    w_key,
    w_value,
    w_out,
    mlp_gain,
    w_gate,
    w_up,
    w_down,
    final_gain,
    w_head,
    seq_lengths,
    targets,
):
    row_count = lax.axis_size("row")
    col_count = lax.axis_size("col")
    chips = col_count // 2
    row_index = lax.axis_index("row")
    col_index = lax.axis_index("col")
    core = col_index % 2
    chip = col_index // 2
    row_tokens, features = residual.shape
    tokens = row_tokens * row_count
    col_tokens = tokens // col_count
    quarter = tokens // 4
    heads = w_query.shape[1] // HEAD_DIM
    kv_heads = w_key.shape[1] // HEAD_DIM
    qkv_width = w_query.shape[1] + 2 * w_key.shape[1]
    rotated = w_query.shape[1] + w_key.shape[1]
    ff_local = w_gate.shape[2]
    vocab_local = w_head.shape[1]

    row_range = jnp.arange(row_count, dtype=jnp.int32)
    col_range = jnp.arange(col_count, dtype=jnp.int32)
    row_rel = row_range ^ row_index
    col_rel = col_range ^ col_index

    token_index = jnp.arange(tokens, dtype=jnp.int32)
    segment, positions = sequence_layout(seq_lengths, token_index)
    block = min(64, tokens)
    window = min(tokens, block + LONGEST)
    first_key = jnp.maximum(0, (token_index // block + 1) * block - window)
    key_index = first_key[:, None] + jnp.arange(window, dtype=jnp.int32)[None, :]
    key_segment, _ = sequence_layout(seq_lengths, key_index.reshape(-1))
    allowed = (key_segment.reshape(tokens, window) == segment[:, None]) & (
        key_index <= token_index[:, None]
    )
    bias = jnp.where(allowed, 0.0, MASKED).astype(F32)
    own_positions = lax.dynamic_slice_in_dim(positions, col_index * col_tokens, col_tokens)
    exponent = jnp.arange(HEAD_DIM // 2, dtype=F32) * 2.0 / HEAD_DIM
    angles = own_positions[:, None] * (ROPE_BASE ** (-exponent))[None, :]
    cosine, sine = jnp.cos(angles), jnp.sin(angles)
    cosine = jnp.concatenate([cosine, cosine], axis=1)
    sine = jnp.concatenate([-sine, sine], axis=1)

    blocks = [residual] + [row_xor(residual, j) for j in range(1, row_count)]
    squares = jnp.stack([jnp.sum(jnp.square(b.astype(F32)), axis=1) for b in blocks])
    scale_rel = lax.rsqrt(col_sum(squares) / D + EPSILON).reshape(-1)
    own_first = col_index * col_tokens
    own_place = ((own_first // row_tokens) ^ row_index) * row_tokens + own_first % row_tokens
    own_scale = lax.dynamic_slice_in_dim(scale_rel, own_place, col_tokens)[:, None]

    per_row = row_tokens // col_tokens
    col_block = (row_rel[:, None] * per_row + jnp.arange(per_row, dtype=jnp.int32)).reshape(-1)
    relative = col_block ^ col_index
    offsets = ((relative & 1) * chips + (relative >> 1)) * col_tokens
    half = tokens // 2
    shape = functools.partial(jax.ShapeDtypeStruct)
    keep, send = pl.pallas_call(
        functools.partial(qkv_kernel, col_tokens, row_count),
        out_shape=[shape((half, qkv_width), BF16)] * 2,
        in_specs=[SMEM] + [VMEM] * (row_count + 4),
        out_specs=[VMEM] * 2,
        scratch_shapes=[pltpu.VMEM((tokens, features), BF16)],
        compiler_params=params(24),
        cost_estimate=cost(
            2 * tokens * features * qkv_width, 2 * qkv_width * (features + tokens)
        ),
        name="qkv_partial",
    )(offsets, *blocks, attn_gain[None, :], w_query, w_key, w_value)
    received = col_xor(send, 1)
    parts = pl.pallas_call(
        core_add_kernel,
        out_shape=[shape((col_tokens, qkv_width), F32 if i == 0 else BF16) for i in range(chips)],
        in_specs=[VMEM] * 2,
        out_specs=[VMEM] * chips,
        compiler_params=params(16),
        cost_estimate=cost(half * qkv_width, 6 * half * qkv_width),
        name="qkv_core_add",
    )(keep, received)
    parts = [parts[0]] + [col_xor(parts[j], 2 * j) for j in range(1, chips)]
    mine = pl.pallas_call(
        functools.partial(rope_kernel, rotated, chips),
        out_shape=shape((col_tokens, qkv_width), BF16),
        in_specs=[VMEM] * (chips + 3),
        out_specs=VMEM,
        compiler_params=params(16),
        cost_estimate=cost(8 * col_tokens * qkv_width, 2 * tokens * qkv_width),
        name="qkv_rope",
    )(*parts, own_scale, cosine, sine)
    pieces = [mine] + [col_xor(mine, 2 * j) for j in range(1, chips)]
    pieces = pieces + [col_xor(piece, 1) for piece in pieces]
    piece_index = [2 * j for j in range(chips)] + [2 * j + 1 for j in range(chips)]
    places = (jnp.array(piece_index, jnp.int32) ^ col_index) * col_tokens

    projected = pl.pallas_call(
        functools.partial(attention_kernel, heads, kv_heads, col_count, block),
        out_shape=[shape((row_tokens, features), F32 if i == 0 else BF16) for i in range(row_count)],
        in_specs=[SMEM] * 2 + [VMEM] * (col_count + 2),
        out_specs=[VMEM] * row_count,
        scratch_shapes=[
            pltpu.VMEM((tokens, qkv_width), BF16),
            pltpu.VMEM((tokens, heads * HEAD_DIM), BF16),
        ],
        compiler_params=params(32),
        cost_estimate=cost(
            2 * tokens * heads * HEAD_DIM * features * 2, 2 * heads * HEAD_DIM * features * 2
        ),
        name="attention_out",
    )(places, row_rel * row_tokens, *pieces, bias, w_out)
    projected = [projected[0]] + [row_xor(projected[j], j) for j in range(1, row_count)]
    stream = residual.astype(F32) + tree_sum([p.astype(F32) for p in projected])
    stream = lax.optimization_barrier(stream.astype(BF16))
    stream_f = stream.astype(F32)

    blocks = [stream] + [row_xor(stream, j) for j in range(1, row_count)]
    squares = jnp.stack([jnp.sum(jnp.square(b.astype(F32)), axis=1) for b in blocks])
    scale_rel = lax.rsqrt(col_sum(squares) / D + EPSILON)
    per_quarter = row_count // 4
    upper = (chip >= chips // 2).astype(jnp.int32)
    quarter_own = upper * 2 + core
    quarter_rows = (quarter_own * per_quarter + jnp.arange(per_quarter, dtype=jnp.int32)) ^ row_index
    near_scale = jnp.take(scale_rel, quarter_rows, axis=0).reshape(quarter)[:, None]
    at_end = (chip == 0) | (chip == chips - 1)
    near_scale_end = jnp.where(at_end, near_scale, 0.0)
    relative = (row_rel // per_quarter) ^ quarter_own
    quarter_offsets = ((relative & 1) * 2 + (relative >> 1)) * quarter + (
        row_rel % per_quarter
    ) * row_tokens
    mlp_in = pl.pallas_call(
        functools.partial(arrange_kernel, row_tokens),
        out_shape=shape((tokens, features), BF16),
        in_specs=[SMEM] + [VMEM] * (row_count + 1),
        out_specs=VMEM,
        compiler_params=params(16),
        cost_estimate=cost(tokens * features, 4 * tokens * features),
        name="mlp_in",
    )(quarter_offsets, *blocks, mlp_gain[None, :])

    chunk_count = 3 if ff_local % (3 * HEAD_DIM) == 0 else 1
    chunk = ff_local // chunk_count
    tile = chunk // 3 if chunk % (3 * HEAD_DIM) == 0 else chunk
    tiles = chunk // tile

    def pairs_of(hop):
        pairs = []
        for k in range(2):
            pairs.append((2 * hop + k, 2 * (hop + 1) + k))
            pairs.append((2 * (chips - 1 - hop) + k, 2 * (chips - 2 - hop) + k))
        return pairs

    def back_of(hop):
        return [(b, a) for a, b in pairs_of(hop)]

    def gate_up(member, index):
        first = index * tiles
        return pl.pallas_call(
            gate_up_kernel,
            grid=(tiles,),
            out_shape=[shape((2, half, chunk), BF16)] * 2,
            in_specs=[
                pl.BlockSpec((tokens, features), lambda i: (0, 0)),
                pl.BlockSpec((1, features, tile), lambda i: (member, 0, first + i)),
                pl.BlockSpec((1, features, tile), lambda i: (member, 0, first + i)),
            ],
            out_specs=[pl.BlockSpec((2, half, tile), lambda i: (0, 0, i))] * 2,
            compiler_params=params(24),
            cost_estimate=cost(
                4 * tokens * features * chunk, 4 * chunk * (features + tokens)
            ),
            name="gate_up",
        )(mlp_in, w_gate, w_up)

    def add_near(near, received, hop):
        total = near.astype(F32) + received.astype(F32)
        if hop < chips - 2:
            return total.astype(BF16)
        gate = total[0] * near_scale_end
        up = total[1] * near_scale_end
        return (gate / (1.0 + jnp.exp(-gate)) * up).astype(BF16)

    def hidden_chunk(member, index):
        keep, send = gate_up(member, index)
        received = col_xor(send, 1)
        far = (keep[:, quarter:].astype(F32) + received[:, quarter:].astype(F32)).astype(BF16)
        near = (keep[:, :quarter].astype(F32) + received[:, :quarter].astype(F32)).astype(BF16)
        hidden = chain_reduce(near, far, add_near, pairs_of)
        middle = chips // 2 - 1
        moving = hidden
        near_sum, far_sum = hidden, None
        for hop in range(chips - 2, -1, -1):
            moving = lax.ppermute(moving, "col", back_of(hop))
            if hop > middle:
                near_sum = near_sum + moving
            else:
                far_sum = moving if far_sum is None else far_sum + moving
        own = jnp.concatenate([near_sum, far_sum], axis=0)
        return own, col_xor(own, 1)

    def down(member, chunks):
        own = [c[0] for c in chunks]
        other = [c[1] for c in chunks]
        count = len(chunks)
        return pl.pallas_call(
            functools.partial(down_kernel, count),
            grid=(1,),
            out_shape=[
                shape((row_tokens, features), F32 if i == 0 else BF16) for i in range(row_count)
            ],
            in_specs=[SMEM]
            + [pl.BlockSpec((half, chunk), lambda i: (0, 0))] * (2 * count)
            + [pl.BlockSpec((1, ff_local, features), lambda i: (member, 0, 0))],
            out_specs=[pl.BlockSpec((row_tokens, features), lambda i: (0, 0))] * row_count,
            scratch_shapes=[pltpu.VMEM((tokens, features), F32)],
            compiler_params=params(32),
            cost_estimate=cost(
                2 * tokens * features * ff_local, 2 * ff_local * (features + tokens)
            ),
            name="down",
        )(quarter_offsets, *own, *other, w_down)

    vocab_start = (row_index * col_count + col_index) * vocab_local
    local_targets = (targets - vocab_start)[:, None]
    vocab_tile = 512 if vocab_local % 512 == 0 else vocab_local

    def head(member, chunks):
        partial_rows = down(member, chunks)
        partial_rows = [partial_rows[0]] + [
            row_xor(partial_rows[j], j) for j in range(1, row_count)
        ]
        output = stream_f + tree_sum([p.astype(F32) for p in partial_rows])
        squares = col_sum(jnp.sum(output * output, axis=1))
        scaled = (output * final_gain[None, :]).astype(BF16)
        squares = jnp.stack([squares] + [row_xor(squares, j) for j in range(1, row_count)])
        squares = jnp.take(squares, row_rel, axis=0).reshape(tokens)
        scale = lax.rsqrt(squares / D + EPSILON)[:, None]
        by_chip = jnp.stack([scaled] + [col_xor(scaled, 2 * j) for j in range(1, chips)])
        own = [by_chip] + [row_xor(by_chip, j) for j in range(1, row_count)]
        other = [col_xor(array, 1) for array in own]
        return pl.pallas_call(
            functools.partial(head_kernel, row_count),
            grid=(vocab_local // vocab_tile,),
            out_shape=shape((tokens, 128), F32),
            in_specs=[SMEM] * 2
            + [pl.BlockSpec((chips, row_tokens, features), lambda i: (0, 0, 0))] * (2 * row_count)
            + [pl.BlockSpec((tokens, 1), lambda i: (0, 0))] * 2
            + [pl.BlockSpec((D, vocab_tile), lambda i: (0, i))],
            out_specs=pl.BlockSpec((tokens, 128), lambda i: (0, 0)),
            scratch_shapes=[pltpu.VMEM((col_count, tokens, features), BF16)]
            + [pltpu.VMEM((tokens, 1), F32)] * 3,
            compiler_params=params(44),
            cost_estimate=cost(2 * tokens * D * vocab_local, 2 * D * vocab_local),
            name="head",
        )(col_rel, row_rel * row_tokens, *own, *other, scale, local_targets, w_head)[:, :3].T

    stats = []
    for member in range(2):
        chunks = [hidden_chunk(member, index) for index in range(chunk_count)]
        stats.append(head(member, chunks))
    stats = jnp.stack(stats, axis=1)

    def combine(parts):
        top = functools.reduce(jnp.maximum, [p[0] for p in parts])
        total = tree_sum([p[1] * jnp.exp(p[0] - top) for p in parts])
        picked = tree_sum([p[2] for p in parts])
        return jnp.stack([top, total, picked])

    stats = combine([stats] + [col_xor(stats, j) for j in range(1, col_count)])
    stats = combine([stats] + [row_xor(stats, j) for j in range(1, row_count)])
    logprob = stats[2] - (stats[0] + jnp.log(stats[1]))
    difference = logprob[0] - logprob[1]
    one_hot = (segment[:, None] == jnp.arange(SEQS, dtype=jnp.int32)[None, :]).astype(F32)
    seq_sums = jnp.dot(difference, one_hot, precision=lax.Precision.HIGHEST)
    return seq_sums / seq_lengths.astype(F32)


def solution(mesh):
    placed = (
        P("row", "col"),
        P("col"),
        P("col", "row"),
        P("col", "row"),
        P("col", "row"),
        P("row", "col"),
        P("col"),
        P(None, "col", "row"),
        P(None, "col", "row"),
        P(None, "row", "col"),
        P("col"),
        P(None, ("row", "col")),
        P(),
        P(),
    )
    return jax.shard_map(per_device, mesh=mesh, in_specs=placed, out_specs=P(), check_vma=False)
```

```python
import functools

import jax
import jax.numpy as jnp
from jax import lax
from jax.experimental import pallas as pl
from jax.experimental.pallas import tpu as pltpu
from jax.sharding import PartitionSpec as P

D = 5120
HEAD_DIM = 128
SEQS = 8
LONGEST = 64

EPSILON = 1e-06
ROPE_BASE = 1000000.0
MASKED = -1e30
LANES = 128
BF16 = jnp.bfloat16
F32 = jnp.float32
MIB = 1 << 20

VMEM = pl.BlockSpec(memory_space=pltpu.VMEM)
ANY = pl.BlockSpec(memory_space=pl.ANY)
SMEM = pl.BlockSpec(memory_space=pltpu.SMEM)


def params(mib):
    return pltpu.CompilerParams(vmem_limit_bytes=mib * MIB)


def cost(flops, byte_count):
    return pl.CostEstimate(flops=flops, bytes_accessed=byte_count, transcendentals=0)


def row_xor(x, mask):
    count = lax.axis_size("row")
    return lax.ppermute(x, "row", [(i, i ^ mask) for i in range(count)])


def col_xor(x, mask):
    count = lax.axis_size("col")
    return lax.ppermute(x, "col", [(i, i ^ mask) for i in range(count)])


def tree_sum(values):
    values = list(values)
    while len(values) > 1:
        values = [values[i] + values[i + 1] for i in range(0, len(values), 2)]
    return values[0]


def sequence_layout(seq_lengths, token_index):
    ends_at = jnp.cumsum(seq_lengths)
    before = ends_at[None, :] <= token_index[:, None]
    segment = jnp.sum(before.astype(jnp.int32), axis=1)
    starts_at = jnp.sum(jnp.where(before, seq_lengths[None, :], 0), axis=1)
    return (segment, (token_index - starts_at).astype(F32))


def split_square(total):
    high = total.astype(BF16)
    low = (total - high.astype(F32)).astype(BF16)
    lane = lax.broadcasted_iota(jnp.int32, total.shape, 1)
    return jnp.where(lane < LANES // 2, high.astype(F32), low.astype(F32)).astype(BF16)


def join_square(tile):
    return tile + pltpu.roll(tile, LANES // 2, 1)


def assemble(offsets, blocks, gain, x_ref, square_ref, unit):
    step = 0
    for block in blocks:
        for first in range(0, block.shape[0], unit):
            rows = block[first : first + unit, :].astype(F32)
            place = pl.multiple_of(offsets[step], unit)
            x_ref[pl.ds(place, unit), :] = (rows * gain[...]).astype(BF16)
            square = jnp.sum(rows * rows, axis=1, keepdims=True)
            square_ref[pl.ds(place, unit), :] = jnp.broadcast_to(square, (unit, LANES))
            step += 1


def put_squares(square_ref, keep, send, at):
    half = keep.shape[0]
    total = square_ref[...]
    lane = lax.broadcasted_iota(jnp.int32, (half, LANES), 1)
    keep[:, at : at + LANES] = jnp.where(lane < LANES // 2, total[:half], 0.0)
    send[:, at : at + LANES] = split_square(total[half:])


def qkv_kernel(unit, count, offsets, *refs):
    blocks, (gain, wq, wk, wv, keep, send, x_ref, square_ref) = refs[:count], refs[count:]
    assemble(offsets, blocks, gain, x_ref, square_ref, unit)
    half = keep.shape[0]
    x = x_ref[...]
    at = 0
    for w in (wq, wk, wv):
        width = w.shape[1]
        part = jnp.dot(x, w[...], preferred_element_type=F32)
        keep[:, at : at + width] = part[:half]
        send[:, at : at + width] = part[half:].astype(BF16)
        at += width
    put_squares(square_ref, keep, send, at)


def core_add_kernel(keep, recv, *outs):
    rows, width = outs[0].shape
    for i, out in enumerate(outs):
        total = keep[i * rows : (i + 1) * rows, :] + recv[
            i * rows : (i + 1) * rows, :
        ].astype(F32)
        if i == 0:
            out[...] = total
        else:
            out[:, : width - LANES] = total[:, : width - LANES].astype(BF16)
            out[:, width - LANES :] = split_square(join_square(total[:, width - LANES :]))


def rope_kernel(rotated, count, *refs):
    parts, (cosine, sine, out) = refs[:count], refs[count:]
    width = out.shape[1]

    def summed(at):
        total = parts[0][:, at : at + LANES].astype(F32)
        for part in parts[1:]:
            total = total + part[:, at : at + LANES].astype(F32)
        return total

    scale = lax.rsqrt(join_square(summed(width)) / D + EPSILON)
    for at in range(0, width, HEAD_DIM):
        total = summed(at) * scale
        if at < rotated:
            total = total * cosine[...] + pltpu.roll(total, HEAD_DIM // 2, 1) * sine[...]
        out[:, at : at + HEAD_DIM] = total.astype(BF16)


def attention_kernel(heads, kv_heads, count, block, places, *refs):
    pieces, (bias, w_out, out, qkv, attended) = refs[:count], refs[count:]
    unit = pieces[0].shape[0]
    for i, piece in enumerate(pieces):
        qkv[pl.ds(pl.multiple_of(places[i], unit), unit), :] = piece[...]
    tokens = qkv.shape[0]
    group = heads // kv_heads
    window = min(tokens, block + LONGEST)
    for start in range(0, tokens, block):
        first = max(0, start + block - window)
        mask = bias[start : start + block, :]
        mask = jnp.concatenate([mask] * group, axis=0)
        for g in range(kv_heads):
            q = jnp.concatenate(
                [
                    qkv[start : start + block, h * HEAD_DIM : (h + 1) * HEAD_DIM]
                    for h in range(g * group, (g + 1) * group)
                ],
                axis=0,
            )
            k_at = (heads + g) * HEAD_DIM
            v_at = (heads + kv_heads + g) * HEAD_DIM
            k = qkv[first : first + window, k_at : k_at + HEAD_DIM]
            v = qkv[first : first + window, v_at : v_at + HEAD_DIM]
            scores = lax.dot_general(
                q, k, (((1,), (1,)), ((), ())), preferred_element_type=F32
            ) * HEAD_DIM ** (-0.5)
            scores = scores + mask
            weights = jnp.exp(scores - jnp.max(scores, axis=1, keepdims=True))
            total = jnp.sum(weights, axis=1, keepdims=True)
            weights = (weights / total).astype(BF16)
            result = jnp.dot(weights, v, preferred_element_type=F32).astype(BF16)
            for h in range(group):
                at = (g * group + h) * HEAD_DIM
                attended[start : start + block, at : at + HEAD_DIM] = result[
                    h * block : (h + 1) * block
                ]
    product = jnp.dot(attended[...], w_out[...], preferred_element_type=F32)
    rows = out.shape[1]
    for i in range(out.shape[0]):
        out[i] = product[i * rows : (i + 1) * rows].astype(out.dtype)


def arrange_kernel(unit, offsets, *refs):
    blocks, (gain, out, square) = refs[:-3], refs[-3:]
    assemble(offsets, blocks, gain, out, square, unit)


def gate_up_kernel(tile, squares, x, w_gate, w_up, *refs):
    keep, send = refs[-2:]
    half = keep.shape[0]
    tiles = keep.shape[1] // (2 * tile)
    for i, w in enumerate((w_gate, w_up)):
        part = jnp.dot(x[...], w[0], preferred_element_type=F32)
        for step in range(tiles):

            @pl.when(pl.program_id(0) == step)
            def _(at=(2 * step + i) * tile, part=part):
                keep[:, at : at + tile] = part[:half]
                send[:, at : at + tile] = part[half:].astype(BF16)

    if squares:

        @pl.when(pl.program_id(0) == 0)
        def _():
            put_squares(refs[0], keep, send, 2 * tiles * tile)


def halve_kernel(squares, keep, recv, *refs):
    kept, send = refs[-2:]
    half, width = kept.shape
    kept[...] = keep[:half, :] + recv[:half, :].astype(F32)
    total = keep[half:, :] + recv[half:, :].astype(F32)
    if squares:
        body = width - LANES
        send[:, :body] = total[:, :body].astype(BF16)
        send[:, body:] = split_square(join_square(total[:, body:]))
    else:
        send[...] = total.astype(BF16)


def hidden_kernel(tile, squares, keep, recv, *refs):
    if squares:
        hidden, scale_ref = refs
        at = keep.shape[1] - LANES
        total = keep[:, at:] + recv[:, at:].astype(F32)
        scale_ref[...] = lax.rsqrt(join_square(total) / D + EPSILON)
    else:
        scale_ref, hidden = refs
    scale = scale_ref[:, :1]
    for i in range(hidden.shape[1] // tile):
        at = 2 * i * tile
        gate = (keep[:, at : at + tile] + recv[:, at : at + tile].astype(F32)) * scale
        at += tile
        up = (keep[:, at : at + tile] + recv[:, at : at + tile].astype(F32)) * scale
        hidden[:, i * tile : (i + 1) * tile] = (gate / (1.0 + jnp.exp(-gate)) * up).astype(BF16)


def down_kernel(sources, count, unit, offsets, *refs):
    own, other, w_down = refs[:count], refs[count : 2 * count], refs[2 * count]
    outs, total = refs[2 * count + 1 : -1], refs[-1]
    tile = w_down.shape[1]
    for i, (which, at) in enumerate(sources):

        @pl.when(pl.program_id(0) == i)
        def _():
            hidden = jnp.concatenate(
                [own[which][:, at : at + tile], other[which][:, at : at + tile]], axis=0
            )
            part = jnp.dot(hidden, w_down[0], preferred_element_type=F32)
            total[...] = part if i == 0 else total[...] + part

    @pl.when(pl.program_id(0) == len(sources) - 1)
    def _():
        step = 0
        for out in outs:
            for first in range(0, out.shape[0], unit):
                place = pl.multiple_of(offsets[step], unit)
                out[first : first + unit, :] = total[pl.ds(place, unit), :].astype(out.dtype)
                step += 1


def head_kernel(col_index, row_places, own, other, gains, target, w, *refs):
    out, lhs, square, top, total, picked = refs[-6:]
    step = pl.program_id(0)
    rows, chips, unit, width = own.shape

    @pl.when(step == 0)
    def _():
        inverse = 1.0 / gains[...]
        for i in range(rows):
            place = pl.multiple_of(row_places[i], unit)
            sums = jnp.zeros((unit, 1), F32)
            for core, array in enumerate((own, other)):
                for j in range(chips):
                    feature = pl.multiple_of(col_index[2 * j + core] * width, LANES)
                    values = array[i, j]
                    lhs[pl.ds(place, unit), pl.ds(feature, width)] = values
                    plain = values.astype(F32) * inverse[2 * j + core : 2 * j + core + 1, :]
                    sums += jnp.sum(plain * plain, axis=1, keepdims=True)
            square[pl.ds(place, unit), :] = sums
        top[...] = jnp.full_like(top, MASKED)
        total[...] = jnp.zeros_like(total)
        picked[...] = jnp.zeros_like(picked)

    logits = jnp.dot(lhs[...], w[...], preferred_element_type=F32)
    logits = logits * lax.rsqrt(square[...] / D + EPSILON)
    lane = lax.broadcasted_iota(jnp.int32, logits.shape, 1) + step * logits.shape[1]
    hit = jnp.where(lane == target[...], logits, 0.0)
    picked[...] += jnp.sum(hit, axis=1, keepdims=True)
    new_top = jnp.maximum(top[...], jnp.max(logits, axis=1, keepdims=True))
    total[...] = total[...] * jnp.exp(top[...] - new_top) + jnp.sum(
        jnp.exp(logits - new_top), axis=1, keepdims=True
    )
    top[...] = new_top

    @pl.when(step == pl.num_programs(0) - 1)
    def _():
        place = lax.broadcasted_iota(jnp.int32, out.shape, 1)
        out[...] = jnp.where(
            place == 0, top[...], jnp.where(place == 1, total[...], picked[...])
        )


def per_device(
    residual,
    attn_gain,
    w_query,
    w_key,
    w_value,
    w_out,
    mlp_gain,
    w_gate,
    w_up,
    w_down,
    final_gain,
    w_head,
    seq_lengths,
    targets,
):
    row_count = lax.axis_size("row")
    col_count = lax.axis_size("col")
    chips = col_count // 2
    row_index = lax.axis_index("row")
    col_index = lax.axis_index("col")
    core = col_index % 2
    chip = col_index // 2
    row_tokens, features = residual.shape
    tokens = row_tokens * row_count
    col_tokens = tokens // col_count
    quarter = tokens // 4
    heads = w_query.shape[1] // HEAD_DIM
    kv_heads = w_key.shape[1] // HEAD_DIM
    qkv_width = w_query.shape[1] + 2 * w_key.shape[1]
    rotated = w_query.shape[1] + w_key.shape[1]
    ff_local = w_gate.shape[2]
    vocab_local = w_head.shape[1]

    row_range = jnp.arange(row_count, dtype=jnp.int32)
    col_range = jnp.arange(col_count, dtype=jnp.int32)
    row_rel = row_range ^ row_index
    col_rel = col_range ^ col_index

    token_index = jnp.arange(tokens, dtype=jnp.int32)
    segment, positions = sequence_layout(seq_lengths, token_index)
    block = min(64, tokens)
    window = min(tokens, block + LONGEST)
    first_key = jnp.maximum(0, (token_index // block + 1) * block - window)
    key_index = first_key[:, None] + jnp.arange(window, dtype=jnp.int32)[None, :]
    key_segment, _ = sequence_layout(seq_lengths, key_index.reshape(-1))
    allowed = (key_segment.reshape(tokens, window) == segment[:, None]) & (
        key_index <= token_index[:, None]
    )
    bias = jnp.where(allowed, 0.0, MASKED).astype(F32)
    own_positions = lax.dynamic_slice_in_dim(positions, col_index * col_tokens, col_tokens)
    exponent = jnp.arange(HEAD_DIM // 2, dtype=F32) * 2.0 / HEAD_DIM
    angles = own_positions[:, None] * (ROPE_BASE ** (-exponent))[None, :]
    cosine, sine = jnp.cos(angles), jnp.sin(angles)
    cosine = jnp.concatenate([cosine, cosine], axis=1)
    sine = jnp.concatenate([-sine, sine], axis=1)

    blocks = [residual] + [row_xor(residual, j) for j in range(1, row_count)]
    shape = jax.ShapeDtypeStruct

    per_row = row_tokens // col_tokens
    col_block = (row_rel[:, None] * per_row + jnp.arange(per_row, dtype=jnp.int32)).reshape(-1)
    relative = col_block ^ col_index
    offsets = ((relative & 1) * chips + (relative >> 1)) * col_tokens
    half = tokens // 2
    wide = qkv_width + LANES
    keep, send = pl.pallas_call(
        functools.partial(qkv_kernel, col_tokens, row_count),
        out_shape=[shape((half, wide), F32), shape((half, wide), BF16)],
        in_specs=[SMEM] + [VMEM] * (row_count + 4),
        out_specs=[VMEM] * 2,
        scratch_shapes=[pltpu.VMEM((tokens, features), BF16), pltpu.VMEM((tokens, LANES), F32)],
        compiler_params=params(24),
        cost_estimate=cost(
            2 * tokens * features * qkv_width, 2 * qkv_width * (features + tokens)
        ),
        name="qkv_partial",
    )(offsets, *blocks, attn_gain[None, :], w_query, w_key, w_value)
    received = col_xor(send, 1)
    parts = pl.pallas_call(
        core_add_kernel,
        out_shape=[shape((col_tokens, wide), F32 if i == 0 else BF16) for i in range(chips)],
        in_specs=[VMEM] * 2,
        out_specs=[VMEM] * chips,
        compiler_params=params(16),
        cost_estimate=cost(half * qkv_width, 6 * half * qkv_width),
        name="qkv_core_add",
    )(keep, received)
    parts = [parts[0]] + [col_xor(parts[j], 2 * j) for j in range(1, chips)]
    mine = pl.pallas_call(
        functools.partial(rope_kernel, rotated, chips),
        out_shape=shape((col_tokens, qkv_width), BF16),
        in_specs=[VMEM] * (chips + 2),
        out_specs=VMEM,
        compiler_params=params(16),
        cost_estimate=cost(8 * col_tokens * qkv_width, 2 * tokens * qkv_width),
        name="qkv_rope",
    )(*parts, cosine, sine)
    pieces = [mine] + [col_xor(mine, 2 * j) for j in range(1, chips)]
    pieces = pieces + [col_xor(piece, 1) for piece in pieces]
    piece_index = [2 * j for j in range(chips)] + [2 * j + 1 for j in range(chips)]
    places = (jnp.array(piece_index, jnp.int32) ^ col_index) * col_tokens

    projected = pl.pallas_call(
        functools.partial(attention_kernel, heads, kv_heads, col_count, block),
        out_shape=shape((row_count, row_tokens, features), BF16),
        in_specs=[SMEM] + [VMEM] * (col_count + 2),
        out_specs=VMEM,
        scratch_shapes=[
            pltpu.VMEM((tokens, qkv_width), BF16),
            pltpu.VMEM((tokens, heads * HEAD_DIM), BF16),
        ],
        compiler_params=params(32),
        cost_estimate=cost(
            2 * tokens * heads * HEAD_DIM * features * 2, 2 * heads * HEAD_DIM * features * 2
        ),
        name="attention_out",
    )(places, *pieces, bias, w_out)
    projected = lax.all_to_all(projected, "row", 0, 0)
    stream = residual.astype(F32) + jnp.sum(projected.astype(F32), axis=0)
    stream = lax.optimization_barrier(stream.astype(BF16))
    stream_f = stream.astype(F32)

    levels = (col_count - 1).bit_length()
    blocks = [stream] + [row_xor(stream, j) for j in range(1, row_count)]
    position = sum(((relative >> level) & 1) << (levels - 1 - level) for level in range(levels))
    half_offsets = position * col_tokens
    mlp_in, squares = pl.pallas_call(
        functools.partial(arrange_kernel, col_tokens),
        out_shape=[shape((tokens, features), BF16), shape((tokens, LANES), F32)],
        in_specs=[SMEM] + [VMEM] * (row_count + 1),
        out_specs=[VMEM] * 2,
        compiler_params=params(16),
        cost_estimate=cost(tokens * features, 4 * tokens * features),
        name="mlp_in",
    )(half_offsets, *blocks, mlp_gain[None, :])

    gains, _ = lax.optimization_barrier((final_gain[None, :], mlp_in))
    for level in range(levels):
        gains = jnp.concatenate([gains, col_xor(gains, 1 << level)], axis=0)

    tile = ff_local // 3 if ff_local % (3 * LANES) == 0 else ff_local
    tiles = ff_local // tile
    plan = [[(0, 1), (1, 2)], [(0, 2), (2, 1)]] if tiles == 3 else [[(0, 1)], [(0, 1)]]

    def gate_up(member, first, count, squared):
        width = 2 * count * tile + (LANES if squared else 0)
        operands = [mlp_in, w_gate, w_up] + ([squares] if squared else [])
        weight = pl.BlockSpec((1, features, tile), lambda i: (member, 0, first + i))
        return pl.pallas_call(
            functools.partial(gate_up_kernel, tile, squared),
            grid=(count,),
            out_shape=[shape((half, width), F32), shape((half, width), BF16)],
            in_specs=[pl.BlockSpec((tokens, features), lambda i: (0, 0)), weight, weight]
            + ([pl.BlockSpec((tokens, LANES), lambda i: (0, 0))] if squared else []),
            out_specs=[pl.BlockSpec((half, width), lambda i: (0, 0))] * 2,
            compiler_params=params(56),
            cost_estimate=cost(4 * tokens * features * tile * count, 4 * tile * count * features),
            name="gate_up",
        )(*operands)

    def halve(keep, received, squared, after):
        rows, width = keep.shape
        step = width if squared or width % (2 * LANES) else width // 2
        return pl.pallas_call(
            functools.partial(halve_kernel, squared),
            grid=(width // step,),
            out_shape=[shape((rows // 2, width), F32), shape((rows // 2, width), BF16)],
            in_specs=[pl.BlockSpec((rows, step), lambda i: (0, i))] * 2 + [ANY] * len(after),
            out_specs=[pl.BlockSpec((rows // 2, step), lambda i: (0, i))] * 2,
            compiler_params=params(24),
            cost_estimate=cost(rows * width, 9 * rows * width),
            name="halve",
        )(keep, received, *after)

    def hidden_of(keep, received, squared, scale):
        rows = keep.shape[0]
        width = keep.shape[1] // (2 * tile) * tile
        scale_shape = shape((rows, LANES), F32)
        hidden_shape = shape((rows, width), BF16)
        return pl.pallas_call(
            functools.partial(hidden_kernel, tile, squared),
            out_shape=[hidden_shape, scale_shape] if squared else hidden_shape,
            in_specs=[VMEM] * (2 if squared else 3),
            out_specs=[VMEM] * 2 if squared else VMEM,
            compiler_params=params(24),
            cost_estimate=cost(8 * rows * width, 14 * rows * width),
            name="hidden",
        )(keep, received, *([] if squared else [scale]))

    arrived, scale, chunks = [], None, [[], []]
    for member in range(2):
        for first, count in plan[member]:
            squared = not arrived
            keep, send = gate_up(member, first, count, squared)
            for level in range(levels - 1):
                received = col_xor(send, 1 << level)
                if level == 1:
                    arrived.append(received)
                after = arrived[-2:-1] if level == 0 else []
                keep, send = halve(keep, received, squared, after)
            received = col_xor(send, 1 << (levels - 1))
            if squared:
                hidden, scale = hidden_of(keep, received, squared, None)
            else:
                hidden = hidden_of(keep, received, squared, scale)
            for level in range(levels - 1, 0, -1):
                hidden = jnp.concatenate([hidden, col_xor(hidden, 1 << level)], axis=0)
            chunks[member].append((hidden, col_xor(hidden, 1)))

    def down(member):
        own = [c[0] for c in chunks[member]]
        other = [c[1] for c in chunks[member]]
        sources = [
            (which, i * tile) for which, (_, count) in enumerate(plan[member]) for i in range(count)
        ]
        return pl.pallas_call(
            functools.partial(down_kernel, sources, len(own), col_tokens),
            grid=(tiles,),
            out_shape=[
                shape((row_tokens, features), F32 if i == 0 else BF16) for i in range(row_count)
            ],
            in_specs=[SMEM]
            + [pl.BlockSpec(array.shape, lambda i: (0, 0)) for array in own + other]
            + [pl.BlockSpec((1, tile, features), lambda i: (member, i, 0))],
            out_specs=[pl.BlockSpec((row_tokens, features), lambda i: (0, 0))] * row_count,
            scratch_shapes=[pltpu.VMEM((tokens, features), F32)],
            compiler_params=params(56),
            cost_estimate=cost(
                2 * tokens * features * ff_local, 2 * ff_local * (features + tokens)
            ),
            name="down",
        )(half_offsets, *own, *other, w_down)

    def final_state(member):
        partial_rows = down(member)
        partial_rows = [partial_rows[0]] + [
            row_xor(partial_rows[j], j) for j in range(1, row_count)
        ]
        output = stream_f + tree_sum([p.astype(F32) for p in partial_rows])
        scaled = (output * final_gain[None, :]).astype(BF16)
        by_chip = jnp.stack([scaled] + [col_xor(scaled, 2 * j) for j in range(1, chips)])
        own = jnp.stack([by_chip] + [row_xor(by_chip, j) for j in range(1, row_count)])
        return by_chip, own, col_xor(own, 1)

    vocab_start = (row_index * col_count + col_index) * vocab_local
    local_targets = (targets - vocab_start)[:, None]
    vocab_tile = 512 if vocab_local % 512 == 0 else vocab_local

    def head(own, other, after):
        return pl.pallas_call(
            head_kernel,
            grid=(vocab_local // vocab_tile,),
            out_shape=shape((tokens, LANES), F32),
            in_specs=[SMEM] * 2
            + [pl.BlockSpec(own.shape, lambda i: (0, 0, 0, 0))] * 2
            + [pl.BlockSpec(gains.shape, lambda i: (0, 0))]
            + [pl.BlockSpec((tokens, 1), lambda i: (0, 0))]
            + [pl.BlockSpec((D, vocab_tile), lambda i: (0, i))]
            + [ANY] * len(after),
            out_specs=pl.BlockSpec((tokens, LANES), lambda i: (0, 0)),
            scratch_shapes=[pltpu.VMEM((tokens, D), BF16)] + [pltpu.VMEM((tokens, 1), F32)] * 4,
            compiler_params=params(56),
            cost_estimate=cost(2 * tokens * D * vocab_local, 2 * D * vocab_local),
            name="head",
        )(col_rel, row_rel * row_tokens, own, other, gains, local_targets, w_head, *after)

    _, policy_own, policy_other = final_state(0)
    by_chip, refer_own, refer_other = final_state(1)
    stats = jnp.stack(
        [head(policy_own, policy_other, [by_chip]), head(refer_own, refer_other, [])]
    )
    stats = stats[:, :, :3].transpose(2, 0, 1)

    stats = lax.all_gather(stats, ("row", "col"), axis=1)
    top = jnp.max(stats[0], axis=0)
    total = jnp.sum(stats[1] * jnp.exp(stats[0] - top[None]), axis=0)
    logprob = jnp.sum(stats[2], axis=0) - (top + jnp.log(total))
    difference = logprob[0] - logprob[1]
    one_hot = (segment[:, None] == jnp.arange(SEQS, dtype=jnp.int32)[None, :]).astype(F32)
    seq_sums = jnp.dot(difference, one_hot, precision=lax.Precision.HIGHEST)
    return seq_sums / seq_lengths.astype(F32)


def solution(mesh):
    placed = (
        P("row", "col"),
        P("col"),
        P("col", "row"),
        P("col", "row"),
        P("col", "row"),
        P("row", "col"),
        P("col"),
        P(None, "col", "row"),
        P(None, "col", "row"),
        P(None, "row", "col"),
        P("col"),
        P(None, ("row", "col")),
        P(),
        P(),
    )
    return jax.shard_map(per_device, mesh=mesh, in_specs=placed, out_specs=P(), check_vma=False)
```

```python
import functools

import jax
import jax.numpy as jnp
from jax import lax
from jax.experimental import pallas as pl
from jax.experimental.pallas import tpu as pltpu
from jax.sharding import PartitionSpec as P

D = 5120
HEAD_DIM = 128
SEQS = 8
LONGEST = 64

EPSILON = 1e-06
ROPE_BASE = 1000000.0
MASKED = -1e30
LANES = 128
BF16 = jnp.bfloat16
F32 = jnp.float32
MIB = 1 << 20

VMEM = pl.BlockSpec(memory_space=pltpu.VMEM)
ANY = pl.BlockSpec(memory_space=pl.ANY)
SMEM = pl.BlockSpec(memory_space=pltpu.SMEM)


def params(mib):
    return pltpu.CompilerParams(vmem_limit_bytes=mib * MIB)


def cost(flops, byte_count):
    return pl.CostEstimate(flops=flops, bytes_accessed=byte_count, transcendentals=0)


def call(kernel, operands, in_specs, after, **options):
    count, extra = len(operands), len(after)

    def body(*refs):
        kernel(*refs[:count], *refs[count + extra :])

    return pl.pallas_call(body, in_specs=in_specs + [ANY] * extra, **options)(*operands, *after)


def row_xor(x, mask):
    count = lax.axis_size("row")
    return lax.ppermute(x, "row", [(i, i ^ mask) for i in range(count)])


def col_xor(x, mask):
    count = lax.axis_size("col")
    return lax.ppermute(x, "col", [(i, i ^ mask) for i in range(count)])


def tree_sum(values):
    values = list(values)
    while len(values) > 1:
        values = [values[i] + values[i + 1] for i in range(0, len(values), 2)]
    return values[0]


def sequence_layout(seq_lengths, token_index):
    ends_at = jnp.cumsum(seq_lengths)
    before = ends_at[None, :] <= token_index[:, None]
    segment = jnp.sum(before.astype(jnp.int32), axis=1)
    starts_at = jnp.sum(jnp.where(before, seq_lengths[None, :], 0), axis=1)
    return (segment, (token_index - starts_at).astype(F32))


def split_square(total):
    high = total.astype(BF16)
    low = (total - high.astype(F32)).astype(BF16)
    lane = lax.broadcasted_iota(jnp.int32, total.shape, 1)
    return jnp.where(lane < LANES // 2, high.astype(F32), low.astype(F32)).astype(BF16)


def join_square(tile):
    return tile + pltpu.roll(tile, LANES // 2, 1)


def assemble(offsets, blocks, gain, x_ref, square_ref, unit):
    step = 0
    for block in blocks:
        for first in range(0, block.shape[0], unit):
            rows = block[first : first + unit, :].astype(F32)
            place = pl.multiple_of(offsets[step], unit)
            x_ref[pl.ds(place, unit), :] = (rows * gain[...]).astype(BF16)
            square = jnp.sum(rows * rows, axis=1, keepdims=True)
            square_ref[pl.ds(place, unit), :] = jnp.broadcast_to(square, (unit, LANES))
            step += 1


def put_squares(square_ref, keep, send, at):
    half = keep.shape[0]
    total = square_ref[...]
    lane = lax.broadcasted_iota(jnp.int32, (half, LANES), 1)
    keep[:, at : at + LANES] = jnp.where(lane < LANES // 2, total[:half], 0.0)
    send[:, at : at + LANES] = split_square(total[half:])


def qkv_kernel(unit, count, offsets, *refs):
    blocks, (gain, wq, wk, wv, keep, send, x_ref, square_ref) = refs[:count], refs[count:]
    assemble(offsets, blocks, gain, x_ref, square_ref, unit)
    half = keep.shape[0]
    x = x_ref[...]
    at = 0
    for w in (wq, wk, wv):
        width = w.shape[1]
        part = jnp.dot(x, w[...], preferred_element_type=F32)
        keep[:, at : at + width] = part[:half]
        send[:, at : at + width] = part[half:].astype(BF16)
        at += width
    put_squares(square_ref, keep, send, at)


def core_add_kernel(keep, recv, *outs):
    rows, width = outs[0].shape
    for i, out in enumerate(outs):
        total = keep[i * rows : (i + 1) * rows, :] + recv[
            i * rows : (i + 1) * rows, :
        ].astype(F32)
        if i == 0:
            out[...] = total
        else:
            out[:, : width - LANES] = total[:, : width - LANES].astype(BF16)
            out[:, width - LANES :] = split_square(join_square(total[:, width - LANES :]))


def rope_kernel(rotated, count, *refs):
    parts, (cosine, sine, out) = refs[:count], refs[count:]
    width = out.shape[1]

    def summed(at):
        total = parts[0][:, at : at + LANES].astype(F32)
        for part in parts[1:]:
            total = total + part[:, at : at + LANES].astype(F32)
        return total

    scale = lax.rsqrt(join_square(summed(width)) / D + EPSILON)
    for at in range(0, width, HEAD_DIM):
        total = summed(at) * scale
        if at < rotated:
            total = total * cosine[...] + pltpu.roll(total, HEAD_DIM // 2, 1) * sine[...]
        out[:, at : at + HEAD_DIM] = total.astype(BF16)


def attention_kernel(heads, kv_heads, count, block, places, row_places, *refs):
    pieces, (bias, w_out), outs, (qkv, attended) = (
        refs[:count],
        refs[count : count + 2],
        refs[count + 2 : -2],
        refs[-2:],
    )
    row_unit = outs[0].shape[0]
    unit = pieces[0].shape[0]
    for i, piece in enumerate(pieces):
        qkv[pl.ds(pl.multiple_of(places[i], unit), unit), :] = piece[...]
    tokens = qkv.shape[0]
    group = heads // kv_heads
    window = min(tokens, block + LONGEST)
    for start in range(0, tokens, block):
        first = max(0, start + block - window)
        mask = bias[start : start + block, :]
        mask = jnp.concatenate([mask] * group, axis=0)
        for g in range(kv_heads):
            q = jnp.concatenate(
                [
                    qkv[start : start + block, h * HEAD_DIM : (h + 1) * HEAD_DIM]
                    for h in range(g * group, (g + 1) * group)
                ],
                axis=0,
            )
            k_at = (heads + g) * HEAD_DIM
            v_at = (heads + kv_heads + g) * HEAD_DIM
            k = qkv[first : first + window, k_at : k_at + HEAD_DIM]
            v = qkv[first : first + window, v_at : v_at + HEAD_DIM]
            scores = lax.dot_general(
                q, k, (((1,), (1,)), ((), ())), preferred_element_type=F32
            ) * HEAD_DIM ** (-0.5)
            scores = scores + mask
            weights = jnp.exp(scores - jnp.max(scores, axis=1, keepdims=True))
            total = jnp.sum(weights, axis=1, keepdims=True)
            weights = (weights / total).astype(BF16)
            result = jnp.dot(weights, v, preferred_element_type=F32).astype(BF16)
            for h in range(group):
                at = (g * group + h) * HEAD_DIM
                for sub in range(0, block, row_unit):
                    place = pl.multiple_of(row_places[(start + sub) // row_unit], row_unit)
                    attended[pl.ds(place, row_unit), at : at + HEAD_DIM] = result[
                        h * block + sub : h * block + sub + row_unit
                    ]
    product = jnp.dot(attended[...], w_out[...], preferred_element_type=F32)
    for i, out in enumerate(outs):
        out[...] = product[i * row_unit : (i + 1) * row_unit].astype(out.dtype)


def arrange_kernel(unit, offsets, *refs):
    blocks, (gain, out, keep, send, square) = refs[:-5], refs[-5:]
    assemble(offsets, blocks, gain, out, square, unit)
    put_squares(square, keep, send, 0)


def gate_up_kernel(x, w_gate, w_up, keep, send):
    half = keep.shape[1]
    for i, w in enumerate((w_gate, w_up)):
        part = jnp.dot(x[...], w[0], preferred_element_type=F32)
        keep[i] = part[:half]
        send[i] = part[half:].astype(BF16)


def halve_kernel(squares, *refs):
    if squares:
        keep, recv, square_keep, square_recv, kept, send, square_kept, square_send = refs
        half = square_kept.shape[0]
        total = square_keep[...] + square_recv[...].astype(F32)
        square_kept[...] = total[:half]
        square_send[...] = split_square(join_square(total[half:]))
    else:
        keep, recv, kept, send = refs
    half = kept.shape[1]
    kept[...] = keep[:, :half, :] + recv[:, :half, :].astype(F32)
    send[...] = (keep[:, half:, :] + recv[:, half:, :].astype(F32)).astype(BF16)


def hidden_kernel(squares, keep, recv, *refs):
    if squares:
        square_keep, square_recv, hidden, scale_ref = refs
        total = square_keep[...] + square_recv[...].astype(F32)
        scale_ref[...] = lax.rsqrt(join_square(total) / D + EPSILON)
    else:
        scale_ref, hidden = refs
    scale = scale_ref[:, :1]
    width = keep.shape[2]
    for i in range(keep.shape[0] // 2):
        gate = (keep[2 * i] + recv[2 * i].astype(F32)) * scale
        up = (keep[2 * i + 1] + recv[2 * i + 1].astype(F32)) * scale
        hidden[:, i * width : (i + 1) * width] = (
            gate / (1.0 + jnp.exp(-gate)) * up
        ).astype(BF16)


def join_kernel(first, second, out):
    rows = first.shape[0]
    out[:rows] = first[...]
    out[rows:] = second[...]


def pack_kernel(*refs):
    parts, out = refs[:-1], refs[-1]
    for i, part in enumerate(parts):
        out[i] = part[...]


def output_kernel(stream, gain, *refs):
    parts, out = refs[:-1], refs[-1]
    total = stream[...].astype(F32)
    for part in parts:
        total = total + part[...].astype(F32)
    out[...] = (total * gain[...]).astype(BF16)


def down_kernel(sources, count, unit, offsets, *refs):
    own, other, w_down = refs[:count], refs[count : 2 * count], refs[2 * count]
    outs, total = refs[2 * count + 1 : -1], refs[-1]
    tile = w_down.shape[1]
    for i, (which, at) in enumerate(sources):

        @pl.when(pl.program_id(0) == i)
        def _():
            hidden = jnp.concatenate(
                [own[which][:, at : at + tile], other[which][:, at : at + tile]], axis=0
            )
            part = jnp.dot(hidden, w_down[0], preferred_element_type=F32)
            total[...] = part if i == 0 else total[...] + part

    @pl.when(pl.program_id(0) == len(sources) - 1)
    def _():
        step = 0
        for out in outs:
            for first in range(0, out.shape[0], unit):
                place = pl.multiple_of(offsets[step], unit)
                out[first : first + unit, :] = total[pl.ds(place, unit), :].astype(out.dtype)
                step += 1


def head_kernel(rows, first, col_index, row_places, *refs):
    own, other = refs[:rows], refs[rows : 2 * rows]
    gains, target, w, out, lhs, square, top, total, picked = refs[2 * rows :]
    step = pl.program_id(0)
    chips, unit, width = own[0].shape

    @pl.when(step == 0)
    def _():
        inverse = 1.0 / gains[...]
        for i in range(rows):
            place = pl.multiple_of(row_places[i], unit)
            sums = jnp.zeros((unit, 1), F32)
            for core, arrays in enumerate((own, other)):
                for j in range(chips):
                    feature = pl.multiple_of(col_index[2 * j + core] * width, LANES)
                    values = arrays[i][j]
                    lhs[pl.ds(place, unit), pl.ds(feature, width)] = values
                    plain = values.astype(F32) * inverse[2 * j + core : 2 * j + core + 1, :]
                    sums += jnp.sum(plain * plain, axis=1, keepdims=True)
            square[pl.ds(place, unit), :] = sums
        top[...] = jnp.full_like(top, MASKED)
        total[...] = jnp.zeros_like(total)
        picked[...] = jnp.zeros_like(picked)

    logits = jnp.dot(lhs[...], w[...], preferred_element_type=F32)
    logits = logits * lax.rsqrt(square[...] / D + EPSILON)
    lane = lax.broadcasted_iota(jnp.int32, logits.shape, 1)
    lane = lane + (step + first) * logits.shape[1]
    hit = jnp.where(lane == target[...], logits, 0.0)
    picked[...] += jnp.sum(hit, axis=1, keepdims=True)
    new_top = jnp.maximum(top[...], jnp.max(logits, axis=1, keepdims=True))
    total[...] = total[...] * jnp.exp(top[...] - new_top) + jnp.sum(
        jnp.exp(logits - new_top), axis=1, keepdims=True
    )
    top[...] = new_top

    @pl.when(step == pl.num_programs(0) - 1)
    def _():
        place = lax.broadcasted_iota(jnp.int32, out.shape, 1)
        out[...] = jnp.where(
            place == 0, top[...], jnp.where(place == 1, total[...], picked[...])
        )


def per_device(
    residual,
    attn_gain,
    w_query,
    w_key,
    w_value,
    w_out,
    mlp_gain,
    w_gate,
    w_up,
    w_down,
    final_gain,
    w_head,
    seq_lengths,
    targets,
):
    row_count = lax.axis_size("row")
    col_count = lax.axis_size("col")
    chips = col_count // 2
    row_index = lax.axis_index("row")
    col_index = lax.axis_index("col")
    core = col_index % 2
    chip = col_index // 2
    row_tokens, features = residual.shape
    tokens = row_tokens * row_count
    col_tokens = tokens // col_count
    quarter = tokens // 4
    heads = w_query.shape[1] // HEAD_DIM
    kv_heads = w_key.shape[1] // HEAD_DIM
    qkv_width = w_query.shape[1] + 2 * w_key.shape[1]
    rotated = w_query.shape[1] + w_key.shape[1]
    ff_local = w_gate.shape[2]
    vocab_local = w_head.shape[1]

    row_range = jnp.arange(row_count, dtype=jnp.int32)
    col_range = jnp.arange(col_count, dtype=jnp.int32)
    row_rel = row_range ^ row_index
    col_rel = col_range ^ col_index

    token_index = jnp.arange(tokens, dtype=jnp.int32)
    segment, positions = sequence_layout(seq_lengths, token_index)
    block = min(64, tokens)
    window = min(tokens, block + LONGEST)
    first_key = jnp.maximum(0, (token_index // block + 1) * block - window)
    key_index = first_key[:, None] + jnp.arange(window, dtype=jnp.int32)[None, :]
    key_segment, _ = sequence_layout(seq_lengths, key_index.reshape(-1))
    allowed = (key_segment.reshape(tokens, window) == segment[:, None]) & (
        key_index <= token_index[:, None]
    )
    bias = jnp.where(allowed, 0.0, MASKED).astype(F32)
    own_positions = lax.dynamic_slice_in_dim(positions, col_index * col_tokens, col_tokens)
    exponent = jnp.arange(HEAD_DIM // 2, dtype=F32) * 2.0 / HEAD_DIM
    angles = own_positions[:, None] * (ROPE_BASE ** (-exponent))[None, :]
    cosine, sine = jnp.cos(angles), jnp.sin(angles)
    cosine = jnp.concatenate([cosine, cosine], axis=1)
    sine = jnp.concatenate([-sine, sine], axis=1)

    blocks = [residual] + [row_xor(residual, j) for j in range(1, row_count)]
    shape = jax.ShapeDtypeStruct

    per_row = row_tokens // col_tokens
    col_block = (row_rel[:, None] * per_row + jnp.arange(per_row, dtype=jnp.int32)).reshape(-1)
    relative = col_block ^ col_index
    offsets = ((relative & 1) * chips + (relative >> 1)) * col_tokens
    half = tokens // 2
    wide = qkv_width + LANES
    keep, send = pl.pallas_call(
        functools.partial(qkv_kernel, col_tokens, row_count),
        out_shape=[shape((half, wide), F32), shape((half, wide), BF16)],
        in_specs=[SMEM] + [VMEM] * (row_count + 4),
        out_specs=[VMEM] * 2,
        scratch_shapes=[pltpu.VMEM((tokens, features), BF16), pltpu.VMEM((tokens, LANES), F32)],
        compiler_params=params(56),
        cost_estimate=cost(
            2 * tokens * features * qkv_width, 2 * qkv_width * (features + tokens)
        ),
        name="qkv_partial",
    )(offsets, *blocks, attn_gain[None, :], w_query, w_key, w_value)
    received = col_xor(send, 1)
    parts = pl.pallas_call(
        core_add_kernel,
        out_shape=[shape((col_tokens, wide), F32 if i == 0 else BF16) for i in range(chips)],
        in_specs=[VMEM] * 2,
        out_specs=[VMEM] * chips,
        compiler_params=params(16),
        cost_estimate=cost(half * qkv_width, 6 * half * qkv_width),
        name="qkv_core_add",
    )(keep, received)
    parts = [parts[0]] + [col_xor(parts[j], 2 * j) for j in range(1, chips)]
    mine = pl.pallas_call(
        functools.partial(rope_kernel, rotated, chips),
        out_shape=shape((col_tokens, qkv_width), BF16),
        in_specs=[VMEM] * (chips + 2),
        out_specs=VMEM,
        compiler_params=params(16),
        cost_estimate=cost(8 * col_tokens * qkv_width, 2 * tokens * qkv_width),
        name="qkv_rope",
    )(*parts, cosine, sine)
    pieces = [mine] + [col_xor(mine, 2 * j) for j in range(1, chips)]
    pieces = pieces + [col_xor(piece, 1) for piece in pieces]
    piece_index = [2 * j for j in range(chips)] + [2 * j + 1 for j in range(chips)]
    places = (jnp.array(piece_index, jnp.int32) ^ col_index) * col_tokens

    projected = pl.pallas_call(
        functools.partial(attention_kernel, heads, kv_heads, col_count, block),
        out_shape=[
            shape((row_tokens, features), F32 if i == 0 else BF16) for i in range(row_count)
        ],
        in_specs=[SMEM] * 2 + [VMEM] * (col_count + 2),
        out_specs=[VMEM] * row_count,
        scratch_shapes=[
            pltpu.VMEM((tokens, qkv_width), BF16),
            pltpu.VMEM((tokens, heads * HEAD_DIM), BF16),
        ],
        compiler_params=params(32),
        cost_estimate=cost(
            2 * tokens * heads * HEAD_DIM * features * 2, 2 * heads * HEAD_DIM * features * 2
        ),
        name="attention_out",
    )(places, row_rel * row_tokens, *pieces, bias, w_out)
    projected = [projected[0]] + [row_xor(projected[j], j) for j in range(1, row_count)]
    stream = residual.astype(F32) + tree_sum([p.astype(F32) for p in projected])
    stream = lax.optimization_barrier(stream.astype(BF16))

    levels = (col_count - 1).bit_length()
    blocks = [stream] + [row_xor(stream, j) for j in range(1, row_count)]
    position = sum(((relative >> level) & 1) << (levels - 1 - level) for level in range(levels))
    half_offsets = position * col_tokens
    mlp_in, square_keep, square_send = pl.pallas_call(
        functools.partial(arrange_kernel, col_tokens),
        out_shape=[
            shape((tokens, features), BF16),
            shape((half, LANES), F32),
            shape((half, LANES), BF16),
        ],
        in_specs=[SMEM] + [VMEM] * (row_count + 1),
        out_specs=[VMEM] * 3,
        scratch_shapes=[pltpu.VMEM((tokens, LANES), F32)],
        compiler_params=params(16),
        cost_estimate=cost(tokens * features, 4 * tokens * features),
        name="mlp_in",
    )(half_offsets, *blocks, mlp_gain[None, :])

    gains, _ = lax.optimization_barrier((final_gain[None, :], mlp_in))
    for level in range(levels):
        gains = jnp.concatenate([gains, col_xor(gains, 1 << level)], axis=0)

    divisible = ff_local % (3 * LANES) == 0
    tile = ff_local // 3 if divisible else ff_local
    tiles = ff_local // tile
    sub = tile // 3 if tile % (3 * LANES) == 0 else tile
    subs = tile // sub
    plan = [(0, 0, 1), (0, 1, 2), (1, 0, 2), (1, 2, 1)] if divisible else [(0, 0, 1), (1, 0, 1)]
    last = levels - 1
    keeps, arrivals, hiddens = {}, {}, {}
    token = [mlp_in]
    scale = [None]
    states = {}

    def gate_up(j):
        member, first, count = plan[j]
        first = first * subs
        weight = pl.BlockSpec((1, features, sub), lambda i: (member, 0, first + i))
        out = pl.BlockSpec((2, half, sub), lambda i: (i, 0, 0))
        groups = 2 * count * subs
        keep, send = call(
            gate_up_kernel,
            [mlp_in, w_gate, w_up],
            [pl.BlockSpec((tokens, features), lambda i: (0, 0)), weight, weight],
            token,
            grid=(count * subs,),
            out_shape=[shape((groups, half, sub), F32), shape((groups, half, sub), BF16)],
            out_specs=[out] * 2,
            compiler_params=params(56),
            cost_estimate=cost(4 * tokens * features * tile * count, 4 * tile * count * features),
            name="gate_up",
        )
        arrived = [col_xor(send, 1)]
        keeps[j] = [keep]
        if j == 0:
            keeps[j].append(square_keep)
            arrived.append(col_xor(square_send, 1))
        arrivals[j] = arrived
        token[:] = [send]

    def halve(j, level):
        count = plan[j][2]
        keep, received = keeps[j], arrivals[j]
        groups, rows, _ = keep[0].shape
        part = groups // count
        squared = len(keep) == 2
        specs = [pl.BlockSpec((part, rows, sub), lambda i: (i, 0, 0))] * 2
        outs = [pl.BlockSpec((part, rows // 2, sub), lambda i: (i, 0, 0))] * 2
        shapes = [shape((groups, rows // 2, sub), F32), shape((groups, rows // 2, sub), BF16)]
        operands = [keep[0], received[0]]
        if squared:
            operands += [keep[1], received[1]]
            specs = specs + [pl.BlockSpec((rows, LANES), lambda i: (0, 0))] * 2
            outs = outs + [pl.BlockSpec((rows // 2, LANES), lambda i: (0, 0))] * 2
            shapes += [shape((rows // 2, LANES), F32), shape((rows // 2, LANES), BF16)]
        result = call(
            functools.partial(halve_kernel, squared),
            operands,
            specs,
            token,
            grid=(count,),
            out_shape=shapes,
            out_specs=outs,
            compiler_params=params(24),
            cost_estimate=cost(rows * sub * groups, 9 * rows * sub * groups),
            name="halve",
        )
        keeps[j] = result[0::2]
        arrivals[j] = [col_xor(send, 2 << level) for send in result[1::2]]
        token[:] = [result[1]]

    def hidden_of(j):
        keep, received = keeps[j], arrivals[j]
        groups, rows, _ = keep[0].shape
        hidden_shape = shape((rows, groups // 2 * sub), BF16)
        scale_shape = shape((rows, LANES), F32)
        squared = len(keep) == 2
        operands = [keep[0], received[0]] + ([keep[1], received[1]] if squared else scale)
        result = call(
            functools.partial(hidden_kernel, squared),
            operands,
            [VMEM] * len(operands),
            token,
            out_shape=[hidden_shape, scale_shape] if squared else [hidden_shape],
            out_specs=[VMEM] * 2 if squared else [VMEM],
            compiler_params=params(24),
            cost_estimate=cost(8 * rows * groups * sub, 6 * rows * groups * sub),
            name="hidden",
        )
        if squared:
            scale[:] = [result[1]]
        hiddens[j] = (result[0], col_xor(result[0], 1 << last))
        token[:] = [result[0]]

    def join(j, level):
        first, second = hiddens[j]
        rows, width = first.shape
        joined = call(
            join_kernel,
            [first, second],
            [VMEM] * 2,
            token,
            out_shape=shape((2 * rows, width), BF16),
            out_specs=VMEM,
            compiler_params=params(16),
            cost_estimate=cost(rows * width, 8 * rows * width),
            name="join",
        )
        hiddens[j] = (joined, col_xor(joined, 1 << level))
        token[:] = [joined]

    def down(member):
        which = [j for j in range(len(plan)) if plan[j][0] == member]
        own = [hiddens[j][0] for j in which]
        other = [hiddens[j][1] for j in which]
        sources = [(k, i * tile) for k, j in enumerate(which) for i in range(plan[j][2])]
        parts = call(
            functools.partial(down_kernel, sources, len(own), col_tokens),
            [half_offsets, *own, *other, w_down],
            [SMEM]
            + [pl.BlockSpec(array.shape, lambda i: (0, 0)) for array in own + other]
            + [pl.BlockSpec((1, tile, features), lambda i: (member, i, 0))],
            token,
            grid=(tiles,),
            out_shape=[
                shape((row_tokens, features), F32 if i == 0 else BF16) for i in range(row_count)
            ],
            out_specs=[pl.BlockSpec((row_tokens, features), lambda i: (0, 0))] * row_count,
            scratch_shapes=[pltpu.VMEM((tokens, features), F32)],
            compiler_params=params(56),
            cost_estimate=cost(
                2 * tokens * features * ff_local, 2 * ff_local * (features + tokens)
            ),
            name="down",
        )
        states[member] = [parts[0]] + [row_xor(parts[j], j) for j in range(1, row_count)]
        token[:] = [parts[1]]

    def output(member):
        parts = states[member]
        scaled = call(
            output_kernel,
            [stream, final_gain[None, :], *parts],
            [VMEM] * (2 + row_count),
            token,
            out_shape=shape((row_tokens, features), BF16),
            out_specs=VMEM,
            compiler_params=params(16),
            cost_estimate=cost(8 * row_tokens * features, 16 * row_tokens * features),
            name="output",
        )
        states[member] = [scaled] + [col_xor(scaled, 2 * j) for j in range(1, chips)]
        token[:] = [scaled]

    def pack(member):
        by_chip = call(
            pack_kernel,
            states[member],
            [VMEM] * chips,
            token,
            out_shape=shape((chips, row_tokens, features), BF16),
            out_specs=VMEM,
            compiler_params=params(16),
            cost_estimate=cost(chips * row_tokens * features, 4 * chips * row_tokens * features),
            name="pack",
        )
        own = [by_chip] + [row_xor(by_chip, j) for j in range(1, row_count)]
        states[member] = own + [col_xor(array, 1) for array in own]
        token[:] = [by_chip]

    vocab_start = (row_index * col_count + col_index) * vocab_local
    local_targets = (targets - vocab_start)[:, None]
    vocab_tile = 512 if vocab_local % 512 == 0 else vocab_local
    vocab_tiles = vocab_local // vocab_tile
    stats = {0: [], 1: []}

    def head(member, first, count):
        state = states[member]
        result = call(
            functools.partial(head_kernel, row_count, first),
            [col_rel, row_rel * row_tokens, *state, gains, local_targets, w_head],
            [SMEM] * 2
            + [pl.BlockSpec(state[0].shape, lambda i: (0, 0, 0))] * (2 * row_count)
            + [pl.BlockSpec(gains.shape, lambda i: (0, 0))]
            + [pl.BlockSpec((tokens, 1), lambda i: (0, 0))]
            + [pl.BlockSpec((D, vocab_tile), lambda i: (0, first + i))],
            token,
            grid=(count,),
            out_shape=shape((tokens, LANES), F32),
            out_specs=pl.BlockSpec((tokens, LANES), lambda i: (0, 0)),
            scratch_shapes=[pltpu.VMEM((tokens, D), BF16)] + [pltpu.VMEM((tokens, 1), F32)] * 4,
            compiler_params=params(56),
            cost_estimate=cost(
                2 * tokens * D * vocab_tile * count, 2 * D * vocab_tile * count
            ),
            name="head",
        )
        token[:] = [result]
        stats[member].append(result[:, :3].T)

    if len(plan) == 4 and levels == 3:
        schedule = [
            (gate_up, 0), (gate_up, 1), (halve, 0, 0), (gate_up, 2), (halve, 1, 0),
            (halve, 0, 1), (gate_up, 3), (hidden_of, 0), (join, 0, 1), (halve, 2, 0),
            (halve, 1, 1), (join, 0, 0), (hidden_of, 1), (join, 1, 1), (halve, 3, 0),
            (halve, 2, 1), (join, 1, 0), (halve, 3, 1), (down, 0), (hidden_of, 2),
            (output, 0), (join, 2, 1), (hidden_of, 3), (pack, 0), (join, 3, 1),
            (join, 2, 0), (join, 3, 0), (down, 1),
        ]
    else:
        schedule = []
        for j in range(len(plan)):
            schedule += [(gate_up, j)] + [(halve, j, level) for level in range(last)]
            schedule += [(hidden_of, j)] + [(join, j, level) for level in range(last - 1, -1, -1)]
        schedule += [(down, 0), (output, 0), (pack, 0), (down, 1)]
    early = min(2, vocab_tiles)
    schedule += [(head, 0, 0, early), (output, 1), (pack, 1)]
    if early < vocab_tiles:
        schedule += [(head, 0, early, vocab_tiles - early)]
    schedule += [(head, 1, 0, vocab_tiles)]
    for step, *arguments in schedule:
        step(*arguments)

    def combine(parts):
        top = functools.reduce(jnp.maximum, [p[0] for p in parts])
        total = tree_sum([p[1] * jnp.exp(p[0] - top) for p in parts])
        picked = tree_sum([p[2] for p in parts])
        return jnp.stack([top, total, picked])

    merged = combine(stats[0]) if len(stats[0]) > 1 else stats[0][0]
    merged = jnp.stack([merged, stats[1][0]], axis=1)
    merged = combine([merged, col_xor(merged, 1)])
    merged = combine([merged] + [col_xor(merged, 2 * j) for j in range(1, chips)])
    merged = combine([merged] + [row_xor(merged, j) for j in range(1, row_count)])
    logprob = merged[2] - (merged[0] + jnp.log(merged[1]))
    difference = logprob[0] - logprob[1]
    one_hot = (segment[:, None] == jnp.arange(SEQS, dtype=jnp.int32)[None, :]).astype(F32)
    seq_sums = jnp.dot(difference, one_hot, precision=lax.Precision.HIGHEST)
    return seq_sums / seq_lengths.astype(F32)


def solution(mesh):
    placed = (
        P("row", "col"),
        P("col"),
        P("col", "row"),
        P("col", "row"),
        P("col", "row"),
        P("row", "col"),
        P("col"),
        P(None, "col", "row"),
        P(None, "col", "row"),
        P(None, "row", "col"),
        P("col"),
        P(None, ("row", "col")),
        P(),
        P(),
    )
    return jax.shard_map(per_device, mesh=mesh, in_specs=placed, out_specs=P(), check_vma=False)
```

```python
import functools

import jax
import jax.numpy as jnp
from jax import lax
from jax.experimental import pallas as pl
from jax.experimental.pallas import tpu as pltpu
from jax.sharding import PartitionSpec as P

D = 5120
HEAD_DIM = 128
SEQS = 8
LONGEST = 64

EPSILON = 1e-06
ROPE_BASE = 1000000.0
MASKED = -1e30
LANES = 128
HEAD_BLOCKS = 4
GATE_MIB = 46
BF16 = jnp.bfloat16
F32 = jnp.float32
MIB = 1 << 20

VMEM = pl.BlockSpec(memory_space=pltpu.VMEM)
ANY = pl.BlockSpec(memory_space=pl.ANY)
SMEM = pl.BlockSpec(memory_space=pltpu.SMEM)


def params(mib):
    return pltpu.CompilerParams(vmem_limit_bytes=mib * MIB)


def cost(flops, byte_count):
    del flops, byte_count
    return pl.CostEstimate(flops=1, bytes_accessed=1, transcendentals=0)


def call(kernel, operands, in_specs, token, out_shape, out_specs, **options):
    count, outs = len(operands), len(out_shape)

    def body(*refs):
        inputs, results, scratch = refs[:count], refs[count + 1 :], refs[count + outs + 2 :]
        kernel(*inputs, *results[:outs], *scratch)

    results = pl.pallas_call(
        body,
        in_specs=in_specs + [ANY],
        out_shape=out_shape + [jax.ShapeDtypeStruct((8, LANES), F32)],
        out_specs=out_specs + [ANY],
        **options,
    )(*operands, token[0])
    token[:] = [results[-1]]
    return results[:-1]


def row_xor(x, mask):
    count = lax.axis_size("row")
    return lax.ppermute(x, "row", [(i, i ^ mask) for i in range(count)])


def col_xor(x, mask):
    count = lax.axis_size("col")
    return lax.ppermute(x, "col", [(i, i ^ mask) for i in range(count)])


def tree_sum(values):
    values = list(values)
    while len(values) > 1:
        values = [values[i] + values[i + 1] for i in range(0, len(values), 2)]
    return values[0]


def sequence_layout(seq_lengths, token_index):
    ends_at = jnp.cumsum(seq_lengths)
    before = ends_at[None, :] <= token_index[:, None]
    segment = jnp.sum(before.astype(jnp.int32), axis=1)
    starts_at = jnp.sum(jnp.where(before, seq_lengths[None, :], 0), axis=1)
    return (segment, (token_index - starts_at).astype(F32))


def split_square(total):
    high = total.astype(BF16)
    low = (total - high.astype(F32)).astype(BF16)
    lane = lax.broadcasted_iota(jnp.int32, total.shape, 1)
    return jnp.where(lane < LANES // 2, high.astype(F32), low.astype(F32)).astype(BF16)


def join_square(tile):
    return tile + pltpu.roll(tile, LANES // 2, 1)


def assemble(offsets, blocks, gain, x_ref, square_ref, unit):
    step = 0
    for block in blocks:
        for first in range(0, block.shape[0], unit):
            rows = block[first : first + unit, :].astype(F32)
            place = pl.multiple_of(offsets[step], unit)
            x_ref[pl.ds(place, unit), :] = (rows * gain[...]).astype(BF16)
            square = jnp.sum(rows * rows, axis=1, keepdims=True)
            square_ref[pl.ds(place, unit), :] = jnp.broadcast_to(square, (unit, LANES))
            step += 1


def put_squares(square_ref, keep, send, at):
    half = keep.shape[0]
    total = square_ref[...]
    lane = lax.broadcasted_iota(jnp.int32, (half, LANES), 1)
    keep[:, at : at + LANES] = jnp.where(lane < LANES // 2, total[:half], 0.0)
    send[:, at : at + LANES] = split_square(total[half:])


def qkv_kernel(unit, count, offsets, *refs):
    blocks, (gain, wq, wk, wv, keep, send, x_ref, square_ref) = refs[:count], refs[count:]
    assemble(offsets, blocks, gain, x_ref, square_ref, unit)
    half = keep.shape[0]
    x = x_ref[...]
    at = 0
    for w in (wq, wk, wv):
        width = w.shape[1]
        part = jnp.dot(x, w[...], preferred_element_type=F32)
        keep[:, at : at + width] = part[:half]
        send[:, at : at + width] = part[half:].astype(BF16)
        at += width
    put_squares(square_ref, keep, send, at)


def core_add_kernel(keep, recv, *outs):
    rows, width = outs[0].shape
    for i, out in enumerate(outs):
        total = keep[i * rows : (i + 1) * rows, :] + recv[
            i * rows : (i + 1) * rows, :
        ].astype(F32)
        if i == 0:
            out[...] = total
        else:
            out[:, : width - LANES] = total[:, : width - LANES].astype(BF16)
            out[:, width - LANES :] = split_square(join_square(total[:, width - LANES :]))


def rope_kernel(rotated, count, *refs):
    parts, (cosine, sine, out) = refs[:count], refs[count:]
    width = out.shape[1]

    def summed(at):
        total = parts[0][:, at : at + LANES].astype(F32)
        for part in parts[1:]:
            total = total + part[:, at : at + LANES].astype(F32)
        return total

    scale = lax.rsqrt(join_square(summed(width)) / D + EPSILON)
    for at in range(0, width, HEAD_DIM):
        total = summed(at) * scale
        if at < rotated:
            total = total * cosine[...] + pltpu.roll(total, HEAD_DIM // 2, 1) * sine[...]
        out[:, at : at + HEAD_DIM] = total.astype(BF16)


def attention_kernel(heads, kv_heads, count, block, places, row_places, *refs):
    pieces, (bias, w_out), outs, (qkv, attended) = (
        refs[:count],
        refs[count : count + 2],
        refs[count + 2 : -2],
        refs[-2:],
    )
    row_unit = outs[0].shape[0]
    unit = pieces[0].shape[0]
    for i, piece in enumerate(pieces):
        qkv[pl.ds(pl.multiple_of(places[i], unit), unit), :] = piece[...]
    tokens = qkv.shape[0]
    group = heads // kv_heads
    window = min(tokens, block + LONGEST)
    for start in range(0, tokens, block):
        first = max(0, start + block - window)
        mask = bias[start : start + block, :]
        mask = jnp.concatenate([mask] * group, axis=0)
        for g in range(kv_heads):
            q = jnp.concatenate(
                [
                    qkv[start : start + block, h * HEAD_DIM : (h + 1) * HEAD_DIM]
                    for h in range(g * group, (g + 1) * group)
                ],
                axis=0,
            )
            k_at = (heads + g) * HEAD_DIM
            v_at = (heads + kv_heads + g) * HEAD_DIM
            k = qkv[first : first + window, k_at : k_at + HEAD_DIM]
            v = qkv[first : first + window, v_at : v_at + HEAD_DIM]
            scores = lax.dot_general(
                q, k, (((1,), (1,)), ((), ())), preferred_element_type=F32
            ) * HEAD_DIM ** (-0.5)
            scores = scores + mask
            weights = jnp.exp(scores - jnp.max(scores, axis=1, keepdims=True))
            total = jnp.sum(weights, axis=1, keepdims=True)
            weights = (weights / total).astype(BF16)
            result = jnp.dot(weights, v, preferred_element_type=F32).astype(BF16)
            for h in range(group):
                at = (g * group + h) * HEAD_DIM
                for sub in range(0, block, row_unit):
                    place = pl.multiple_of(row_places[(start + sub) // row_unit], row_unit)
                    attended[pl.ds(place, row_unit), at : at + HEAD_DIM] = result[
                        h * block + sub : h * block + sub + row_unit
                    ]
    product = jnp.dot(attended[...], w_out[...], preferred_element_type=F32)
    for i, out in enumerate(outs):
        out[...] = product[i * row_unit : (i + 1) * row_unit].astype(out.dtype)


def arrange_kernel(unit, offsets, *refs):
    blocks, (gain, out, keep, send, square) = refs[:-5], refs[-5:]
    assemble(offsets, blocks, gain, out, square, unit)
    put_squares(square, keep, send, 0)


def gate_up_kernel(x, *refs):
    weights, (keep, send) = refs[:-2], refs[-2:]
    half = keep.shape[1]
    count = len(weights) // 2
    for i in range(2):
        w = jnp.concatenate([w[0] for w in weights[i * count : (i + 1) * count]], axis=0)
        part = jnp.dot(x[...], w, preferred_element_type=F32)
        keep[i] = part[:half]
        send[i] = part[half:].astype(BF16)


def halve_kernel(squares, *refs):
    if squares:
        keep, recv, square_keep, square_recv, kept, send, square_kept, square_send = refs
        half = square_kept.shape[0]
        total = square_keep[...] + square_recv[...].astype(F32)
        square_kept[...] = total[:half]
        square_send[...] = split_square(join_square(total[half:]))
    else:
        keep, recv, kept, send = refs
    half = kept.shape[1]
    kept[...] = keep[:, :half, :] + recv[:, :half, :].astype(F32)
    send[...] = (keep[:, half:, :] + recv[:, half:, :].astype(F32)).astype(BF16)


def hidden_kernel(squares, keep, recv, *refs):
    if squares:
        square_keep, square_recv, hidden, scale_ref = refs
        total = square_keep[...] + square_recv[...].astype(F32)
        scale_ref[...] = lax.rsqrt(join_square(total) / D + EPSILON)
    else:
        scale_ref, hidden = refs
    scale = scale_ref[:, :1]
    width = keep.shape[2]
    for i in range(keep.shape[0] // 2):
        gate = (keep[2 * i] + recv[2 * i].astype(F32)) * scale
        up = (keep[2 * i + 1] + recv[2 * i + 1].astype(F32)) * scale
        hidden[:, i * width : (i + 1) * width] = (
            gate / (1.0 + jnp.exp(-gate)) * up
        ).astype(BF16)


def join_kernel(first, second, out):
    rows = first.shape[0]
    out[:rows] = first[...]
    out[rows:] = second[...]


def pack_kernel(*refs):
    parts, out = refs[:-1], refs[-1]
    for i, part in enumerate(parts):
        out[i] = part[...]


def output_kernel(stream, gain, *refs):
    parts, out = refs[:-1], refs[-1]
    total = stream[...].astype(F32)
    for part in parts:
        total = total + part[...].astype(F32)
    out[...] = (total * gain[...]).astype(BF16)


def down_kernel(sources, count, unit, rows, offsets, *refs):
    own, other, weights = refs[:count], refs[count : 2 * count], refs[2 * count : -rows - 1]
    outs, total = refs[-rows - 1 : -1], refs[-1]
    tile = len(weights) * weights[0].shape[1]
    for i, (which, at) in enumerate(sources):

        @pl.when(pl.program_id(0) == i)
        def _():
            hidden = jnp.concatenate(
                [own[which][:, at : at + tile], other[which][:, at : at + tile]], axis=0
            )
            w = jnp.concatenate([w[0] for w in weights], axis=0)
            part = jnp.dot(hidden, w, preferred_element_type=F32)
            total[...] = part if i == 0 else total[...] + part

    @pl.when(pl.program_id(0) == len(sources) - 1)
    def _():
        step = 0
        for out in outs:
            for first in range(0, out.shape[0], unit):
                place = pl.multiple_of(offsets[step], unit)
                out[first : first + unit, :] = total[pl.ds(place, unit), :].astype(out.dtype)
                step += 1


def head_kernel(rows, first, col_index, row_places, *refs):
    own, other = refs[:rows], refs[rows : 2 * rows]
    gains, target, *weights = refs[2 * rows : -6]
    out, lhs, square, top, total, picked = refs[-6:]
    step = pl.program_id(0)
    chips, unit, width = own[0].shape

    @pl.when(step == 0)
    def _():
        inverse = 1.0 / gains[...]
        for i in range(rows):
            place = pl.multiple_of(row_places[i], unit)
            sums = jnp.zeros((unit, 1), F32)
            for core, arrays in enumerate((own, other)):
                for j in range(chips):
                    feature = pl.multiple_of(col_index[2 * j + core] * width, LANES)
                    values = arrays[i][j]
                    lhs[pl.ds(place, unit), pl.ds(feature, width)] = values
                    plain = values.astype(F32) * inverse[2 * j + core : 2 * j + core + 1, :]
                    sums += jnp.sum(plain * plain, axis=1, keepdims=True)
            square[pl.ds(place, unit), :] = sums
        top[...] = jnp.full_like(top, MASKED)
        total[...] = jnp.zeros_like(total)
        picked[...] = jnp.zeros_like(picked)

    depth = weights[0].shape[0]
    logits = jnp.dot(lhs[:, :depth], weights[0][...], preferred_element_type=F32)
    for i in range(1, len(weights)):
        logits += jnp.dot(
            lhs[:, i * depth : (i + 1) * depth], weights[i][...], preferred_element_type=F32
        )
    logits = logits * lax.rsqrt(square[...] / D + EPSILON)
    lane = lax.broadcasted_iota(jnp.int32, logits.shape, 1)
    lane = lane + (step + first) * logits.shape[1]
    hit = jnp.where(lane == target[...], logits, 0.0)
    picked[...] += jnp.sum(hit, axis=1, keepdims=True)
    new_top = jnp.maximum(top[...], jnp.max(logits, axis=1, keepdims=True))
    total[...] = total[...] * jnp.exp(top[...] - new_top) + jnp.sum(
        jnp.exp(logits - new_top), axis=1, keepdims=True
    )
    top[...] = new_top

    @pl.when(step == pl.num_programs(0) - 1)
    def _():
        place = lax.broadcasted_iota(jnp.int32, out.shape, 1)
        out[...] = jnp.where(
            place == 0, top[...], jnp.where(place == 1, total[...], picked[...])
        )


def hold(arrays, token):
    def kernel(*refs):
        del refs

    count = len(arrays)
    results = pl.pallas_call(
        kernel,
        out_shape=[jax.ShapeDtypeStruct(array.shape, array.dtype) for array in arrays]
        + [jax.ShapeDtypeStruct((8, LANES), F32)],
        in_specs=[ANY] * (count + 1),
        out_specs=[ANY] * (count + 1),
        input_output_aliases={i: i for i in range(count)},
        compiler_params=params(16),
        cost_estimate=cost(0, 0),
        name="hold",
    )(*arrays, token[0])
    token[:] = [results[-1]]
    return results[:-1]


def per_device(
    residual,
    attn_gain,
    w_query,
    w_key,
    w_value,
    w_out,
    mlp_gain,
    w_gate,
    w_up,
    w_down,
    final_gain,
    w_head,
    seq_lengths,
    targets,
):
    row_count = lax.axis_size("row")
    col_count = lax.axis_size("col")
    chips = col_count // 2
    row_index = lax.axis_index("row")
    col_index = lax.axis_index("col")
    core = col_index % 2
    chip = col_index // 2
    row_tokens, features = residual.shape
    tokens = row_tokens * row_count
    col_tokens = tokens // col_count
    quarter = tokens // 4
    heads = w_query.shape[1] // HEAD_DIM
    kv_heads = w_key.shape[1] // HEAD_DIM
    qkv_width = w_query.shape[1] + 2 * w_key.shape[1]
    rotated = w_query.shape[1] + w_key.shape[1]
    ff_local = w_gate.shape[2]
    vocab_local = w_head.shape[1]

    row_range = jnp.arange(row_count, dtype=jnp.int32)
    col_range = jnp.arange(col_count, dtype=jnp.int32)
    row_rel = row_range ^ row_index
    col_rel = col_range ^ col_index

    token_index = jnp.arange(tokens, dtype=jnp.int32)
    segment, positions = sequence_layout(seq_lengths, token_index)
    block = min(64, tokens)
    window = min(tokens, block + LONGEST)
    first_key = jnp.maximum(0, (token_index // block + 1) * block - window)
    key_index = first_key[:, None] + jnp.arange(window, dtype=jnp.int32)[None, :]
    key_segment, _ = sequence_layout(seq_lengths, key_index.reshape(-1))
    allowed = (key_segment.reshape(tokens, window) == segment[:, None]) & (
        key_index <= token_index[:, None]
    )
    bias = jnp.where(allowed, 0.0, MASKED).astype(F32)
    own_positions = lax.dynamic_slice_in_dim(positions, col_index * col_tokens, col_tokens)
    exponent = jnp.arange(HEAD_DIM // 2, dtype=F32) * 2.0 / HEAD_DIM
    angles = own_positions[:, None] * (ROPE_BASE ** (-exponent))[None, :]
    cosine, sine = jnp.cos(angles), jnp.sin(angles)
    cosine = jnp.concatenate([cosine, cosine], axis=1)
    sine = jnp.concatenate([-sine, sine], axis=1)

    blocks = [residual] + [row_xor(residual, j) for j in range(1, row_count)]
    shape = jax.ShapeDtypeStruct

    per_row = row_tokens // col_tokens
    col_block = (row_rel[:, None] * per_row + jnp.arange(per_row, dtype=jnp.int32)).reshape(-1)
    relative = col_block ^ col_index
    offsets = ((relative & 1) * chips + (relative >> 1)) * col_tokens
    half = tokens // 2
    wide = qkv_width + LANES
    keep, send = pl.pallas_call(
        functools.partial(qkv_kernel, col_tokens, row_count),
        out_shape=[shape((half, wide), F32), shape((half, wide), BF16)],
        in_specs=[SMEM] + [VMEM] * (row_count + 4),
        out_specs=[VMEM] * 2,
        scratch_shapes=[pltpu.VMEM((tokens, features), BF16), pltpu.VMEM((tokens, LANES), F32)],
        compiler_params=params(56),
        cost_estimate=cost(
            2 * tokens * features * qkv_width, 2 * qkv_width * (features + tokens)
        ),
        name="qkv_partial",
    )(offsets, *blocks, attn_gain[None, :], w_query, w_key, w_value)
    received = col_xor(send, 1)
    parts = pl.pallas_call(
        core_add_kernel,
        out_shape=[shape((col_tokens, wide), F32 if i == 0 else BF16) for i in range(chips)],
        in_specs=[VMEM] * 2,
        out_specs=[VMEM] * chips,
        compiler_params=params(16),
        cost_estimate=cost(half * qkv_width, 6 * half * qkv_width),
        name="qkv_core_add",
    )(keep, received)
    parts = [parts[0]] + [col_xor(parts[j], 2 * j) for j in range(1, chips)]
    mine = pl.pallas_call(
        functools.partial(rope_kernel, rotated, chips),
        out_shape=shape((col_tokens, qkv_width), BF16),
        in_specs=[VMEM] * (chips + 2),
        out_specs=VMEM,
        compiler_params=params(16),
        cost_estimate=cost(8 * col_tokens * qkv_width, 2 * tokens * qkv_width),
        name="qkv_rope",
    )(*parts, cosine, sine)
    pieces = [mine] + [col_xor(mine, 2 * j) for j in range(1, chips)]
    pieces = pieces + [col_xor(piece, 1) for piece in pieces]
    piece_index = [2 * j for j in range(chips)] + [2 * j + 1 for j in range(chips)]
    places = (jnp.array(piece_index, jnp.int32) ^ col_index) * col_tokens

    projected = pl.pallas_call(
        functools.partial(attention_kernel, heads, kv_heads, col_count, block),
        out_shape=[
            shape((row_tokens, features), F32 if i == 0 else BF16) for i in range(row_count)
        ],
        in_specs=[SMEM] * 2 + [VMEM] * (col_count + 2),
        out_specs=[VMEM] * row_count,
        scratch_shapes=[
            pltpu.VMEM((tokens, qkv_width), BF16),
            pltpu.VMEM((tokens, heads * HEAD_DIM), BF16),
        ],
        compiler_params=params(32),
        cost_estimate=cost(
            2 * tokens * heads * HEAD_DIM * features * 2, 2 * heads * HEAD_DIM * features * 2
        ),
        name="attention_out",
    )(places, row_rel * row_tokens, *pieces, bias, w_out)
    projected = [projected[0]] + [row_xor(projected[j], j) for j in range(1, row_count)]
    stream = residual.astype(F32) + tree_sum([p.astype(F32) for p in projected])
    stream = lax.optimization_barrier(stream.astype(BF16))

    levels = (col_count - 1).bit_length()
    blocks = [stream] + [row_xor(stream, j) for j in range(1, row_count)]
    position = sum(((relative >> level) & 1) << (levels - 1 - level) for level in range(levels))
    half_offsets = position * col_tokens
    token = [mlp_gain]
    mlp_in, square_keep, square_send = call(
        functools.partial(arrange_kernel, col_tokens),
        [half_offsets, *blocks, mlp_gain[None, :]],
        [SMEM] + [VMEM] * (row_count + 1),
        token,
        out_shape=[
            shape((tokens, features), BF16),
            shape((half, LANES), F32),
            shape((half, LANES), BF16),
        ],
        out_specs=[VMEM] * 3,
        scratch_shapes=[pltpu.VMEM((tokens, LANES), F32)],
        compiler_params=params(16),
        cost_estimate=cost(tokens * features, 4 * tokens * features),
        name="mlp_in",
    )

    divisible = ff_local % (3 * LANES) == 0
    tile = ff_local // 3 if divisible else ff_local
    tiles = ff_local // tile
    sub = tile // 3 if tile % (3 * LANES) == 0 else tile
    subs = tile // sub
    plan = [(0, 0, 1), (0, 1, 2), (1, 0, 2), (1, 2, 1)] if divisible else [(0, 0, 1), (1, 0, 1)]
    last = levels - 1
    keeps, arrivals, hiddens = {}, {}, {}
    scale = [None]
    states = {}

    def gate_up(j):
        member, first, count = plan[j]
        first = first * subs
        weights = [
            pl.BlockSpec((1, features // 2, sub), lambda i, q=q: (member, q, first + i))
            for q in range(2)
        ]
        out = pl.BlockSpec((2, half, sub), lambda i: (i, 0, 0))
        groups = 2 * count * subs
        keep, send = call(
            gate_up_kernel,
            [mlp_in, w_gate, w_gate, w_up, w_up],
            [pl.BlockSpec((tokens, features), lambda i: (0, 0))] + weights * 2,
            token,
            grid=(count * subs,),
            out_shape=[shape((groups, half, sub), F32), shape((groups, half, sub), BF16)],
            out_specs=[out] * 2,
            compiler_params=params(GATE_MIB),
            cost_estimate=cost(4 * tokens * features * tile * count, 4 * tile * count * features),
            name="gate_up",
        )
        arrived = [col_xor(send, 1)]
        keeps[j] = [keep]
        if j == 0:
            keeps[j].append(square_keep)
            arrived.append(col_xor(square_send, 1))
        arrivals[j] = arrived

    def halve(j, level):
        count = plan[j][2]
        keep, received = keeps[j], arrivals[j]
        groups, rows, _ = keep[0].shape
        part = groups // count
        squared = len(keep) == 2
        specs = [pl.BlockSpec((part, rows, sub), lambda i: (i, 0, 0))] * 2
        outs = [pl.BlockSpec((part, rows // 2, sub), lambda i: (i, 0, 0))] * 2
        shapes = [shape((groups, rows // 2, sub), F32), shape((groups, rows // 2, sub), BF16)]
        operands = [keep[0], received[0]]
        if squared:
            operands += [keep[1], received[1]]
            specs = specs + [pl.BlockSpec((rows, LANES), lambda i: (0, 0))] * 2
            outs = outs + [pl.BlockSpec((rows // 2, LANES), lambda i: (0, 0))] * 2
            shapes += [shape((rows // 2, LANES), F32), shape((rows // 2, LANES), BF16)]
        result = call(
            functools.partial(halve_kernel, squared),
            operands,
            specs,
            token,
            grid=(count,),
            out_shape=shapes,
            out_specs=outs,
            compiler_params=params(24),
            cost_estimate=cost(rows * sub * groups, 9 * rows * sub * groups),
            name="halve",
        )
        keeps[j] = result[0::2]
        arrivals[j] = [col_xor(send, 2 << level) for send in result[1::2]]

    def hidden_of(j):
        keep, received = keeps[j], arrivals[j]
        groups, rows, _ = keep[0].shape
        hidden_shape = shape((rows, groups // 2 * sub), BF16)
        scale_shape = shape((rows, LANES), F32)
        squared = len(keep) == 2
        operands = [keep[0], received[0]] + ([keep[1], received[1]] if squared else scale)
        result = call(
            functools.partial(hidden_kernel, squared),
            operands,
            [VMEM] * len(operands),
            token,
            out_shape=[hidden_shape, scale_shape] if squared else [hidden_shape],
            out_specs=[VMEM] * 2 if squared else [VMEM],
            compiler_params=params(24),
            cost_estimate=cost(8 * rows * groups * sub, 6 * rows * groups * sub),
            name="hidden",
        )
        if squared:
            scale[:] = [result[1]]
        hiddens[j] = (result[0], col_xor(result[0], 1 << last))

    def join(j, level):
        first, second = hiddens[j]
        rows, width = first.shape
        (joined,) = call(
            join_kernel,
            [first, second],
            [VMEM] * 2,
            token,
            out_shape=[shape((2 * rows, width), BF16)],
            out_specs=[VMEM],
            compiler_params=params(16),
            cost_estimate=cost(rows * width, 8 * rows * width),
            name="join",
        )
        hiddens[j] = (joined, col_xor(joined, 1 << level))

    def down(member):
        which = [j for j in range(len(plan)) if plan[j][0] == member]
        own = [hiddens[j][0] for j in which]
        other = [hiddens[j][1] for j in which]
        sources = [(k, i * tile) for k, j in enumerate(which) for i in range(plan[j][2])]
        parts = call(
            functools.partial(down_kernel, sources, len(own), col_tokens, row_count),
            [half_offsets, *own, *other] + [w_down] * 3,
            [SMEM]
            + [pl.BlockSpec(array.shape, lambda i: (0, 0)) for array in own + other]
            + [
                pl.BlockSpec((1, tile // 3, features), lambda i, q=q: (member, 3 * i + q, 0))
                for q in range(3)
            ],
            token,
            grid=(tiles,),
            out_shape=[
                shape((row_tokens, features), F32 if i == 0 else BF16)
                for i in range(row_count)
            ],
            out_specs=[pl.BlockSpec((row_tokens, features), lambda i: (0, 0))] * row_count,
            scratch_shapes=[pltpu.VMEM((tokens, features), F32)],
            compiler_params=params(56),
            cost_estimate=cost(
                2 * tokens * features * ff_local, 2 * ff_local * (features + tokens)
            ),
            name="down",
        )
        states[member] = [parts[0]] + [row_xor(parts[j], j) for j in range(1, row_count)]

    def output(member):
        parts = states[member]
        (scaled,) = call(
            output_kernel,
            [stream, final_gain[None, :], *parts],
            [VMEM] * (2 + row_count),
            token,
            out_shape=[shape((row_tokens, features), BF16)],
            out_specs=[VMEM],
            compiler_params=params(16),
            cost_estimate=cost(8 * row_tokens * features, 16 * row_tokens * features),
            name="output",
        )
        states[member] = [scaled] + [col_xor(scaled, 2 * j) for j in range(1, chips)]

    def pack(member):
        (by_chip,) = call(
            pack_kernel,
            states[member],
            [VMEM] * chips,
            token,
            out_shape=[shape((chips, row_tokens, features), BF16)],
            out_specs=[VMEM],
            compiler_params=params(16),
            cost_estimate=cost(chips * row_tokens * features, 4 * chips * row_tokens * features),
            name="pack",
        )
        other = col_xor(by_chip, 1)
        states[member] = [by_chip, other] + [row_xor(by_chip, j) for j in range(1, row_count)]

    def forward(member):
        by_chip, other, *rows = states[member]
        rows = hold(rows, token)
        states[member] = [by_chip, *rows, other] + [col_xor(array, 1) for array in rows]

    vocab_start = (row_index * col_count + col_index) * vocab_local
    local_targets = (targets - vocab_start)[:, None]
    vocab_tile = 512 if vocab_local % 512 == 0 else vocab_local
    vocab_tiles = vocab_local // vocab_tile
    stats = {0: [], 1: []}

    gain_parts = [final_gain[None, :]]

    def gather_gain(level):
        (part,) = hold(gain_parts[-1:], token)
        gain_parts.append(jnp.concatenate([part, col_xor(part, 1 << level)], axis=0))

    def head(member, first, count):
        gains = gain_parts[-1]
        state = states[member]
        (result,) = call(
            functools.partial(head_kernel, row_count, first),
            [col_rel, row_rel * row_tokens, *state, gains, local_targets] + [w_head] * HEAD_BLOCKS,
            [SMEM] * 2
            + [pl.BlockSpec(state[0].shape, lambda i: (0, 0, 0))] * (2 * row_count)
            + [pl.BlockSpec(gains.shape, lambda i: (0, 0))]
            + [pl.BlockSpec((tokens, 1), lambda i: (0, 0))]
            + [
                pl.BlockSpec((D // HEAD_BLOCKS, vocab_tile), lambda i, q=q: (q, first + i))
                for q in range(HEAD_BLOCKS)
            ],
            token,
            grid=(count,),
            out_shape=[shape((tokens, LANES), F32)],
            out_specs=[pl.BlockSpec((tokens, LANES), lambda i: (0, 0))],
            scratch_shapes=[pltpu.VMEM((tokens, D), BF16)] + [pltpu.VMEM((tokens, 1), F32)] * 4,
            compiler_params=params(56),
            cost_estimate=cost(
                2 * tokens * D * vocab_tile * count, 2 * D * vocab_tile * count
            ),
            name="head",
        )
        stats[member].append(result[:, :3].T)

    if len(plan) == 4 and levels == 3:
        schedule = [
            (gate_up, 0), (gate_up, 1), (halve, 0, 0), (gate_up, 2), (halve, 1, 0),
            (halve, 0, 1), (gate_up, 3), (halve, 2, 0), (hidden_of, 0), (halve, 1, 1),
            (halve, 3, 0), (join, 0, 1), (gather_gain, 0), (hidden_of, 1), (halve, 2, 1),
            (join, 0, 0), (join, 1, 1), (gather_gain, 1), (halve, 3, 1), (hidden_of, 2),
            (join, 1, 0), (join, 2, 1), (gather_gain, 2), (down, 0), (hidden_of, 3),
            (join, 3, 1), (output, 0), (join, 2, 0), (join, 3, 0), (down, 1),
        ]
    else:
        schedule = []
        for j in range(len(plan)):
            schedule += [(gate_up, j)] + [(halve, j, level) for level in range(last)]
            schedule += [(hidden_of, j)] + [(join, j, level) for level in range(last - 1, -1, -1)]
        schedule += [(gather_gain, level) for level in range(levels)]
        schedule += [(down, 0), (output, 0), (down, 1)]
    early = (3 * vocab_tiles + 4) // 5
    schedule += [(output, 1), (pack, 0), (pack, 1), (forward, 0), (head, 0, 0, early)]
    schedule += [(forward, 1)]
    if early < vocab_tiles:
        schedule += [(head, 0, early, vocab_tiles - early)]
    schedule += [(head, 1, 0, vocab_tiles)]
    for step, *arguments in schedule:
        step(*arguments)

    def combine(parts):
        top = functools.reduce(jnp.maximum, [p[0] for p in parts])
        total = tree_sum([p[1] * jnp.exp(p[0] - top) for p in parts])
        picked = tree_sum([p[2] for p in parts])
        return jnp.stack([top, total, picked])

    merged = combine(stats[0]) if len(stats[0]) > 1 else stats[0][0]
    merged = jnp.stack([merged, stats[1][0]], axis=1)
    merged = combine([merged, col_xor(merged, 1)])
    merged = combine([merged] + [col_xor(merged, 2 * j) for j in range(1, chips)])
    merged = combine([merged] + [row_xor(merged, j) for j in range(1, row_count)])
    logprob = merged[2] - (merged[0] + jnp.log(merged[1]))
    difference = logprob[0] - logprob[1]
    one_hot = (segment[:, None] == jnp.arange(SEQS, dtype=jnp.int32)[None, :]).astype(F32)
    seq_sums = jnp.dot(difference, one_hot, precision=lax.Precision.HIGHEST)
    return seq_sums / seq_lengths.astype(F32)


def solution(mesh):
    placed = (
        P("row", "col"),
        P("col"),
        P("col", "row"),
        P("col", "row"),
        P("col", "row"),
        P("row", "col"),
        P("col"),
        P(None, "col", "row"),
        P(None, "col", "row"),
        P(None, "row", "col"),
        P("col"),
        P(None, ("row", "col")),
        P(),
        P(),
    )
    return jax.shard_map(per_device, mesh=mesh, in_specs=placed, out_specs=P(), check_vma=False)
```

```python
import functools

import jax
import jax.numpy as jnp
from jax import lax
from jax.experimental import pallas as pl
from jax.experimental.pallas import tpu as pltpu
from jax.sharding import PartitionSpec as P

D = 5120
HEAD_DIM = 128
SEQS = 8
LONGEST = 64

EPSILON = 1e-06
ROPE_BASE = 1000000.0
MASKED = -1e30
LANES = 128
HEAD_BLOCKS = 4
GATE_MIB = 46
BF16 = jnp.bfloat16
F32 = jnp.float32
MIB = 1 << 20

VMEM = pl.BlockSpec(memory_space=pltpu.VMEM)
ANY = pl.BlockSpec(memory_space=pl.ANY)
SMEM = pl.BlockSpec(memory_space=pltpu.SMEM)


def params(mib):
    return pltpu.CompilerParams(vmem_limit_bytes=mib * MIB)


def cost(flops, byte_count):
    del flops, byte_count
    return pl.CostEstimate(flops=1, bytes_accessed=1, transcendentals=0)


def call(kernel, operands, in_specs, token, out_shape, out_specs, **options):
    count, outs = len(operands), len(out_shape)

    def body(*refs):
        inputs, results, scratch = refs[:count], refs[count + 1 :], refs[count + outs + 2 :]
        kernel(*inputs, *results[:outs], *scratch)

    results = pl.pallas_call(
        body,
        in_specs=in_specs + [ANY],
        out_shape=out_shape + [jax.ShapeDtypeStruct((8, LANES), F32)],
        out_specs=out_specs + [ANY],
        **options,
    )(*operands, token[0])
    token[:] = [results[-1]]
    return results[:-1]


def row_xor(x, mask):
    count = lax.axis_size("row")
    return lax.ppermute(x, "row", [(i, i ^ mask) for i in range(count)])


def col_xor(x, mask):
    count = lax.axis_size("col")
    return lax.ppermute(x, "col", [(i, i ^ mask) for i in range(count)])


def tree_sum(values):
    values = list(values)
    while len(values) > 1:
        values = [values[i] + values[i + 1] for i in range(0, len(values), 2)]
    return values[0]


def sequence_layout(seq_lengths, token_index):
    ends_at = jnp.cumsum(seq_lengths)
    before = ends_at[None, :] <= token_index[:, None]
    segment = jnp.sum(before.astype(jnp.int32), axis=1)
    starts_at = jnp.sum(jnp.where(before, seq_lengths[None, :], 0), axis=1)
    return (segment, (token_index - starts_at).astype(F32))


def split_square(total):
    high = total.astype(BF16)
    low = (total - high.astype(F32)).astype(BF16)
    lane = lax.broadcasted_iota(jnp.int32, total.shape, 1)
    return jnp.where(lane < LANES // 2, high.astype(F32), low.astype(F32)).astype(BF16)


def join_square(tile):
    return tile + pltpu.roll(tile, LANES // 2, 1)


def assemble(offsets, blocks, gain, x_ref, square_ref, unit):
    step = 0
    for block in blocks:
        for first in range(0, block.shape[0], unit):
            rows = block[first : first + unit, :].astype(F32)
            place = pl.multiple_of(offsets[step], unit)
            x_ref[pl.ds(place, unit), :] = (rows * gain[...]).astype(BF16)
            square = jnp.sum(rows * rows, axis=1, keepdims=True)
            square_ref[pl.ds(place, unit), :] = jnp.broadcast_to(square, (unit, LANES))
            step += 1


def put_squares(square_ref, keep, send, at):
    half = keep.shape[0]
    total = square_ref[...]
    lane = lax.broadcasted_iota(jnp.int32, (half, LANES), 1)
    keep[:, at : at + LANES] = jnp.where(lane < LANES // 2, total[:half], 0.0)
    send[:, at : at + LANES] = split_square(total[half:])


def qkv_kernel(unit, count, offsets, *refs):
    blocks, (gain, wq, wk, wv, keep, send, x_ref, square_ref) = refs[:count], refs[count:]
    assemble(offsets, blocks, gain, x_ref, square_ref, unit)
    half = keep.shape[0]
    x = x_ref[...]
    at = 0
    for w in (wq, wk, wv):
        width = w.shape[1]
        part = jnp.dot(x, w[...], preferred_element_type=F32)
        keep[:, at : at + width] = part[:half]
        send[:, at : at + width] = part[half:].astype(BF16)
        at += width
    put_squares(square_ref, keep, send, at)


def core_add_kernel(keep, recv, *outs):
    rows, width = outs[0].shape
    for i, out in enumerate(outs):
        total = keep[i * rows : (i + 1) * rows, :] + recv[
            i * rows : (i + 1) * rows, :
        ].astype(F32)
        if i == 0:
            out[...] = total
        else:
            out[:, : width - LANES] = total[:, : width - LANES].astype(BF16)
            out[:, width - LANES :] = split_square(join_square(total[:, width - LANES :]))


def rope_kernel(rotated, count, *refs):
    parts, (cosine, sine, out) = refs[:count], refs[count:]
    width = out.shape[1]

    def summed(at):
        total = parts[0][:, at : at + LANES].astype(F32)
        for part in parts[1:]:
            total = total + part[:, at : at + LANES].astype(F32)
        return total

    scale = lax.rsqrt(join_square(summed(width)) / D + EPSILON)
    for at in range(0, width, HEAD_DIM):
        total = summed(at) * scale
        if at < rotated:
            total = total * cosine[...] + pltpu.roll(total, HEAD_DIM // 2, 1) * sine[...]
        out[:, at : at + HEAD_DIM] = total.astype(BF16)


def attention_kernel(heads, kv_heads, count, block, places, row_places, *refs):
    pieces, (bias, w_out), outs, (qkv, attended) = (
        refs[:count],
        refs[count : count + 2],
        refs[count + 2 : -2],
        refs[-2:],
    )
    row_unit = outs[0].shape[0]
    unit = pieces[0].shape[0]
    for i, piece in enumerate(pieces):
        qkv[pl.ds(pl.multiple_of(places[i], unit), unit), :] = piece[...]
    tokens = qkv.shape[0]
    group = heads // kv_heads
    window = min(tokens, block + LONGEST)
    for start in range(0, tokens, block):
        first = max(0, start + block - window)
        mask = bias[start : start + block, :]
        mask = jnp.concatenate([mask] * group, axis=0)
        for g in range(kv_heads):
            q = jnp.concatenate(
                [
                    qkv[start : start + block, h * HEAD_DIM : (h + 1) * HEAD_DIM]
                    for h in range(g * group, (g + 1) * group)
                ],
                axis=0,
            )
            k_at = (heads + g) * HEAD_DIM
            v_at = (heads + kv_heads + g) * HEAD_DIM
            k = qkv[first : first + window, k_at : k_at + HEAD_DIM]
            v = qkv[first : first + window, v_at : v_at + HEAD_DIM]
            scores = lax.dot_general(
                q, k, (((1,), (1,)), ((), ())), preferred_element_type=F32
            ) * HEAD_DIM ** (-0.5)
            scores = scores + mask
            weights = jnp.exp(scores - jnp.max(scores, axis=1, keepdims=True))
            total = jnp.sum(weights, axis=1, keepdims=True)
            weights = (weights / total).astype(BF16)
            result = jnp.dot(weights, v, preferred_element_type=F32).astype(BF16)
            for h in range(group):
                at = (g * group + h) * HEAD_DIM
                for sub in range(0, block, row_unit):
                    place = pl.multiple_of(row_places[(start + sub) // row_unit], row_unit)
                    attended[pl.ds(place, row_unit), at : at + HEAD_DIM] = result[
                        h * block + sub : h * block + sub + row_unit
                    ]
    product = jnp.dot(attended[...], w_out[...], preferred_element_type=F32)
    for i, out in enumerate(outs):
        out[...] = product[i * row_unit : (i + 1) * row_unit].astype(out.dtype)


def arrange_kernel(unit, offsets, *refs):
    blocks, (gain, out, square) = refs[:-3], refs[-3:]
    assemble(offsets, blocks, gain, out, square, unit)


def gate_up_kernel(squares, x, *refs):
    weights, (keep, send) = refs[: -2 - squares], refs[-2:]
    half = keep.shape[1]
    count = len(weights) // 2
    base = 2 * pl.program_id(0) if squares else 0
    for i in range(2):
        w = jnp.concatenate([w[0] for w in weights[i * count : (i + 1) * count]], axis=0)
        part = jnp.dot(x[...], w, preferred_element_type=F32)
        keep[base + i] = part[:half]
        send[base + i] = part[half:].astype(BF16)
    if squares:

        @pl.when(pl.program_id(0) == 0)
        def _():
            group = keep.shape[0] - 1
            keep[group] = jnp.zeros(keep.shape[1:], F32)
            send[group] = jnp.zeros(send.shape[1:], BF16)
            total = refs[-3][...]
            lane = lax.broadcasted_iota(jnp.int32, (half, LANES), 1)
            keep[group, :, :LANES] = jnp.where(lane < LANES // 2, total[:half], 0.0)
            send[group, :, :LANES] = split_square(total[half:])


def halve_kernel(squares, keep, recv, kept, send):
    half = kept.shape[1]
    body = keep.shape[0] - squares
    kept[...] = keep[:, :half, :] + recv[:, :half, :].astype(F32)
    send[:body] = (keep[:body, half:, :] + recv[:body, half:, :].astype(F32)).astype(BF16)
    if squares:
        total = keep[body, half:, :LANES] + recv[body, half:, :LANES].astype(F32)
        send[body] = jnp.zeros(send.shape[1:], BF16)
        send[body, :, :LANES] = split_square(join_square(total))


def hidden_kernel(squares, keep, recv, *refs):
    if squares:
        hidden, scale_ref = refs
        group = keep.shape[0] - 1
        total = keep[group, :, :LANES] + recv[group, :, :LANES].astype(F32)
        scale_ref[...] = lax.rsqrt(join_square(total) / D + EPSILON)
    else:
        scale_ref, hidden = refs
    scale = scale_ref[:, :1]
    width = keep.shape[2]
    for i in range(keep.shape[0] // 2):
        gate = (keep[2 * i] + recv[2 * i].astype(F32)) * scale
        up = (keep[2 * i + 1] + recv[2 * i + 1].astype(F32)) * scale
        hidden[:, i * width : (i + 1) * width] = (
            gate / (1.0 + jnp.exp(-gate)) * up
        ).astype(BF16)


def join_kernel(first, second, out):
    rows = first.shape[0]
    out[:rows] = first[...]
    out[rows:] = second[...]


def pack_kernel(*refs):
    parts, out = refs[:-1], refs[-1]
    for i, part in enumerate(parts):
        out[i] = part[...]


def output_kernel(stream, gain, *refs):
    parts, out = refs[:-1], refs[-1]
    total = stream[...].astype(F32)
    for part in parts:
        total = total + part[...].astype(F32)
    out[...] = (total * gain[...]).astype(BF16)


def down_kernel(sources, count, unit, rows, offsets, *refs):
    own, other, weights = refs[:count], refs[count : 2 * count], refs[2 * count : -rows - 1]
    outs, total = refs[-rows - 1 : -1], refs[-1]
    tile = len(weights) * weights[0].shape[1]
    for i, (which, at) in enumerate(sources):

        @pl.when(pl.program_id(0) == i)
        def _():
            hidden = jnp.concatenate(
                [own[which][:, at : at + tile], other[which][:, at : at + tile]], axis=0
            )
            w = jnp.concatenate([w[0] for w in weights], axis=0)
            part = jnp.dot(hidden, w, preferred_element_type=F32)
            total[...] = part if i == 0 else total[...] + part

    @pl.when(pl.program_id(0) == len(sources) - 1)
    def _():
        step = 0
        for out in outs:
            for first in range(0, out.shape[0], unit):
                place = pl.multiple_of(offsets[step], unit)
                out[first : first + unit, :] = total[pl.ds(place, unit), :].astype(out.dtype)
                step += 1


def head_kernel(rows, first, col_index, row_places, *refs):
    own, other = refs[:rows], refs[rows : 2 * rows]
    gains, target, *weights = refs[2 * rows : -6]
    out, lhs, square, top, total, picked = refs[-6:]
    step = pl.program_id(0)
    chips, unit, width = own[0].shape

    @pl.when(step == 0)
    def _():
        inverse = 1.0 / gains[...]
        for i in range(rows):
            place = pl.multiple_of(row_places[i], unit)
            sums = jnp.zeros((unit, 1), F32)
            for core, arrays in enumerate((own, other)):
                for j in range(chips):
                    feature = pl.multiple_of(col_index[2 * j + core] * width, LANES)
                    values = arrays[i][j]
                    lhs[pl.ds(place, unit), pl.ds(feature, width)] = values
                    plain = values.astype(F32) * inverse[2 * j + core : 2 * j + core + 1, :]
                    sums += jnp.sum(plain * plain, axis=1, keepdims=True)
            square[pl.ds(place, unit), :] = sums
        top[...] = jnp.full_like(top, MASKED)
        total[...] = jnp.zeros_like(total)
        picked[...] = jnp.zeros_like(picked)

    depth = weights[0].shape[0]
    logits = jnp.dot(lhs[:, :depth], weights[0][...], preferred_element_type=F32)
    for i in range(1, len(weights)):
        logits += jnp.dot(
            lhs[:, i * depth : (i + 1) * depth], weights[i][...], preferred_element_type=F32
        )
    logits = logits * lax.rsqrt(square[...] / D + EPSILON)
    lane = lax.broadcasted_iota(jnp.int32, logits.shape, 1)
    lane = lane + (step + first) * logits.shape[1]
    hit = jnp.where(lane == target[...], logits, 0.0)
    picked[...] += jnp.sum(hit, axis=1, keepdims=True)
    new_top = jnp.maximum(top[...], jnp.max(logits, axis=1, keepdims=True))
    total[...] = total[...] * jnp.exp(top[...] - new_top) + jnp.sum(
        jnp.exp(logits - new_top), axis=1, keepdims=True
    )
    top[...] = new_top

    @pl.when(step == pl.num_programs(0) - 1)
    def _():
        place = lax.broadcasted_iota(jnp.int32, out.shape, 1)
        out[...] = jnp.where(
            place == 0, top[...], jnp.where(place == 1, total[...], picked[...])
        )


def hold(arrays, token):
    def kernel(*refs):
        del refs

    count = len(arrays)
    results = pl.pallas_call(
        kernel,
        out_shape=[jax.ShapeDtypeStruct(array.shape, array.dtype) for array in arrays]
        + [jax.ShapeDtypeStruct((8, LANES), F32)],
        in_specs=[ANY] * (count + 1),
        out_specs=[ANY] * (count + 1),
        input_output_aliases={i: i for i in range(count)},
        compiler_params=params(16),
        cost_estimate=cost(0, 0),
        name="hold",
    )(*arrays, token[0])
    token[:] = [results[-1]]
    return results[:-1]


def per_device(
    residual,
    attn_gain,
    w_query,
    w_key,
    w_value,
    w_out,
    mlp_gain,
    w_gate,
    w_up,
    w_down,
    final_gain,
    w_head,
    seq_lengths,
    targets,
):
    row_count = lax.axis_size("row")
    col_count = lax.axis_size("col")
    chips = col_count // 2
    row_index = lax.axis_index("row")
    col_index = lax.axis_index("col")
    core = col_index % 2
    chip = col_index // 2
    row_tokens, features = residual.shape
    tokens = row_tokens * row_count
    col_tokens = tokens // col_count
    quarter = tokens // 4
    heads = w_query.shape[1] // HEAD_DIM
    kv_heads = w_key.shape[1] // HEAD_DIM
    qkv_width = w_query.shape[1] + 2 * w_key.shape[1]
    rotated = w_query.shape[1] + w_key.shape[1]
    ff_local = w_gate.shape[2]
    vocab_local = w_head.shape[1]

    row_range = jnp.arange(row_count, dtype=jnp.int32)
    col_range = jnp.arange(col_count, dtype=jnp.int32)
    row_rel = row_range ^ row_index
    col_rel = col_range ^ col_index

    token_index = jnp.arange(tokens, dtype=jnp.int32)
    segment, positions = sequence_layout(seq_lengths, token_index)
    block = min(64, tokens)
    window = min(tokens, block + LONGEST)
    first_key = jnp.maximum(0, (token_index // block + 1) * block - window)
    key_index = first_key[:, None] + jnp.arange(window, dtype=jnp.int32)[None, :]
    key_segment, _ = sequence_layout(seq_lengths, key_index.reshape(-1))
    allowed = (key_segment.reshape(tokens, window) == segment[:, None]) & (
        key_index <= token_index[:, None]
    )
    bias = jnp.where(allowed, 0.0, MASKED).astype(F32)
    own_positions = lax.dynamic_slice_in_dim(positions, col_index * col_tokens, col_tokens)
    exponent = jnp.arange(HEAD_DIM // 2, dtype=F32) * 2.0 / HEAD_DIM
    angles = own_positions[:, None] * (ROPE_BASE ** (-exponent))[None, :]
    cosine, sine = jnp.cos(angles), jnp.sin(angles)
    cosine = jnp.concatenate([cosine, cosine], axis=1)
    sine = jnp.concatenate([-sine, sine], axis=1)

    blocks = [residual] + [row_xor(residual, j) for j in range(1, row_count)]
    shape = jax.ShapeDtypeStruct

    per_row = row_tokens // col_tokens
    col_block = (row_rel[:, None] * per_row + jnp.arange(per_row, dtype=jnp.int32)).reshape(-1)
    relative = col_block ^ col_index
    offsets = ((relative & 1) * chips + (relative >> 1)) * col_tokens
    half = tokens // 2
    wide = qkv_width + LANES
    keep, send = pl.pallas_call(
        functools.partial(qkv_kernel, col_tokens, row_count),
        out_shape=[shape((half, wide), F32), shape((half, wide), BF16)],
        in_specs=[SMEM] + [VMEM] * (row_count + 4),
        out_specs=[VMEM] * 2,
        scratch_shapes=[pltpu.VMEM((tokens, features), BF16), pltpu.VMEM((tokens, LANES), F32)],
        compiler_params=params(56),
        cost_estimate=cost(
            2 * tokens * features * qkv_width, 2 * qkv_width * (features + tokens)
        ),
        name="qkv_partial",
    )(offsets, *blocks, attn_gain[None, :], w_query, w_key, w_value)
    received = col_xor(send, 1)
    parts = pl.pallas_call(
        core_add_kernel,
        out_shape=[shape((col_tokens, wide), F32 if i == 0 else BF16) for i in range(chips)],
        in_specs=[VMEM] * 2,
        out_specs=[VMEM] * chips,
        compiler_params=params(16),
        cost_estimate=cost(half * qkv_width, 6 * half * qkv_width),
        name="qkv_core_add",
    )(keep, received)
    parts = [parts[0]] + [col_xor(parts[j], 2 * j) for j in range(1, chips)]
    mine = pl.pallas_call(
        functools.partial(rope_kernel, rotated, chips),
        out_shape=shape((col_tokens, qkv_width), BF16),
        in_specs=[VMEM] * (chips + 2),
        out_specs=VMEM,
        compiler_params=params(16),
        cost_estimate=cost(8 * col_tokens * qkv_width, 2 * tokens * qkv_width),
        name="qkv_rope",
    )(*parts, cosine, sine)
    pieces = [mine] + [col_xor(mine, 2 * j) for j in range(1, chips)]
    pieces = pieces + [col_xor(piece, 1) for piece in pieces]
    piece_index = [2 * j for j in range(chips)] + [2 * j + 1 for j in range(chips)]
    places = (jnp.array(piece_index, jnp.int32) ^ col_index) * col_tokens

    projected = pl.pallas_call(
        functools.partial(attention_kernel, heads, kv_heads, col_count, block),
        out_shape=[
            shape((row_tokens, features), F32 if i == 0 else BF16) for i in range(row_count)
        ],
        in_specs=[SMEM] * 2 + [VMEM] * (col_count + 2),
        out_specs=[VMEM] * row_count,
        scratch_shapes=[
            pltpu.VMEM((tokens, qkv_width), BF16),
            pltpu.VMEM((tokens, heads * HEAD_DIM), BF16),
        ],
        compiler_params=params(32),
        cost_estimate=cost(
            2 * tokens * heads * HEAD_DIM * features * 2, 2 * heads * HEAD_DIM * features * 2
        ),
        name="attention_out",
    )(places, row_rel * row_tokens, *pieces, bias, w_out)
    projected = [projected[0]] + [row_xor(projected[j], j) for j in range(1, row_count)]
    stream = residual.astype(F32) + tree_sum([p.astype(F32) for p in projected])
    stream = lax.optimization_barrier(stream.astype(BF16))

    levels = (col_count - 1).bit_length()
    blocks = [stream] + [row_xor(stream, j) for j in range(1, row_count)]
    position = sum(((relative >> level) & 1) << (levels - 1 - level) for level in range(levels))
    half_offsets = position * col_tokens
    token = [mlp_gain]
    mlp_in, squares = call(
        functools.partial(arrange_kernel, col_tokens),
        [half_offsets, *blocks, mlp_gain[None, :]],
        [SMEM] + [VMEM] * (row_count + 1),
        token,
        out_shape=[
            shape((tokens, features), BF16),
            shape((tokens, LANES), F32),
        ],
        out_specs=[VMEM] * 2,
        compiler_params=params(16),
        cost_estimate=cost(tokens * features, 4 * tokens * features),
        name="mlp_in",
    )

    divisible = ff_local % (3 * LANES) == 0
    tile = ff_local // 3 if divisible else ff_local
    tiles = ff_local // tile
    sub = tile // 3 if tile % (3 * LANES) == 0 else tile
    subs = tile // sub
    plan = [(0, 0, 1), (0, 1, 2), (1, 0, 2), (1, 2, 1)] if divisible else [(0, 0, 1), (1, 0, 1)]
    last = levels - 1
    keeps, arrivals, hiddens = {}, {}, {}
    scale = []
    states = {}

    def gate_up(j):
        member, first, count = plan[j]
        first = first * subs
        squared = j == 0
        groups = 2 * count * subs + squared
        weights = [
            pl.BlockSpec((1, features // 2, sub), lambda i, q=q: (member, q, first + i))
            for q in range(2)
        ]
        whole = pl.BlockSpec((tokens, features), lambda i: (0, 0))
        if squared:
            out = pl.BlockSpec((groups, half, sub), lambda i: (0, 0, 0))
        else:
            out = pl.BlockSpec((2, half, sub), lambda i: (i, 0, 0))
        keep, send = call(
            functools.partial(gate_up_kernel, squared),
            [mlp_in, w_gate, w_gate, w_up, w_up] + [squares] * squared,
            [whole] + weights * 2 + [pl.BlockSpec((tokens, LANES), lambda i: (0, 0))] * squared,
            token,
            grid=(count * subs,),
            out_shape=[shape((groups, half, sub), F32), shape((groups, half, sub), BF16)],
            out_specs=[out] * 2,
            compiler_params=params(GATE_MIB),
            cost_estimate=cost(4 * tokens * features * tile * count, 4 * tile * count * features),
            name="gate_up",
        )
        keeps[j], arrivals[j] = keep, col_xor(send, 1)

    def halve(j, level):
        count = 1 if j == 0 else plan[j][2]
        keep = keeps[j]
        groups, rows, _ = keep.shape
        part = groups // count
        keeps[j], send = call(
            functools.partial(halve_kernel, j == 0),
            [keep, arrivals[j]],
            [pl.BlockSpec((part, rows, sub), lambda i: (i, 0, 0))] * 2,
            token,
            grid=(count,),
            out_shape=[
                shape((groups, rows // 2, sub), F32),
                shape((groups, rows // 2, sub), BF16),
            ],
            out_specs=[pl.BlockSpec((part, rows // 2, sub), lambda i: (i, 0, 0))] * 2,
            compiler_params=params(24),
            cost_estimate=cost(rows * sub * groups, 9 * rows * sub * groups),
            name="halve",
        )
        arrivals[j] = col_xor(send, 2 << level)

    def hidden_of(j):
        groups, rows, _ = keeps[j].shape
        squared = j == 0
        hidden_shape = shape((rows, groups // 2 * sub), BF16)
        operands = [keeps[j], arrivals[j]] + ([] if squared else scale)
        hidden, *extra = call(
            functools.partial(hidden_kernel, squared),
            operands,
            [VMEM] * len(operands),
            token,
            out_shape=[hidden_shape] + [shape((rows, LANES), F32)] * squared,
            out_specs=[VMEM] * (1 + squared),
            compiler_params=params(24),
            cost_estimate=cost(8 * rows * groups * sub, 6 * rows * groups * sub),
            name="hidden",
        )
        if squared:
            scale[:] = extra
        hiddens[j] = (hidden, col_xor(hidden, 1 << last))

    def join(j, level):
        first, second = hiddens[j]
        rows, width = first.shape
        (joined,) = call(
            join_kernel,
            [first, second],
            [VMEM] * 2,
            token,
            out_shape=[shape((2 * rows, width), BF16)],
            out_specs=[VMEM],
            compiler_params=params(16),
            cost_estimate=cost(rows * width, 8 * rows * width),
            name="join",
        )
        hiddens[j] = (joined, col_xor(joined, 1 << level))

    def down(member):
        which = [j for j in range(len(plan)) if plan[j][0] == member]
        own = [hiddens[j][0] for j in which]
        other = [hiddens[j][1] for j in which]
        sources = [(k, i * tile) for k, j in enumerate(which) for i in range(plan[j][2])]
        parts = call(
            functools.partial(down_kernel, sources, len(own), col_tokens, row_count),
            [half_offsets, *own, *other] + [w_down] * 3,
            [SMEM]
            + [pl.BlockSpec(array.shape, lambda i: (0, 0)) for array in own + other]
            + [
                pl.BlockSpec((1, tile // 3, features), lambda i, q=q: (member, 3 * i + q, 0))
                for q in range(3)
            ],
            token,
            grid=(tiles,),
            out_shape=[
                shape((row_tokens, features), F32 if i == 0 else BF16)
                for i in range(row_count)
            ],
            out_specs=[pl.BlockSpec((row_tokens, features), lambda i: (0, 0))] * row_count,
            scratch_shapes=[pltpu.VMEM((tokens, features), F32)],
            compiler_params=params(56),
            cost_estimate=cost(
                2 * tokens * features * ff_local, 2 * ff_local * (features + tokens)
            ),
            name="down",
        )
        states[member] = [parts[0]] + [row_xor(parts[j], j) for j in range(1, row_count)]

    def output(member):
        parts = states[member]
        (scaled,) = call(
            output_kernel,
            [stream, final_gain[None, :], *parts],
            [VMEM] * (2 + row_count),
            token,
            out_shape=[shape((row_tokens, features), BF16)],
            out_specs=[VMEM],
            compiler_params=params(16),
            cost_estimate=cost(8 * row_tokens * features, 16 * row_tokens * features),
            name="output",
        )
        states[member] = [scaled] + [col_xor(scaled, 2 * j) for j in range(1, chips)]

    def pack(member):
        (by_chip,) = call(
            pack_kernel,
            states[member],
            [VMEM] * chips,
            token,
            out_shape=[shape((chips, row_tokens, features), BF16)],
            out_specs=[VMEM],
            compiler_params=params(16),
            cost_estimate=cost(chips * row_tokens * features, 4 * chips * row_tokens * features),
            name="pack",
        )
        other = col_xor(by_chip, 1)
        states[member] = [by_chip, other] + [row_xor(by_chip, j) for j in range(1, row_count)]

    def forward(member):
        by_chip, other, *rows = states[member]
        rows = hold(rows, token)
        states[member] = [by_chip, *rows, other] + [col_xor(array, 1) for array in rows]

    vocab_start = (row_index * col_count + col_index) * vocab_local
    local_targets = (targets - vocab_start)[:, None]
    vocab_tile = 512 if vocab_local % 512 == 0 else vocab_local
    vocab_tiles = vocab_local // vocab_tile
    stats = {0: [], 1: []}

    gain_parts = [final_gain[None, :]]
    small = []

    def gather_gain(level):
        (part,) = hold(gain_parts[-1:], token)
        gain_parts.append(jnp.concatenate([part, col_xor(part, 1 << level)], axis=0))

    def ready():
        small[:] = hold([gain_parts[-1], local_targets, col_rel, row_rel * row_tokens], token)

    def head(member, first, count):
        gains, target, features_at, rows_at = small
        state = states[member]
        (result,) = call(
            functools.partial(head_kernel, row_count, first),
            [features_at, rows_at, *state, gains, target] + [w_head] * HEAD_BLOCKS,
            [SMEM] * 2
            + [pl.BlockSpec(state[0].shape, lambda i: (0, 0, 0))] * (2 * row_count)
            + [pl.BlockSpec(gains.shape, lambda i: (0, 0))]
            + [pl.BlockSpec((tokens, 1), lambda i: (0, 0))]
            + [
                pl.BlockSpec((D // HEAD_BLOCKS, vocab_tile), lambda i, q=q: (q, first + i))
                for q in range(HEAD_BLOCKS)
            ],
            token,
            grid=(count,),
            out_shape=[shape((tokens, LANES), F32)],
            out_specs=[pl.BlockSpec((tokens, LANES), lambda i: (0, 0))],
            scratch_shapes=[pltpu.VMEM((tokens, D), BF16)] + [pltpu.VMEM((tokens, 1), F32)] * 4,
            compiler_params=params(56),
            cost_estimate=cost(
                2 * tokens * D * vocab_tile * count, 2 * D * vocab_tile * count
            ),
            name="head",
        )
        stats[member].append(result[:, :3].T)

    if len(plan) == 4 and levels == 3:
        schedule = [
            (gate_up, 0), (gate_up, 1), (halve, 0, 0), (gate_up, 2), (halve, 1, 0),
            (halve, 0, 1), (gate_up, 3), (halve, 2, 0), (hidden_of, 0), (halve, 1, 1),
            (halve, 3, 0), (join, 0, 1), (gather_gain, 0), (hidden_of, 1), (halve, 2, 1),
            (join, 0, 0), (join, 1, 1), (gather_gain, 1), (halve, 3, 1), (hidden_of, 2),
            (join, 1, 0), (join, 2, 1), (gather_gain, 2), (ready,), (down, 0), (hidden_of, 3),
            (join, 3, 1), (output, 0), (join, 2, 0), (join, 3, 0), (down, 1),
        ]
    else:
        schedule = []
        for j in range(len(plan)):
            schedule += [(gate_up, j)] + [(halve, j, level) for level in range(last)]
            schedule += [(hidden_of, j)] + [(join, j, level) for level in range(last - 1, -1, -1)]
        schedule += [(gather_gain, level) for level in range(levels)] + [(ready,)]
        schedule += [(down, 0), (output, 0), (down, 1)]
    early = (3 * vocab_tiles + 4) // 5
    schedule += [(output, 1), (pack, 0), (pack, 1), (forward, 0), (head, 0, 0, early)]
    schedule += [(forward, 1)]
    if early < vocab_tiles:
        schedule += [(head, 0, early, vocab_tiles - early)]
    schedule += [(head, 1, 0, vocab_tiles)]
    for step, *arguments in schedule:
        step(*arguments)

    def combine(parts):
        top = functools.reduce(jnp.maximum, [p[0] for p in parts])
        total = tree_sum([p[1] * jnp.exp(p[0] - top) for p in parts])
        picked = tree_sum([p[2] for p in parts])
        return jnp.stack([top, total, picked])

    merged = combine(stats[0]) if len(stats[0]) > 1 else stats[0][0]
    merged = jnp.stack([merged, stats[1][0]], axis=1)
    for level in range(levels):
        merged = combine([merged, col_xor(merged, 1 << level)])
    for level in range((row_count - 1).bit_length()):
        merged = combine([merged, row_xor(merged, 1 << level)])
    logprob = merged[2] - (merged[0] + jnp.log(merged[1]))
    difference = logprob[0] - logprob[1]
    one_hot = (segment[:, None] == jnp.arange(SEQS, dtype=jnp.int32)[None, :]).astype(F32)
    seq_sums = jnp.dot(difference, one_hot, precision=lax.Precision.HIGHEST)
    return seq_sums / seq_lengths.astype(F32)


def solution(mesh):
    placed = (
        P("row", "col"),
        P("col"),
        P("col", "row"),
        P("col", "row"),
        P("col", "row"),
        P("row", "col"),
        P("col"),
        P(None, "col", "row"),
        P(None, "col", "row"),
        P(None, "row", "col"),
        P("col"),
        P(None, ("row", "col")),
        P(),
        P(),
    )
    return jax.shard_map(per_device, mesh=mesh, in_specs=placed, out_specs=P(), check_vma=False)
```

```python
import functools

import jax
import jax.numpy as jnp
from jax import lax
from jax.experimental import pallas as pl
from jax.experimental.pallas import tpu as pltpu
from jax.sharding import PartitionSpec as P

D = 5120
HEAD_DIM = 128
SEQS = 8
LONGEST = 64

EPSILON = 1e-06
ROPE_BASE = 1000000.0
MASKED = -1e30
LANES = 128
HEAD_BLOCKS = 4
GATE_MIB = 46
DOWN_MIB = 46
BF16 = jnp.bfloat16
F32 = jnp.float32
MIB = 1 << 20

VMEM = pl.BlockSpec(memory_space=pltpu.VMEM)
ANY = pl.BlockSpec(memory_space=pl.ANY)
SMEM = pl.BlockSpec(memory_space=pltpu.SMEM)


def params(mib):
    return pltpu.CompilerParams(vmem_limit_bytes=mib * MIB)


def cost(flops, byte_count):
    del flops, byte_count
    return pl.CostEstimate(flops=1, bytes_accessed=1, transcendentals=0)


def call(kernel, operands, in_specs, token, out_shape, out_specs, **options):
    count, outs = len(operands), len(out_shape)

    def body(*refs):
        inputs, results, scratch = refs[:count], refs[count + 1 :], refs[count + outs + 2 :]
        kernel(*inputs, *results[:outs], *scratch)

    results = pl.pallas_call(
        body,
        in_specs=in_specs + [ANY],
        out_shape=out_shape + [jax.ShapeDtypeStruct((8, LANES), F32)],
        out_specs=out_specs + [ANY],
        **options,
    )(*operands, token[0])
    token[:] = [results[-1]]
    return results[:-1]


def row_xor(x, mask):
    count = lax.axis_size("row")
    return lax.ppermute(x, "row", [(i, i ^ mask) for i in range(count)])


def col_xor(x, mask):
    count = lax.axis_size("col")
    return lax.ppermute(x, "col", [(i, i ^ mask) for i in range(count)])


def tree_sum(values):
    values = list(values)
    while len(values) > 1:
        values = [values[i] + values[i + 1] for i in range(0, len(values), 2)]
    return values[0]


def sequence_layout(seq_lengths, token_index):
    ends_at = jnp.cumsum(seq_lengths)
    before = ends_at[None, :] <= token_index[:, None]
    segment = jnp.sum(before.astype(jnp.int32), axis=1)
    starts_at = jnp.sum(jnp.where(before, seq_lengths[None, :], 0), axis=1)
    return (segment, (token_index - starts_at).astype(F32))


def split_square(total):
    high = total.astype(BF16)
    low = (total - high.astype(F32)).astype(BF16)
    lane = lax.broadcasted_iota(jnp.int32, total.shape, 1)
    return jnp.where(lane < LANES // 2, high.astype(F32), low.astype(F32)).astype(BF16)


def join_square(tile):
    return tile + pltpu.roll(tile, LANES // 2, 1)


def assemble(offsets, blocks, gain, x_ref, square_ref, unit):
    step = 0
    for block in blocks:
        for first in range(0, block.shape[0], unit):
            rows = block[first : first + unit, :].astype(F32)
            place = pl.multiple_of(offsets[step], unit)
            x_ref[pl.ds(place, unit), :] = (rows * gain[...]).astype(BF16)
            square = jnp.sum(rows * rows, axis=1, keepdims=True)
            square_ref[pl.ds(place, unit), :] = jnp.broadcast_to(square, (unit, LANES))
            step += 1


def put_squares(square_ref, keep, send, at):
    half = keep.shape[0]
    total = square_ref[...]
    lane = lax.broadcasted_iota(jnp.int32, (half, LANES), 1)
    keep[:, at : at + LANES] = jnp.where(lane < LANES // 2, total[:half], 0.0)
    send[:, at : at + LANES] = jnp.where(lane < LANES // 2, total[half:], 0.0)


def qkv_kernel(unit, count, offsets, *refs):
    blocks, (gain, wq, wk, wv, keep, send, x_ref, square_ref) = refs[:count], refs[count:]
    assemble(offsets, blocks, gain, x_ref, square_ref, unit)
    half = keep.shape[0]
    x = x_ref[...]
    at = 0
    for w in (wq, wk, wv):
        width = w.shape[1]
        part = jnp.dot(x, w[...], preferred_element_type=F32)
        keep[:, at : at + width] = part[:half]
        send[:, at : at + width] = part[half:]
        at += width
    put_squares(square_ref, keep, send, at)


def core_add_kernel(keep, recv, *outs):
    rows, width = outs[0].shape
    for i, out in enumerate(outs):
        total = keep[i * rows : (i + 1) * rows, :] + recv[
            i * rows : (i + 1) * rows, :
        ].astype(F32)
        if i == 0:
            out[...] = total
        else:
            out[:, : width - LANES] = total[:, : width - LANES].astype(BF16)
            out[:, width - LANES :] = split_square(join_square(total[:, width - LANES :]))


def rope_kernel(rotated, count, *refs):
    parts, (cosine, sine, out) = refs[:count], refs[count:]
    width = out.shape[1]

    def summed(at):
        total = parts[0][:, at : at + LANES].astype(F32)
        for part in parts[1:]:
            total = total + part[:, at : at + LANES].astype(F32)
        return total

    scale = lax.rsqrt(join_square(summed(width)) / D + EPSILON)
    for at in range(0, width, HEAD_DIM):
        total = summed(at) * scale
        if at < rotated:
            total = total * cosine[...] + pltpu.roll(total, HEAD_DIM // 2, 1) * sine[...]
        out[:, at : at + HEAD_DIM] = total.astype(BF16)


def attention_kernel(heads, kv_heads, count, block, places, row_places, *refs):
    pieces, (bias, w_out), outs, (qkv, attended) = (
        refs[:count],
        refs[count : count + 2],
        refs[count + 2 : -2],
        refs[-2:],
    )
    row_unit = outs[0].shape[0]
    unit = pieces[0].shape[0]
    for i, piece in enumerate(pieces):
        qkv[pl.ds(pl.multiple_of(places[i], unit), unit), :] = piece[...]
    tokens = qkv.shape[0]
    group = heads // kv_heads
    window = min(tokens, block + LONGEST)
    for start in range(0, tokens, block):
        first = max(0, start + block - window)
        mask = bias[start : start + block, :]
        mask = jnp.concatenate([mask] * group, axis=0)
        for g in range(kv_heads):
            q = jnp.concatenate(
                [
                    qkv[start : start + block, h * HEAD_DIM : (h + 1) * HEAD_DIM]
                    for h in range(g * group, (g + 1) * group)
                ],
                axis=0,
            )
            k_at = (heads + g) * HEAD_DIM
            v_at = (heads + kv_heads + g) * HEAD_DIM
            k = qkv[first : first + window, k_at : k_at + HEAD_DIM]
            v = qkv[first : first + window, v_at : v_at + HEAD_DIM]
            scores = lax.dot_general(
                q, k, (((1,), (1,)), ((), ())), preferred_element_type=F32
            ) * HEAD_DIM ** (-0.5)
            scores = scores + mask
            weights = jnp.exp(scores - jnp.max(scores, axis=1, keepdims=True))
            total = jnp.sum(weights, axis=1, keepdims=True)
            weights = weights / total
            high = weights.astype(BF16)
            low = (weights - high.astype(F32)).astype(BF16)
            result = jnp.dot(high, v, preferred_element_type=F32)
            result = (result + jnp.dot(low, v, preferred_element_type=F32)).astype(BF16)
            for h in range(group):
                at = (g * group + h) * HEAD_DIM
                for sub in range(0, block, row_unit):
                    place = pl.multiple_of(row_places[(start + sub) // row_unit], row_unit)
                    attended[pl.ds(place, row_unit), at : at + HEAD_DIM] = result[
                        h * block + sub : h * block + sub + row_unit
                    ]
    product = jnp.dot(attended[...], w_out[...], preferred_element_type=F32)
    for i, out in enumerate(outs):
        out[...] = product[i * row_unit : (i + 1) * row_unit].astype(out.dtype)


def arrange_kernel(unit, offsets, *refs):
    blocks, (gain, out, square_ref) = refs[:-3], refs[-3:]
    inverse = 1.0 / gain[...]
    step = 0
    for block in blocks:
        for first in range(0, block.shape[0], unit):
            rows = block[first : first + unit, :]
            place = pl.multiple_of(offsets[step], unit)
            out[pl.ds(place, unit), :] = rows
            plain = rows.astype(F32) * inverse
            square = jnp.sum(plain * plain, axis=1, keepdims=True)
            square_ref[pl.ds(place, unit), :] = jnp.broadcast_to(square, (unit, LANES))
            step += 1


def gate_up_kernel(squares, x, *refs):
    weights, (keep, send) = refs[: -2 - squares], refs[-2:]
    half = keep.shape[1]
    count = len(weights) // 2
    base = 2 * pl.program_id(0) if squares else 0
    for i in range(2):
        w = jnp.concatenate([w[0] for w in weights[i * count : (i + 1) * count]], axis=0)
        part = jnp.dot(x[...], w, preferred_element_type=F32)
        keep[base + i] = part[:half]
        send[base + i] = part[half:]
    if squares:

        @pl.when(pl.program_id(0) == 0)
        def _():
            group = keep.shape[0] - 1
            keep[group] = jnp.zeros(keep.shape[1:], F32)
            send[group] = jnp.zeros(send.shape[1:], F32)
            total = refs[-3][...]
            lane = lax.broadcasted_iota(jnp.int32, (half, LANES), 1)
            keep[group, :, :LANES] = jnp.where(lane < LANES // 2, total[:half], 0.0)
            send[group, :, :LANES] = jnp.where(lane < LANES // 2, total[half:], 0.0)


def halve_kernel(squares, keep, recv, kept, send):
    half = kept.shape[1]
    body = keep.shape[0] - squares
    kept[...] = keep[:, :half, :] + recv[:, :half, :].astype(F32)
    send[:body] = (keep[:body, half:, :] + recv[:body, half:, :].astype(F32)).astype(BF16)
    if squares:
        total = keep[body, half:, :LANES] + recv[body, half:, :LANES].astype(F32)
        send[body] = jnp.zeros(send.shape[1:], BF16)
        send[body, :, :LANES] = split_square(join_square(total))


def hidden_kernel(squares, keep, recv, *refs):
    if squares:
        hidden, scale_ref = refs
        group = keep.shape[0] - 1
        total = keep[group, :, :LANES] + recv[group, :, :LANES].astype(F32)
        scale_ref[...] = lax.rsqrt(join_square(total) / D + EPSILON)
    else:
        scale_ref, hidden = refs
    scale = scale_ref[:, :1]
    width = keep.shape[2]
    for i in range(keep.shape[0] // 2):
        gate = (keep[2 * i] + recv[2 * i].astype(F32)) * scale
        up = (keep[2 * i + 1] + recv[2 * i + 1].astype(F32)) * scale
        hidden[:, i * width : (i + 1) * width] = (
            gate / (1.0 + jnp.exp(-gate)) * up
        ).astype(BF16)


def join_kernel(first, second, out):
    rows = first.shape[0]
    out[:rows] = first[...]
    out[rows:] = second[...]


def pack_kernel(*refs):
    parts, out = refs[:-1], refs[-1]
    for i, part in enumerate(parts):
        out[i] = part[...]


def output_kernel(stream, gain, *refs):
    parts, out = refs[:-1], refs[-1]
    total = stream[...].astype(F32)
    for part in parts:
        total = total + part[...].astype(F32)
    out[...] = (total * gain[...]).astype(BF16)


def down_kernel(sources, count, added, unit, rows, offsets, *refs):
    own, other, before = refs[:count], refs[count : 2 * count], refs[2 * count : 2 * count + added]
    outs, total = refs[-rows - 1 : -1], refs[-1]
    weights = refs[2 * count + added : -rows - 1]
    tile = len(weights) * weights[0].shape[1]
    for i, (which, at) in enumerate(sources):

        @pl.when(pl.program_id(0) == i)
        def _():
            hidden = jnp.concatenate(
                [own[which][:, at : at + tile], other[which][:, at : at + tile]], axis=0
            )
            w = jnp.concatenate([w[0] for w in weights], axis=0)
            part = jnp.dot(hidden, w, preferred_element_type=F32)
            if i > 0:
                part = part + total[...]
            elif added:
                part = part + before[0][...]
            total[...] = part

    @pl.when(pl.program_id(0) == len(sources) - 1)
    def _():
        step = 0
        for out in outs:
            for first in range(0, out.shape[0], unit):
                place = pl.multiple_of(offsets[step], unit)
                out[first : first + unit, :] = total[pl.ds(place, unit), :].astype(out.dtype)
                step += 1


def head_kernel(rows, first, col_index, row_places, *refs):
    own, other = refs[:rows], refs[rows : 2 * rows]
    gains, target, *weights = refs[2 * rows : -6]
    out, lhs, square, top, total, picked = refs[-6:]
    step = pl.program_id(0)
    chips, unit, width = own[0].shape

    @pl.when(step == 0)
    def _():
        inverse = 1.0 / gains[...]
        for i in range(rows):
            place = pl.multiple_of(row_places[i], unit)
            sums = jnp.zeros((unit, 1), F32)
            for core, arrays in enumerate((own, other)):
                for j in range(chips):
                    feature = pl.multiple_of(col_index[2 * j + core] * width, LANES)
                    values = arrays[i][j]
                    lhs[pl.ds(place, unit), pl.ds(feature, width)] = values
                    plain = values.astype(F32) * inverse[2 * j + core : 2 * j + core + 1, :]
                    sums += jnp.sum(plain * plain, axis=1, keepdims=True)
            square[pl.ds(place, unit), :] = sums
        top[...] = jnp.full_like(top, MASKED)
        total[...] = jnp.zeros_like(total)
        picked[...] = jnp.zeros_like(picked)

    depth = weights[0].shape[0]
    logits = jnp.dot(lhs[:, :depth], weights[0][...], preferred_element_type=F32)
    for i in range(1, len(weights)):
        logits += jnp.dot(
            lhs[:, i * depth : (i + 1) * depth], weights[i][...], preferred_element_type=F32
        )
    logits = logits * lax.rsqrt(square[...] / D + EPSILON)
    lane = lax.broadcasted_iota(jnp.int32, logits.shape, 1)
    lane = lane + (step + first) * logits.shape[1]
    hit = jnp.where(lane == target[...], logits, 0.0)
    picked[...] += jnp.sum(hit, axis=1, keepdims=True)
    new_top = jnp.maximum(top[...], jnp.max(logits, axis=1, keepdims=True))
    total[...] = total[...] * jnp.exp(top[...] - new_top) + jnp.sum(
        jnp.exp(logits - new_top), axis=1, keepdims=True
    )
    top[...] = new_top

    @pl.when(step == pl.num_programs(0) - 1)
    def _():
        place = lax.broadcasted_iota(jnp.int32, out.shape, 1)
        out[...] = jnp.where(
            place == 0, top[...], jnp.where(place == 1, total[...], picked[...])
        )


def hold(arrays, token):
    def kernel(*refs):
        del refs

    count = len(arrays)
    results = pl.pallas_call(
        kernel,
        out_shape=[jax.ShapeDtypeStruct(array.shape, array.dtype) for array in arrays]
        + [jax.ShapeDtypeStruct((8, LANES), F32)],
        in_specs=[ANY] * (count + 1),
        out_specs=[ANY] * (count + 1),
        input_output_aliases={i: i for i in range(count)},
        compiler_params=params(16),
        cost_estimate=cost(0, 0),
        name="hold",
    )(*arrays, token[0])
    token[:] = [results[-1]]
    return results[:-1]


def per_device(
    residual,
    attn_gain,
    w_query,
    w_key,
    w_value,
    w_out,
    mlp_gain,
    w_gate,
    w_up,
    w_down,
    final_gain,
    w_head,
    seq_lengths,
    targets,
):
    row_count = lax.axis_size("row")
    col_count = lax.axis_size("col")
    chips = col_count // 2
    row_index = lax.axis_index("row")
    col_index = lax.axis_index("col")
    core = col_index % 2
    chip = col_index // 2
    row_tokens, features = residual.shape
    tokens = row_tokens * row_count
    col_tokens = tokens // col_count
    quarter = tokens // 4
    heads = w_query.shape[1] // HEAD_DIM
    kv_heads = w_key.shape[1] // HEAD_DIM
    qkv_width = w_query.shape[1] + 2 * w_key.shape[1]
    rotated = w_query.shape[1] + w_key.shape[1]
    ff_local = w_gate.shape[2]
    vocab_local = w_head.shape[1]

    row_range = jnp.arange(row_count, dtype=jnp.int32)
    col_range = jnp.arange(col_count, dtype=jnp.int32)
    row_rel = row_range ^ row_index
    col_rel = col_range ^ col_index

    token_index = jnp.arange(tokens, dtype=jnp.int32)
    segment, positions = sequence_layout(seq_lengths, token_index)
    block = min(64, tokens)
    window = min(tokens, block + LONGEST)
    first_key = jnp.maximum(0, (token_index // block + 1) * block - window)
    key_index = first_key[:, None] + jnp.arange(window, dtype=jnp.int32)[None, :]
    key_segment, _ = sequence_layout(seq_lengths, key_index.reshape(-1))
    allowed = (key_segment.reshape(tokens, window) == segment[:, None]) & (
        key_index <= token_index[:, None]
    )
    bias = jnp.where(allowed, 0.0, MASKED).astype(F32)
    own_positions = lax.dynamic_slice_in_dim(positions, col_index * col_tokens, col_tokens)
    exponent = jnp.arange(HEAD_DIM // 2, dtype=F32) * 2.0 / HEAD_DIM
    angles = own_positions[:, None] * (ROPE_BASE ** (-exponent))[None, :]
    cosine, sine = jnp.cos(angles), jnp.sin(angles)
    cosine = jnp.concatenate([cosine, cosine], axis=1)
    sine = jnp.concatenate([-sine, sine], axis=1)

    blocks = [residual] + [row_xor(residual, j) for j in range(1, row_count)]
    shape = jax.ShapeDtypeStruct

    per_row = row_tokens // col_tokens
    col_block = (row_rel[:, None] * per_row + jnp.arange(per_row, dtype=jnp.int32)).reshape(-1)
    relative = col_block ^ col_index
    offsets = ((relative & 1) * chips + (relative >> 1)) * col_tokens
    half = tokens // 2
    wide = qkv_width + LANES
    keep, send = pl.pallas_call(
        functools.partial(qkv_kernel, col_tokens, row_count),
        out_shape=[shape((half, wide), F32)] * 2,
        in_specs=[SMEM] + [VMEM] * (row_count + 4),
        out_specs=[VMEM] * 2,
        scratch_shapes=[pltpu.VMEM((tokens, features), BF16), pltpu.VMEM((tokens, LANES), F32)],
        compiler_params=params(56),
        cost_estimate=cost(
            2 * tokens * features * qkv_width, 2 * qkv_width * (features + tokens)
        ),
        name="qkv_partial",
    )(offsets, *blocks, attn_gain[None, :], w_query, w_key, w_value)
    received = col_xor(send, 1)
    parts = pl.pallas_call(
        core_add_kernel,
        out_shape=[shape((col_tokens, wide), F32 if i == 0 else BF16) for i in range(chips)],
        in_specs=[VMEM] * 2,
        out_specs=[VMEM] * chips,
        compiler_params=params(16),
        cost_estimate=cost(half * qkv_width, 6 * half * qkv_width),
        name="qkv_core_add",
    )(keep, received)
    parts = [parts[0]] + [col_xor(parts[j], 2 * j) for j in range(1, chips)]
    mine = pl.pallas_call(
        functools.partial(rope_kernel, rotated, chips),
        out_shape=shape((col_tokens, qkv_width), BF16),
        in_specs=[VMEM] * (chips + 2),
        out_specs=VMEM,
        compiler_params=params(16),
        cost_estimate=cost(8 * col_tokens * qkv_width, 2 * tokens * qkv_width),
        name="qkv_rope",
    )(*parts, cosine, sine)
    pieces = [mine] + [col_xor(mine, 2 * j) for j in range(1, chips)]
    pieces = pieces + [col_xor(piece, 1) for piece in pieces]
    piece_index = [2 * j for j in range(chips)] + [2 * j + 1 for j in range(chips)]
    places = (jnp.array(piece_index, jnp.int32) ^ col_index) * col_tokens

    projected = pl.pallas_call(
        functools.partial(attention_kernel, heads, kv_heads, col_count, block),
        out_shape=[
            shape((row_tokens, features), F32 if i == 0 else BF16) for i in range(row_count)
        ],
        in_specs=[SMEM] * 2 + [VMEM] * (col_count + 2),
        out_specs=[VMEM] * row_count,
        scratch_shapes=[
            pltpu.VMEM((tokens, qkv_width), BF16),
            pltpu.VMEM((tokens, heads * HEAD_DIM), BF16),
        ],
        compiler_params=params(32),
        cost_estimate=cost(
            2 * tokens * heads * HEAD_DIM * features * 2, 2 * heads * HEAD_DIM * features * 2
        ),
        name="attention_out",
    )(places, row_rel * row_tokens, *pieces, bias, w_out)
    projected = [projected[0]] + [row_xor(projected[j], j) for j in range(1, row_count)]
    stream = residual.astype(F32) + tree_sum([p.astype(F32) for p in projected])
    scaled_stream = (stream * mlp_gain[None, :]).astype(BF16)

    levels = (col_count - 1).bit_length()
    blocks = [scaled_stream] + [row_xor(scaled_stream, j) for j in range(1, row_count)]
    position = sum(((relative >> level) & 1) << (levels - 1 - level) for level in range(levels))
    half_offsets = position * col_tokens
    token = [mlp_gain]
    mlp_in, squares = call(
        functools.partial(arrange_kernel, col_tokens),
        [half_offsets, *blocks, mlp_gain[None, :]],
        [SMEM] + [VMEM] * (row_count + 1),
        token,
        out_shape=[
            shape((tokens, features), BF16),
            shape((tokens, LANES), F32),
        ],
        out_specs=[VMEM] * 2,
        compiler_params=params(16),
        cost_estimate=cost(tokens * features, 4 * tokens * features),
        name="mlp_in",
    )

    divisible = ff_local % (3 * LANES) == 0
    tile = ff_local // 3 if divisible else ff_local
    tiles = ff_local // tile
    sub = tile // 3 if tile % (3 * LANES) == 0 else tile
    subs = tile // sub
    plan = [(0, 0, 1), (1, 0, 1)]
    if divisible:
        plan = [(0, 0, 1), (0, 1, 2), (1, 0, 2), (1, 2, 1)]
    last = levels - 1
    keeps, arrivals, hiddens = {}, {}, {}
    scale = []
    states = {}

    def gate_up(j):
        member, first, count = plan[j]
        first = first * subs
        squared = j == 0
        groups = 2 * count * subs + squared
        weights = [
            pl.BlockSpec((1, features // 2, sub), lambda i, q=q: (member, q, first + i))
            for q in range(2)
        ]
        whole = pl.BlockSpec((tokens, features), lambda i: (0, 0))
        if squared:
            out = pl.BlockSpec((groups, half, sub), lambda i: (0, 0, 0))
        else:
            out = pl.BlockSpec((2, half, sub), lambda i: (i, 0, 0))
        keep, send = call(
            functools.partial(gate_up_kernel, squared),
            [mlp_in, w_gate, w_gate, w_up, w_up] + [squares] * squared,
            [whole] + weights * 2 + [pl.BlockSpec((tokens, LANES), lambda i: (0, 0))] * squared,
            token,
            grid=(count * subs,),
            out_shape=[shape((groups, half, sub), F32)] * 2,
            out_specs=[out] * 2,
            compiler_params=params(GATE_MIB),
            cost_estimate=cost(4 * tokens * features * tile * count, 4 * tile * count * features),
            name="gate_up",
        )
        keeps[j], arrivals[j] = keep, col_xor(send, 1)

    def halve(j, level):
        count = 1 if j == 0 else plan[j][2]
        keep = keeps[j]
        groups, rows, _ = keep.shape
        part = groups // count
        keeps[j], send = call(
            functools.partial(halve_kernel, j == 0),
            [keep, arrivals[j]],
            [pl.BlockSpec((part, rows, sub), lambda i: (i, 0, 0))] * 2,
            token,
            grid=(count,),
            out_shape=[
                shape((groups, rows // 2, sub), F32),
                shape((groups, rows // 2, sub), BF16),
            ],
            out_specs=[pl.BlockSpec((part, rows // 2, sub), lambda i: (i, 0, 0))] * 2,
            compiler_params=params(24),
            cost_estimate=cost(rows * sub * groups, 9 * rows * sub * groups),
            name="halve",
        )
        arrivals[j] = col_xor(send, 2 << level)

    def hidden_of(j):
        groups, rows, _ = keeps[j].shape
        squared = j == 0
        hidden_shape = shape((rows, groups // 2 * sub), BF16)
        operands = [keeps[j], arrivals[j]] + ([] if squared else scale)
        hidden, *extra = call(
            functools.partial(hidden_kernel, squared),
            operands,
            [VMEM] * len(operands),
            token,
            out_shape=[hidden_shape] + [shape((rows, LANES), F32)] * squared,
            out_specs=[VMEM] * (1 + squared),
            compiler_params=params(24),
            cost_estimate=cost(8 * rows * groups * sub, 6 * rows * groups * sub),
            name="hidden",
        )
        if squared:
            scale[:] = extra
        hiddens[j] = (hidden, col_xor(hidden, 1 << last))

    def join(j, level):
        first, second = hiddens[j]
        rows, width = first.shape
        (joined,) = call(
            join_kernel,
            [first, second],
            [VMEM] * 2,
            token,
            out_shape=[shape((2 * rows, width), BF16)],
            out_specs=[VMEM],
            compiler_params=params(16),
            cost_estimate=cost(rows * width, 8 * rows * width),
            name="join",
        )
        hiddens[j] = (joined, col_xor(joined, 1 << level))

    partial = {0: [], 1: []}
    summed = {0: [], 1: []}

    def down(member, early=False):
        which = [j for j in range(len(plan)) if plan[j][0] == member and j not in summed[member]]
        if early:
            which = which[:1]
            summed[member] = which
        own = [hiddens[j][0] for j in which]
        other = [hiddens[j][1] for j in which]
        sources = [(k, i * tile) for k, j in enumerate(which) for i in range(plan[j][2])]
        first = plan[which[0]][1]
        before = partial[member]
        count = len(which)
        rows = 0 if early else row_count
        sum_spec = pl.BlockSpec((tokens, features), lambda i: (0, 0))
        sum_shape = shape((tokens, features), F32)
        row_shapes = [
            shape((row_tokens, features), F32 if i == 0 else BF16) for i in range(row_count)
        ]
        parts = call(
            functools.partial(down_kernel, sources, count, len(before), col_tokens, rows),
            [half_offsets, *own, *other, *before] + [w_down] * 3,
            [SMEM]
            + [pl.BlockSpec(array.shape, lambda i: (0, 0)) for array in own + other]
            + [sum_spec] * len(before)
            + [
                pl.BlockSpec((1, tile // 3, features), lambda i, q=q: (member, 3 * (first + i) + q, 0))
                for q in range(3)
            ],
            token,
            grid=(len(sources),),
            out_shape=[sum_shape] if early else row_shapes,
            out_specs=[sum_spec]
            if early
            else [pl.BlockSpec((row_tokens, features), lambda i: (0, 0))] * row_count,
            scratch_shapes=[] if early else [pltpu.VMEM((tokens, features), F32)],
            compiler_params=params(DOWN_MIB),
            cost_estimate=cost(
                2 * tokens * features * ff_local, 2 * ff_local * (features + tokens)
            ),
            name="down",
        )
        if early:
            partial[member] = [parts[0]]
        else:
            states[member] = [parts[0]] + [row_xor(parts[j], j) for j in range(1, row_count)]

    def output(member):
        parts = states[member]
        (scaled,) = call(
            output_kernel,
            [stream, final_gain[None, :], *parts],
            [VMEM] * (2 + row_count),
            token,
            out_shape=[shape((row_tokens, features), BF16)],
            out_specs=[VMEM],
            compiler_params=params(16),
            cost_estimate=cost(8 * row_tokens * features, 16 * row_tokens * features),
            name="output",
        )
        states[member] = [scaled] + [col_xor(scaled, 2 * j) for j in range(1, chips)]

    def pack(member):
        (by_chip,) = call(
            pack_kernel,
            states[member],
            [VMEM] * chips,
            token,
            out_shape=[shape((chips, row_tokens, features), BF16)],
            out_specs=[VMEM],
            compiler_params=params(16),
            cost_estimate=cost(chips * row_tokens * features, 4 * chips * row_tokens * features),
            name="pack",
        )
        other = col_xor(by_chip, 1)
        states[member] = [by_chip, other] + [row_xor(by_chip, j) for j in range(1, row_count)]

    def forward(member):
        by_chip, other, *rows = states[member]
        rows = hold(rows, token)
        states[member] = [by_chip, *rows, other] + [col_xor(array, 1) for array in rows]

    vocab_start = (row_index * col_count + col_index) * vocab_local
    local_targets = (targets - vocab_start)[:, None]
    vocab_tile = 512 if vocab_local % 512 == 0 else vocab_local
    vocab_tiles = vocab_local // vocab_tile
    stats = {0: [], 1: []}

    gain_parts = [final_gain[None, :]]
    small = []

    def gather_gain(level):
        (part,) = hold(gain_parts[-1:], token)
        gain_parts.append(jnp.concatenate([part, col_xor(part, 1 << level)], axis=0))

    def ready():
        small[:] = hold([gain_parts[-1], local_targets, col_rel, row_rel * row_tokens], token)

    def head(member, first, count):
        gains, target, features_at, rows_at = small
        state = states[member]
        (result,) = call(
            functools.partial(head_kernel, row_count, first),
            [features_at, rows_at, *state, gains, target] + [w_head] * HEAD_BLOCKS,
            [SMEM] * 2
            + [pl.BlockSpec(state[0].shape, lambda i: (0, 0, 0))] * (2 * row_count)
            + [pl.BlockSpec(gains.shape, lambda i: (0, 0))]
            + [pl.BlockSpec((tokens, 1), lambda i: (0, 0))]
            + [
                pl.BlockSpec((D // HEAD_BLOCKS, vocab_tile), lambda i, q=q: (q, first + i))
                for q in range(HEAD_BLOCKS)
            ],
            token,
            grid=(count,),
            out_shape=[shape((tokens, LANES), F32)],
            out_specs=[pl.BlockSpec((tokens, LANES), lambda i: (0, 0))],
            scratch_shapes=[pltpu.VMEM((tokens, D), BF16)] + [pltpu.VMEM((tokens, 1), F32)] * 4,
            compiler_params=params(56),
            cost_estimate=cost(
                2 * tokens * D * vocab_tile * count, 2 * D * vocab_tile * count
            ),
            name="head",
        )
        stats[member].append(result[:, :3].T)

    early = (3 * vocab_tiles + 4) // 5
    rest = vocab_tiles - early
    if divisible and levels == 3 and rest > 0:
        schedule = [
            (gate_up, 0), (gate_up, 1), (halve, 0, 0), (gate_up, 2), (halve, 1, 0),
            (halve, 0, 1), (gate_up, 3), (halve, 2, 0), (hidden_of, 0), (halve, 1, 1),
            (join, 0, 1), (halve, 3, 0), (hidden_of, 1), (halve, 2, 1), (halve, 3, 1),
            (join, 1, 1), (gather_gain, 0), (hidden_of, 2), (join, 1, 0), (join, 0, 0),
            (gather_gain, 1), (hidden_of, 3), (join, 2, 1), (gather_gain, 2), (ready,),
            (down, 0), (join, 3, 1), (join, 2, 0), (down, 1, True), (join, 3, 0), (down, 1),
            (output, 0), (output, 1), (pack, 0), (pack, 1), (forward, 0), (head, 0, 0, early),
            (forward, 1), (head, 0, early, rest), (head, 1, 0, vocab_tiles),
        ]
    else:
        schedule = []
        for j in range(len(plan)):
            schedule += [(gate_up, j)] + [(halve, j, level) for level in range(last)]
            schedule += [(hidden_of, j)] + [(join, j, level) for level in range(last - 1, -1, -1)]
        schedule += [(gather_gain, level) for level in range(levels)] + [(ready,)]
        schedule += [(down, 0), (output, 0), (down, 1), (output, 1), (pack, 0), (pack, 1)]
        schedule += [(forward, 0), (forward, 1), (head, 0, 0, vocab_tiles)]
        schedule += [(head, 1, 0, vocab_tiles)]
    for step, *arguments in schedule:
        step(*arguments)

    def combine(parts):
        top = functools.reduce(jnp.maximum, [p[0] for p in parts])
        total = tree_sum([p[1] * jnp.exp(p[0] - top) for p in parts])
        picked = tree_sum([p[2] for p in parts])
        return jnp.stack([top, total, picked])

    merged = combine(stats[0]) if len(stats[0]) > 1 else stats[0][0]
    merged = jnp.stack([merged, stats[1][0]], axis=1)
    for level in range(levels):
        merged = combine([merged, col_xor(merged, 1 << level)])
    for level in range((row_count - 1).bit_length()):
        merged = combine([merged, row_xor(merged, 1 << level)])
    logprob = merged[2] - (merged[0] + jnp.log(merged[1]))
    difference = logprob[0] - logprob[1]
    one_hot = (segment[:, None] == jnp.arange(SEQS, dtype=jnp.int32)[None, :]).astype(F32)
    seq_sums = jnp.dot(difference, one_hot, precision=lax.Precision.HIGHEST)
    return seq_sums / seq_lengths.astype(F32)


def solution(mesh):
    placed = (
        P("row", "col"),
        P("col"),
        P("col", "row"),
        P("col", "row"),
        P("col", "row"),
        P("row", "col"),
        P("col"),
        P(None, "col", "row"),
        P(None, "col", "row"),
        P(None, "row", "col"),
        P("col"),
        P(None, ("row", "col")),
        P(),
        P(),
    )
    return jax.shard_map(per_device, mesh=mesh, in_specs=placed, out_specs=P(), check_vma=False)
```

```python
import functools

import jax
import jax.numpy as jnp
from jax import lax
from jax.experimental import pallas as pl
from jax.experimental.pallas import tpu as pltpu
from jax.sharding import PartitionSpec as P

D = 5120
HEAD_DIM = 128
SEQS = 8
LONGEST = 64

EPSILON = 1e-06
ROPE_BASE = 1000000.0
MASKED = -1e30
LANES = 128
HEAD_BLOCKS = 4
GATE_MIB = 46
DOWN_MIB = 46
BF16 = jnp.bfloat16
F32 = jnp.float32
MIB = 1 << 20

VMEM = pl.BlockSpec(memory_space=pltpu.VMEM)
ANY = pl.BlockSpec(memory_space=pl.ANY)
SMEM = pl.BlockSpec(memory_space=pltpu.SMEM)


def params(mib):
    return pltpu.CompilerParams(vmem_limit_bytes=mib * MIB)


def cost(flops, byte_count):
    del flops, byte_count
    return pl.CostEstimate(flops=1, bytes_accessed=1, transcendentals=0)


def call(kernel, operands, in_specs, token, out_shape, out_specs, **options):
    count, outs = len(operands), len(out_shape)

    def body(*refs):
        inputs, results, scratch = refs[:count], refs[count + 1 :], refs[count + outs + 2 :]
        kernel(*inputs, *results[:outs], *scratch)

    results = pl.pallas_call(
        body,
        in_specs=in_specs + [ANY],
        out_shape=out_shape + [jax.ShapeDtypeStruct((8, LANES), F32)],
        out_specs=out_specs + [ANY],
        **options,
    )(*operands, token[0])
    token[:] = [results[-1]]
    return results[:-1]


def row_xor(x, mask):
    count = lax.axis_size("row")
    return lax.ppermute(x, "row", [(i, i ^ mask) for i in range(count)])


def col_xor(x, mask):
    count = lax.axis_size("col")
    return lax.ppermute(x, "col", [(i, i ^ mask) for i in range(count)])


def tree_sum(values):
    values = list(values)
    while len(values) > 1:
        values = [values[i] + values[i + 1] for i in range(0, len(values), 2)]
    return values[0]


def sequence_layout(seq_lengths, token_index):
    ends_at = jnp.cumsum(seq_lengths)
    before = ends_at[None, :] <= token_index[:, None]
    segment = jnp.sum(before.astype(jnp.int32), axis=1)
    starts_at = jnp.sum(jnp.where(before, seq_lengths[None, :], 0), axis=1)
    return (segment, (token_index - starts_at).astype(F32))


def split_square(total):
    high = total.astype(BF16)
    low = (total - high.astype(F32)).astype(BF16)
    lane = lax.broadcasted_iota(jnp.int32, total.shape, 1)
    return jnp.where(lane < LANES // 2, high.astype(F32), low.astype(F32)).astype(BF16)


def join_square(tile):
    return tile + pltpu.roll(tile, LANES // 2, 1)


def assemble(offsets, blocks, gain, x_ref, square_ref, unit):
    step = 0
    for block in blocks:
        for first in range(0, block.shape[0], unit):
            rows = block[first : first + unit, :].astype(F32)
            place = pl.multiple_of(offsets[step], unit)
            x_ref[pl.ds(place, unit), :] = (rows * gain[...]).astype(BF16)
            square = jnp.sum(rows * rows, axis=1, keepdims=True)
            square_ref[pl.ds(place, unit), :] = jnp.broadcast_to(square, (unit, LANES))
            step += 1


def put_squares(square_ref, keep, send, at):
    half = keep.shape[0]
    total = square_ref[...]
    lane = lax.broadcasted_iota(jnp.int32, (half, LANES), 1)
    keep[:, at : at + LANES] = jnp.where(lane < LANES // 2, total[:half], 0.0)
    send[:, at : at + LANES] = split_square(total[half:])


def qkv_kernel(unit, count, offsets, *refs):
    blocks, (gain, wq, wk, wv, keep, send, x_ref, square_ref) = refs[:count], refs[count:]
    assemble(offsets, blocks, gain, x_ref, square_ref, unit)
    half = keep.shape[0]
    x = x_ref[...]
    at = 0
    for w in (wq, wk, wv):
        width = w.shape[1]
        part = jnp.dot(x, w[...], preferred_element_type=F32)
        keep[:, at : at + width] = part[:half]
        send[:, at : at + width] = part[half:].astype(BF16)
        at += width
    put_squares(square_ref, keep, send, at)


def core_add_kernel(keep, recv, *outs):
    rows, width = outs[0].shape
    for i, out in enumerate(outs):
        total = keep[i * rows : (i + 1) * rows, :] + recv[
            i * rows : (i + 1) * rows, :
        ].astype(F32)
        if i == 0:
            out[...] = total
        else:
            out[:, : width - LANES] = total[:, : width - LANES].astype(BF16)
            out[:, width - LANES :] = split_square(join_square(total[:, width - LANES :]))


def rope_kernel(rotated, count, *refs):
    parts, (cosine, sine, out) = refs[:count], refs[count:]
    width = out.shape[1]

    def summed(at):
        total = parts[0][:, at : at + LANES].astype(F32)
        for part in parts[1:]:
            total = total + part[:, at : at + LANES].astype(F32)
        return total

    scale = lax.rsqrt(join_square(summed(width)) / D + EPSILON)
    for at in range(0, width, HEAD_DIM):
        total = summed(at) * scale
        if at < rotated:
            total = total * cosine[...] + pltpu.roll(total, HEAD_DIM // 2, 1) * sine[...]
        out[:, at : at + HEAD_DIM] = total.astype(BF16)


def attention_kernel(heads, kv_heads, count, block, places, row_places, *refs):
    pieces, (bias, w_out), outs, (qkv, attended) = (
        refs[:count],
        refs[count : count + 2],
        refs[count + 2 : -2],
        refs[-2:],
    )
    row_unit = outs[0].shape[0]
    unit = pieces[0].shape[0]
    for i, piece in enumerate(pieces):
        qkv[pl.ds(pl.multiple_of(places[i], unit), unit), :] = piece[...]
    tokens = qkv.shape[0]
    group = heads // kv_heads
    window = min(tokens, block + LONGEST)
    for start in range(0, tokens, block):
        first = max(0, start + block - window)
        mask = bias[start : start + block, :]
        mask = jnp.concatenate([mask] * group, axis=0)
        for g in range(kv_heads):
            q = jnp.concatenate(
                [
                    qkv[start : start + block, h * HEAD_DIM : (h + 1) * HEAD_DIM]
                    for h in range(g * group, (g + 1) * group)
                ],
                axis=0,
            )
            k_at = (heads + g) * HEAD_DIM
            v_at = (heads + kv_heads + g) * HEAD_DIM
            k = qkv[first : first + window, k_at : k_at + HEAD_DIM]
            v = qkv[first : first + window, v_at : v_at + HEAD_DIM]
            scores = lax.dot_general(
                q, k, (((1,), (1,)), ((), ())), preferred_element_type=F32
            ) * HEAD_DIM ** (-0.5)
            scores = scores + mask
            weights = jnp.exp(scores - jnp.max(scores, axis=1, keepdims=True))
            total = jnp.sum(weights, axis=1, keepdims=True)
            weights = weights / total
            high = weights.astype(BF16)
            low = (weights - high.astype(F32)).astype(BF16)
            result = jnp.dot(high, v, preferred_element_type=F32)
            result = (result + jnp.dot(low, v, preferred_element_type=F32)).astype(BF16)
            for h in range(group):
                at = (g * group + h) * HEAD_DIM
                for sub in range(0, block, row_unit):
                    place = pl.multiple_of(row_places[(start + sub) // row_unit], row_unit)
                    attended[pl.ds(place, row_unit), at : at + HEAD_DIM] = result[
                        h * block + sub : h * block + sub + row_unit
                    ]
    product = jnp.dot(attended[...], w_out[...], preferred_element_type=F32)
    for i, out in enumerate(outs):
        out[...] = product[i * row_unit : (i + 1) * row_unit].astype(out.dtype)


def arrange_kernel(unit, offsets, *refs):
    blocks, (gain, out, square_ref) = refs[:-3], refs[-3:]
    inverse = 1.0 / gain[...]
    step = 0
    for block in blocks:
        for first in range(0, block.shape[0], unit):
            rows = block[first : first + unit, :]
            place = pl.multiple_of(offsets[step], unit)
            out[pl.ds(place, unit), :] = rows
            plain = rows.astype(F32) * inverse
            square = jnp.sum(plain * plain, axis=1, keepdims=True)
            square_ref[pl.ds(place, unit), :] = jnp.broadcast_to(square, (unit, LANES))
            step += 1


def gate_up_kernel(squares, x, *refs):
    weights, (keep, send) = refs[: -2 - squares], refs[-2:]
    half = keep.shape[1]
    count = len(weights) // 2
    base = 2 * pl.program_id(0) if squares else 0
    for i in range(2):
        w = jnp.concatenate([w[0] for w in weights[i * count : (i + 1) * count]], axis=0)
        part = jnp.dot(x[...], w, preferred_element_type=F32)
        keep[base + i] = part[:half]
        send[base + i] = part[half:].astype(BF16)
    if squares:

        @pl.when(pl.program_id(0) == 0)
        def _():
            group = keep.shape[0] - 1
            keep[group] = jnp.zeros(keep.shape[1:], F32)
            send[group] = jnp.zeros(send.shape[1:], BF16)
            total = refs[-3][...]
            lane = lax.broadcasted_iota(jnp.int32, (half, LANES), 1)
            keep[group, :, :LANES] = jnp.where(lane < LANES // 2, total[:half], 0.0)
            send[group, :, :LANES] = split_square(total[half:])


def halve_kernel(squares, keep, recv, kept, send):
    half = kept.shape[1]
    body = keep.shape[0] - squares
    kept[...] = keep[:, :half, :] + recv[:, :half, :].astype(F32)
    send[:body] = (keep[:body, half:, :] + recv[:body, half:, :].astype(F32)).astype(BF16)
    if squares:
        total = keep[body, half:, :LANES] + recv[body, half:, :LANES].astype(F32)
        send[body] = jnp.zeros(send.shape[1:], BF16)
        send[body, :, :LANES] = split_square(join_square(total))


def hidden_kernel(squares, keep, recv, *refs):
    if squares:
        hidden, scale_ref = refs
        group = keep.shape[0] - 1
        total = keep[group, :, :LANES] + recv[group, :, :LANES].astype(F32)
        scale_ref[...] = lax.rsqrt(join_square(total) / D + EPSILON)
    else:
        scale_ref, hidden = refs
    scale = scale_ref[:, :1]
    width = keep.shape[2]
    for i in range(keep.shape[0] // 2):
        gate = (keep[2 * i] + recv[2 * i].astype(F32)) * scale
        up = (keep[2 * i + 1] + recv[2 * i + 1].astype(F32)) * scale
        hidden[:, i * width : (i + 1) * width] = (
            gate / (1.0 + jnp.exp(-gate)) * up
        ).astype(BF16)


def join_kernel(first, second, out):
    rows = first.shape[0]
    out[:rows] = first[...]
    out[rows:] = second[...]


def pack_kernel(*refs):
    parts, out = refs[:-1], refs[-1]
    for i, part in enumerate(parts):
        out[i] = part[...]


def output_kernel(stream, gain, *refs):
    parts, out = refs[:-1], refs[-1]
    total = stream[...].astype(F32)
    for part in parts:
        total = total + part[...].astype(F32)
    out[...] = (total * gain[...]).astype(BF16)


def down_kernel(sources, count, added, unit, rows, offsets, *refs):
    own, other, before = refs[:count], refs[count : 2 * count], refs[2 * count : 2 * count + added]
    outs, total = refs[-rows - 1 : -1], refs[-1]
    weights = refs[2 * count + added : -rows - 1]
    tile = len(weights) * weights[0].shape[1]
    for i, (which, at) in enumerate(sources):

        @pl.when(pl.program_id(0) == i)
        def _():
            hidden = jnp.concatenate(
                [own[which][:, at : at + tile], other[which][:, at : at + tile]], axis=0
            )
            w = jnp.concatenate([w[0] for w in weights], axis=0)
            part = jnp.dot(hidden, w, preferred_element_type=F32)
            if i > 0:
                part = part + total[...]
            elif added:
                part = part + before[0][...]
            total[...] = part

    @pl.when(pl.program_id(0) == len(sources) - 1)
    def _():
        step = 0
        for out in outs:
            for first in range(0, out.shape[0], unit):
                place = pl.multiple_of(offsets[step], unit)
                out[first : first + unit, :] = total[pl.ds(place, unit), :].astype(out.dtype)
                step += 1


def head_kernel(rows, first, col_index, row_places, *refs):
    own, other = refs[:rows], refs[rows : 2 * rows]
    gains, target, *weights = refs[2 * rows : -6]
    out, lhs, square, top, total, picked = refs[-6:]
    step = pl.program_id(0)
    chips, unit, width = own[0].shape

    @pl.when(step == 0)
    def _():
        inverse = 1.0 / gains[...]
        for i in range(rows):
            place = pl.multiple_of(row_places[i], unit)
            sums = jnp.zeros((unit, 1), F32)
            for core, arrays in enumerate((own, other)):
                for j in range(chips):
                    feature = pl.multiple_of(col_index[2 * j + core] * width, LANES)
                    values = arrays[i][j]
                    lhs[pl.ds(place, unit), pl.ds(feature, width)] = values
                    plain = values.astype(F32) * inverse[2 * j + core : 2 * j + core + 1, :]
                    sums += jnp.sum(plain * plain, axis=1, keepdims=True)
            square[pl.ds(place, unit), :] = sums
        top[...] = jnp.full_like(top, MASKED)
        total[...] = jnp.zeros_like(total)
        picked[...] = jnp.zeros_like(picked)

    depth = weights[0].shape[0]
    logits = jnp.dot(lhs[:, :depth], weights[0][...], preferred_element_type=F32)
    for i in range(1, len(weights)):
        logits += jnp.dot(
            lhs[:, i * depth : (i + 1) * depth], weights[i][...], preferred_element_type=F32
        )
    logits = logits * lax.rsqrt(square[...] / D + EPSILON)
    lane = lax.broadcasted_iota(jnp.int32, logits.shape, 1)
    lane = lane + (step + first) * logits.shape[1]
    hit = jnp.where(lane == target[...], logits, 0.0)
    picked[...] += jnp.sum(hit, axis=1, keepdims=True)
    new_top = jnp.maximum(top[...], jnp.max(logits, axis=1, keepdims=True))
    total[...] = total[...] * jnp.exp(top[...] - new_top) + jnp.sum(
        jnp.exp(logits - new_top), axis=1, keepdims=True
    )
    top[...] = new_top

    @pl.when(step == pl.num_programs(0) - 1)
    def _():
        place = lax.broadcasted_iota(jnp.int32, out.shape, 1)
        out[...] = jnp.where(
            place == 0, top[...], jnp.where(place == 1, total[...], picked[...])
        )


def hold(arrays, token):
    def kernel(*refs):
        del refs

    count = len(arrays)
    results = pl.pallas_call(
        kernel,
        out_shape=[jax.ShapeDtypeStruct(array.shape, array.dtype) for array in arrays]
        + [jax.ShapeDtypeStruct((8, LANES), F32)],
        in_specs=[ANY] * (count + 1),
        out_specs=[ANY] * (count + 1),
        input_output_aliases={i: i for i in range(count)},
        compiler_params=params(16),
        cost_estimate=cost(0, 0),
        name="hold",
    )(*arrays, token[0])
    token[:] = [results[-1]]
    return results[:-1]


def per_device(
    residual,
    attn_gain,
    w_query,
    w_key,
    w_value,
    w_out,
    mlp_gain,
    w_gate,
    w_up,
    w_down,
    final_gain,
    w_head,
    seq_lengths,
    targets,
):
    row_count = lax.axis_size("row")
    col_count = lax.axis_size("col")
    chips = col_count // 2
    row_index = lax.axis_index("row")
    col_index = lax.axis_index("col")
    core = col_index % 2
    chip = col_index // 2
    row_tokens, features = residual.shape
    tokens = row_tokens * row_count
    col_tokens = tokens // col_count
    quarter = tokens // 4
    heads = w_query.shape[1] // HEAD_DIM
    kv_heads = w_key.shape[1] // HEAD_DIM
    qkv_width = w_query.shape[1] + 2 * w_key.shape[1]
    rotated = w_query.shape[1] + w_key.shape[1]
    ff_local = w_gate.shape[2]
    vocab_local = w_head.shape[1]

    row_range = jnp.arange(row_count, dtype=jnp.int32)
    col_range = jnp.arange(col_count, dtype=jnp.int32)
    row_rel = row_range ^ row_index
    col_rel = col_range ^ col_index

    token_index = jnp.arange(tokens, dtype=jnp.int32)
    segment, positions = sequence_layout(seq_lengths, token_index)
    block = min(64, tokens)
    window = min(tokens, block + LONGEST)
    first_key = jnp.maximum(0, (token_index // block + 1) * block - window)
    key_index = first_key[:, None] + jnp.arange(window, dtype=jnp.int32)[None, :]
    key_segment, _ = sequence_layout(seq_lengths, key_index.reshape(-1))
    allowed = (key_segment.reshape(tokens, window) == segment[:, None]) & (
        key_index <= token_index[:, None]
    )
    bias = jnp.where(allowed, 0.0, MASKED).astype(F32)
    own_positions = lax.dynamic_slice_in_dim(positions, col_index * col_tokens, col_tokens)
    exponent = jnp.arange(HEAD_DIM // 2, dtype=F32) * 2.0 / HEAD_DIM
    angles = own_positions[:, None] * (ROPE_BASE ** (-exponent))[None, :]
    cosine, sine = jnp.cos(angles), jnp.sin(angles)
    cosine = jnp.concatenate([cosine, cosine], axis=1)
    sine = jnp.concatenate([-sine, sine], axis=1)

    blocks = [residual] + [row_xor(residual, j) for j in range(1, row_count)]
    shape = jax.ShapeDtypeStruct

    per_row = row_tokens // col_tokens
    col_block = (row_rel[:, None] * per_row + jnp.arange(per_row, dtype=jnp.int32)).reshape(-1)
    relative = col_block ^ col_index
    offsets = ((relative & 1) * chips + (relative >> 1)) * col_tokens
    half = tokens // 2
    wide = qkv_width + LANES
    keep, send = pl.pallas_call(
        functools.partial(qkv_kernel, col_tokens, row_count),
        out_shape=[shape((half, wide), F32), shape((half, wide), BF16)],
        in_specs=[SMEM] + [VMEM] * (row_count + 4),
        out_specs=[VMEM] * 2,
        scratch_shapes=[pltpu.VMEM((tokens, features), BF16), pltpu.VMEM((tokens, LANES), F32)],
        compiler_params=params(56),
        cost_estimate=cost(
            2 * tokens * features * qkv_width, 2 * qkv_width * (features + tokens)
        ),
        name="qkv_partial",
    )(offsets, *blocks, attn_gain[None, :], w_query, w_key, w_value)
    received = col_xor(send, 1)
    parts = pl.pallas_call(
        core_add_kernel,
        out_shape=[shape((col_tokens, wide), F32 if i == 0 else BF16) for i in range(chips)],
        in_specs=[VMEM] * 2,
        out_specs=[VMEM] * chips,
        compiler_params=params(16),
        cost_estimate=cost(half * qkv_width, 6 * half * qkv_width),
        name="qkv_core_add",
    )(keep, received)
    parts = [parts[0]] + [col_xor(parts[j], 2 * j) for j in range(1, chips)]
    mine = pl.pallas_call(
        functools.partial(rope_kernel, rotated, chips),
        out_shape=shape((col_tokens, qkv_width), BF16),
        in_specs=[VMEM] * (chips + 2),
        out_specs=VMEM,
        compiler_params=params(16),
        cost_estimate=cost(8 * col_tokens * qkv_width, 2 * tokens * qkv_width),
        name="qkv_rope",
    )(*parts, cosine, sine)
    pieces = [mine] + [col_xor(mine, 2 * j) for j in range(1, chips)]
    pieces = pieces + [col_xor(piece, 1) for piece in pieces]
    piece_index = [2 * j for j in range(chips)] + [2 * j + 1 for j in range(chips)]
    places = (jnp.array(piece_index, jnp.int32) ^ col_index) * col_tokens

    projected = pl.pallas_call(
        functools.partial(attention_kernel, heads, kv_heads, col_count, block),
        out_shape=[
            shape((row_tokens, features), F32 if i == 0 else BF16) for i in range(row_count)
        ],
        in_specs=[SMEM] * 2 + [VMEM] * (col_count + 2),
        out_specs=[VMEM] * row_count,
        scratch_shapes=[
            pltpu.VMEM((tokens, qkv_width), BF16),
            pltpu.VMEM((tokens, heads * HEAD_DIM), BF16),
        ],
        compiler_params=params(32),
        cost_estimate=cost(
            2 * tokens * heads * HEAD_DIM * features * 2, 2 * heads * HEAD_DIM * features * 2
        ),
        name="attention_out",
    )(places, row_rel * row_tokens, *pieces, bias, w_out)
    projected = [projected[0]] + [row_xor(projected[j], j) for j in range(1, row_count)]
    stream = residual.astype(F32) + tree_sum([p.astype(F32) for p in projected])
    scaled_stream = (stream * mlp_gain[None, :]).astype(BF16)

    levels = (col_count - 1).bit_length()
    blocks = [scaled_stream] + [row_xor(scaled_stream, j) for j in range(1, row_count)]
    position = sum(((relative >> level) & 1) << (levels - 1 - level) for level in range(levels))
    half_offsets = position * col_tokens
    token = [mlp_gain]
    mlp_in, squares = call(
        functools.partial(arrange_kernel, col_tokens),
        [half_offsets, *blocks, mlp_gain[None, :]],
        [SMEM] + [VMEM] * (row_count + 1),
        token,
        out_shape=[
            shape((tokens, features), BF16),
            shape((tokens, LANES), F32),
        ],
        out_specs=[VMEM] * 2,
        compiler_params=params(16),
        cost_estimate=cost(tokens * features, 4 * tokens * features),
        name="mlp_in",
    )

    divisible = ff_local % (3 * LANES) == 0
    tile = ff_local // 3 if divisible else ff_local
    tiles = ff_local // tile
    sub = tile // 3 if tile % (3 * LANES) == 0 else tile
    subs = tile // sub
    plan = [(0, 0, 1), (1, 0, 1)]
    if divisible:
        plan = [(0, 0, 1), (0, 1, 2), (1, 0, 2), (1, 2, 1)]
    last = levels - 1
    keeps, arrivals, hiddens = {}, {}, {}
    scale = []
    states = {}

    def gate_up(j):
        member, first, count = plan[j]
        first = first * subs
        squared = j == 0
        groups = 2 * count * subs + squared
        weights = [
            pl.BlockSpec((1, features // 2, sub), lambda i, q=q: (member, q, first + i))
            for q in range(2)
        ]
        whole = pl.BlockSpec((tokens, features), lambda i: (0, 0))
        if squared:
            out = pl.BlockSpec((groups, half, sub), lambda i: (0, 0, 0))
        else:
            out = pl.BlockSpec((2, half, sub), lambda i: (i, 0, 0))
        keep, send = call(
            functools.partial(gate_up_kernel, squared),
            [mlp_in, w_gate, w_gate, w_up, w_up] + [squares] * squared,
            [whole] + weights * 2 + [pl.BlockSpec((tokens, LANES), lambda i: (0, 0))] * squared,
            token,
            grid=(count * subs,),
            out_shape=[shape((groups, half, sub), F32), shape((groups, half, sub), BF16)],
            out_specs=[out] * 2,
            compiler_params=params(GATE_MIB),
            cost_estimate=cost(4 * tokens * features * tile * count, 4 * tile * count * features),
            name="gate_up",
        )
        keeps[j], arrivals[j] = keep, col_xor(send, 1)

    def halve(j, level):
        count = 1 if j == 0 else plan[j][2]
        keep = keeps[j]
        groups, rows, _ = keep.shape
        part = groups // count
        keeps[j], send = call(
            functools.partial(halve_kernel, j == 0),
            [keep, arrivals[j]],
            [pl.BlockSpec((part, rows, sub), lambda i: (i, 0, 0))] * 2,
            token,
            grid=(count,),
            out_shape=[
                shape((groups, rows // 2, sub), F32),
                shape((groups, rows // 2, sub), BF16),
            ],
            out_specs=[pl.BlockSpec((part, rows // 2, sub), lambda i: (i, 0, 0))] * 2,
            compiler_params=params(24),
            cost_estimate=cost(rows * sub * groups, 9 * rows * sub * groups),
            name="halve",
        )
        arrivals[j] = col_xor(send, 2 << level)

    def hidden_of(j):
        groups, rows, _ = keeps[j].shape
        squared = j == 0
        hidden_shape = shape((rows, groups // 2 * sub), BF16)
        operands = [keeps[j], arrivals[j]] + ([] if squared else scale)
        hidden, *extra = call(
            functools.partial(hidden_kernel, squared),
            operands,
            [VMEM] * len(operands),
            token,
            out_shape=[hidden_shape] + [shape((rows, LANES), F32)] * squared,
            out_specs=[VMEM] * (1 + squared),
            compiler_params=params(24),
            cost_estimate=cost(8 * rows * groups * sub, 6 * rows * groups * sub),
            name="hidden",
        )
        if squared:
            scale[:] = extra
        hiddens[j] = (hidden, col_xor(hidden, 1 << last))

    def join(j, level):
        first, second = hiddens[j]
        rows, width = first.shape
        (joined,) = call(
            join_kernel,
            [first, second],
            [VMEM] * 2,
            token,
            out_shape=[shape((2 * rows, width), BF16)],
            out_specs=[VMEM],
            compiler_params=params(16),
            cost_estimate=cost(rows * width, 8 * rows * width),
            name="join",
        )
        hiddens[j] = (joined, col_xor(joined, 1 << level))

    partial = {0: [], 1: []}
    summed = {0: [], 1: []}

    def down(member, early=False):
        which = [j for j in range(len(plan)) if plan[j][0] == member and j not in summed[member]]
        if early:
            which = which[:1]
            summed[member] = which
        own = [hiddens[j][0] for j in which]
        other = [hiddens[j][1] for j in which]
        sources = [(k, i * tile) for k, j in enumerate(which) for i in range(plan[j][2])]
        first = plan[which[0]][1]
        before = partial[member]
        count = len(which)
        rows = 0 if early else row_count
        sum_spec = pl.BlockSpec((tokens, features), lambda i: (0, 0))
        sum_shape = shape((tokens, features), F32)
        row_shapes = [
            shape((row_tokens, features), F32 if i == 0 else BF16) for i in range(row_count)
        ]
        parts = call(
            functools.partial(down_kernel, sources, count, len(before), col_tokens, rows),
            [half_offsets, *own, *other, *before] + [w_down] * 3,
            [SMEM]
            + [pl.BlockSpec(array.shape, lambda i: (0, 0)) for array in own + other]
            + [sum_spec] * len(before)
            + [
                pl.BlockSpec((1, tile // 3, features), lambda i, q=q: (member, 3 * (first + i) + q, 0))
                for q in range(3)
            ],
            token,
            grid=(len(sources),),
            out_shape=[sum_shape] if early else row_shapes,
            out_specs=[sum_spec]
            if early
            else [pl.BlockSpec((row_tokens, features), lambda i: (0, 0))] * row_count,
            scratch_shapes=[] if early else [pltpu.VMEM((tokens, features), F32)],
            compiler_params=params(DOWN_MIB),
            cost_estimate=cost(
                2 * tokens * features * ff_local, 2 * ff_local * (features + tokens)
            ),
            name="down",
        )
        if early:
            partial[member] = [parts[0]]
        else:
            states[member] = [parts[0]] + [row_xor(parts[j], j) for j in range(1, row_count)]

    def output(member):
        parts = states[member]
        (scaled,) = call(
            output_kernel,
            [stream, final_gain[None, :], *parts],
            [VMEM] * (2 + row_count),
            token,
            out_shape=[shape((row_tokens, features), BF16)],
            out_specs=[VMEM],
            compiler_params=params(16),
            cost_estimate=cost(8 * row_tokens * features, 16 * row_tokens * features),
            name="output",
        )
        states[member] = [scaled] + [col_xor(scaled, 2 * j) for j in range(1, chips)]

    def pack(member):
        (by_chip,) = call(
            pack_kernel,
            states[member],
            [VMEM] * chips,
            token,
            out_shape=[shape((chips, row_tokens, features), BF16)],
            out_specs=[VMEM],
            compiler_params=params(16),
            cost_estimate=cost(chips * row_tokens * features, 4 * chips * row_tokens * features),
            name="pack",
        )
        other = col_xor(by_chip, 1)
        states[member] = [by_chip, other] + [row_xor(by_chip, j) for j in range(1, row_count)]

    def forward(member):
        by_chip, other, *rows = states[member]
        rows = hold(rows, token)
        states[member] = [by_chip, *rows, other] + [col_xor(array, 1) for array in rows]

    vocab_start = (row_index * col_count + col_index) * vocab_local
    local_targets = (targets - vocab_start)[:, None]
    vocab_tile = 512 if vocab_local % 512 == 0 else vocab_local
    vocab_tiles = vocab_local // vocab_tile
    stats = {0: [], 1: []}

    gain_parts = [final_gain[None, :]]
    small = []

    def gather_gain(level):
        (part,) = hold(gain_parts[-1:], token)
        gain_parts.append(jnp.concatenate([part, col_xor(part, 1 << level)], axis=0))

    def ready():
        small[:] = hold([gain_parts[-1], local_targets, col_rel, row_rel * row_tokens], token)

    def head(member, first, count):
        gains, target, features_at, rows_at = small
        state = states[member]
        (result,) = call(
            functools.partial(head_kernel, row_count, first),
            [features_at, rows_at, *state, gains, target] + [w_head] * HEAD_BLOCKS,
            [SMEM] * 2
            + [pl.BlockSpec(state[0].shape, lambda i: (0, 0, 0))] * (2 * row_count)
            + [pl.BlockSpec(gains.shape, lambda i: (0, 0))]
            + [pl.BlockSpec((tokens, 1), lambda i: (0, 0))]
            + [
                pl.BlockSpec((D // HEAD_BLOCKS, vocab_tile), lambda i, q=q: (q, first + i))
                for q in range(HEAD_BLOCKS)
            ],
            token,
            grid=(count,),
            out_shape=[shape((tokens, LANES), F32)],
            out_specs=[pl.BlockSpec((tokens, LANES), lambda i: (0, 0))],
            scratch_shapes=[pltpu.VMEM((tokens, D), BF16)] + [pltpu.VMEM((tokens, 1), F32)] * 4,
            compiler_params=params(56),
            cost_estimate=cost(
                2 * tokens * D * vocab_tile * count, 2 * D * vocab_tile * count
            ),
            name="head",
        )
        stats[member].append(result[:, :3].T)

    if divisible and levels == 3:
        schedule = [
            (gate_up, 0), (gate_up, 1), (halve, 0, 0), (gate_up, 2), (halve, 1, 0),
            (halve, 0, 1), (gate_up, 3), (halve, 2, 0), (hidden_of, 0), (halve, 1, 1),
            (join, 0, 1), (halve, 3, 0), (hidden_of, 1), (halve, 2, 1), (halve, 3, 1),
            (join, 1, 1), (gather_gain, 0), (hidden_of, 2), (join, 1, 0), (join, 0, 0),
            (gather_gain, 1), (hidden_of, 3), (join, 2, 1), (gather_gain, 2), (join, 3, 1),
            (ready,), (down, 0), (join, 2, 0), (down, 1, True), (join, 3, 0), (down, 1),
            (output, 0), (output, 1), (pack, 0), (pack, 1), (forward, 0),
            (head, 0, 0, vocab_tiles), (forward, 1), (head, 1, 0, vocab_tiles),
        ]
    else:
        schedule = []
        for j in range(len(plan)):
            schedule += [(gate_up, j)] + [(halve, j, level) for level in range(last)]
            schedule += [(hidden_of, j)] + [(join, j, level) for level in range(last - 1, -1, -1)]
        schedule += [(gather_gain, level) for level in range(levels)] + [(ready,)]
        schedule += [(down, 0), (output, 0), (down, 1), (output, 1), (pack, 0), (pack, 1)]
        schedule += [(forward, 0), (forward, 1), (head, 0, 0, vocab_tiles)]
        schedule += [(head, 1, 0, vocab_tiles)]
    for step, *arguments in schedule:
        step(*arguments)

    def combine(parts):
        top = functools.reduce(jnp.maximum, [p[0] for p in parts])
        total = tree_sum([p[1] * jnp.exp(p[0] - top) for p in parts])
        picked = tree_sum([p[2] for p in parts])
        return jnp.stack([top, total, picked])

    merged = combine(stats[0]) if len(stats[0]) > 1 else stats[0][0]
    merged = jnp.stack([merged, stats[1][0]], axis=1)
    for level in range(levels):
        merged = combine([merged, col_xor(merged, 1 << level)])
    for level in range((row_count - 1).bit_length()):
        merged = combine([merged, row_xor(merged, 1 << level)])
    logprob = merged[2] - (merged[0] + jnp.log(merged[1]))
    difference = logprob[0] - logprob[1]
    one_hot = (segment[:, None] == jnp.arange(SEQS, dtype=jnp.int32)[None, :]).astype(F32)
    seq_sums = jnp.dot(difference, one_hot, precision=lax.Precision.HIGHEST)
    return seq_sums / seq_lengths.astype(F32)


def solution(mesh):
    placed = (
        P("row", "col"),
        P("col"),
        P("col", "row"),
        P("col", "row"),
        P("col", "row"),
        P("row", "col"),
        P("col"),
        P(None, "col", "row"),
        P(None, "col", "row"),
        P(None, "row", "col"),
        P("col"),
        P(None, ("row", "col")),
        P(),
        P(),
    )
    return jax.shard_map(per_device, mesh=mesh, in_specs=placed, out_specs=P(), check_vma=False)
```

```python
import functools

import jax
import jax.numpy as jnp
from jax import lax
from jax.experimental import pallas as pl
from jax.experimental.pallas import tpu as pltpu
from jax.sharding import PartitionSpec as P

D = 5120
HEAD_DIM = 128
SEQS = 8
LONGEST = 64

EPSILON = 1e-06
ROPE_BASE = 1000000.0
MASKED = -1e30
LANES = 128
HEAD_BLOCKS = 4
GATE_MIB = 46
DOWN_MIB = 46
HEAD_MIB = 46
BF16 = jnp.bfloat16
F32 = jnp.float32
MIB = 1 << 20

VMEM = pl.BlockSpec(memory_space=pltpu.VMEM)
ANY = pl.BlockSpec(memory_space=pl.ANY)
SMEM = pl.BlockSpec(memory_space=pltpu.SMEM)


def params(mib):
    return pltpu.CompilerParams(vmem_limit_bytes=mib * MIB)


def cost(flops, byte_count):
    del flops, byte_count
    return pl.CostEstimate(flops=1, bytes_accessed=1, transcendentals=0)


def call(kernel, operands, in_specs, token, out_shape, out_specs, **options):
    count, outs = len(operands), len(out_shape)

    def body(*refs):
        inputs, results, scratch = refs[:count], refs[count + 1 :], refs[count + outs + 2 :]
        kernel(*inputs, *results[:outs], *scratch)

    results = pl.pallas_call(
        body,
        in_specs=in_specs + [ANY],
        out_shape=out_shape + [jax.ShapeDtypeStruct((8, LANES), F32)],
        out_specs=out_specs + [ANY],
        **options,
    )(*operands, token[0])
    token[:] = [results[-1]]
    return results[:-1]


def row_xor(x, mask):
    count = lax.axis_size("row")
    return lax.ppermute(x, "row", [(i, i ^ mask) for i in range(count)])


def col_xor(x, mask):
    count = lax.axis_size("col")
    return lax.ppermute(x, "col", [(i, i ^ mask) for i in range(count)])


def tree_sum(values):
    values = list(values)
    while len(values) > 1:
        values = [values[i] + values[i + 1] for i in range(0, len(values), 2)]
    return values[0]


def sequence_layout(seq_lengths, token_index):
    ends_at = jnp.cumsum(seq_lengths)
    before = ends_at[None, :] <= token_index[:, None]
    segment = jnp.sum(before.astype(jnp.int32), axis=1)
    starts_at = jnp.sum(jnp.where(before, seq_lengths[None, :], 0), axis=1)
    return (segment, (token_index - starts_at).astype(F32))


def split_square(total):
    high = total.astype(BF16)
    low = (total - high.astype(F32)).astype(BF16)
    lane = lax.broadcasted_iota(jnp.int32, total.shape, 1)
    return jnp.where(lane < LANES // 2, high.astype(F32), low.astype(F32)).astype(BF16)


def join_square(tile):
    return tile + pltpu.roll(tile, LANES // 2, 1)


def assemble(offsets, blocks, gain, x_ref, square_ref, unit):
    step = 0
    for block in blocks:
        for first in range(0, block.shape[0], unit):
            rows = block[first : first + unit, :].astype(F32)
            place = pl.multiple_of(offsets[step], unit)
            x_ref[pl.ds(place, unit), :] = (rows * gain[...]).astype(BF16)
            square = jnp.sum(rows * rows, axis=1, keepdims=True)
            square_ref[pl.ds(place, unit), :] = jnp.broadcast_to(square, (unit, LANES))
            step += 1


def put_squares(square_ref, keep, send, at):
    half = keep.shape[0]
    total = square_ref[...]
    lane = lax.broadcasted_iota(jnp.int32, (half, LANES), 1)
    keep[:, at : at + LANES] = jnp.where(lane < LANES // 2, total[:half], 0.0)
    send[:, at : at + LANES] = split_square(total[half:])


def qkv_kernel(unit, count, offsets, *refs):
    blocks, (gain, wq, wk, wv, keep, send, x_ref, square_ref) = refs[:count], refs[count:]
    assemble(offsets, blocks, gain, x_ref, square_ref, unit)
    half = keep.shape[0]
    x = x_ref[...]
    at = 0
    for w in (wq, wk, wv):
        width = w.shape[1]
        part = jnp.dot(x, w[...], preferred_element_type=F32)
        keep[:, at : at + width] = part[:half]
        send[:, at : at + width] = part[half:].astype(BF16)
        at += width
    put_squares(square_ref, keep, send, at)


def core_add_kernel(keep, recv, *outs):
    rows, width = outs[0].shape
    for i, out in enumerate(outs):
        total = keep[i * rows : (i + 1) * rows, :] + recv[
            i * rows : (i + 1) * rows, :
        ].astype(F32)
        if i == 0:
            out[...] = total
        else:
            out[:, : width - LANES] = total[:, : width - LANES].astype(BF16)
            out[:, width - LANES :] = split_square(join_square(total[:, width - LANES :]))


def rope_kernel(rotated, count, *refs):
    parts, (cosine, sine, out) = refs[:count], refs[count:]
    width = out.shape[1]

    def summed(at):
        total = parts[0][:, at : at + LANES].astype(F32)
        for part in parts[1:]:
            total = total + part[:, at : at + LANES].astype(F32)
        return total

    scale = lax.rsqrt(join_square(summed(width)) / D + EPSILON)
    for at in range(0, width, HEAD_DIM):
        total = summed(at) * scale
        if at < rotated:
            total = total * cosine[...] + pltpu.roll(total, HEAD_DIM // 2, 1) * sine[...]
        out[:, at : at + HEAD_DIM] = total.astype(BF16)


def attention_kernel(heads, kv_heads, count, block, places, row_places, *refs):
    pieces, (bias, w_out), outs, (qkv, attended) = (
        refs[:count],
        refs[count : count + 2],
        refs[count + 2 : -2],
        refs[-2:],
    )
    row_unit = outs[0].shape[0]
    unit = pieces[0].shape[0]
    for i, piece in enumerate(pieces):
        qkv[pl.ds(pl.multiple_of(places[i], unit), unit), :] = piece[...]
    tokens = qkv.shape[0]
    group = heads // kv_heads
    window = min(tokens, block + LONGEST)
    for start in range(0, tokens, block):
        first = max(0, start + block - window)
        mask = bias[start : start + block, :]
        mask = jnp.concatenate([mask] * group, axis=0)
        for g in range(kv_heads):
            q = jnp.concatenate(
                [
                    qkv[start : start + block, h * HEAD_DIM : (h + 1) * HEAD_DIM]
                    for h in range(g * group, (g + 1) * group)
                ],
                axis=0,
            )
            k_at = (heads + g) * HEAD_DIM
            v_at = (heads + kv_heads + g) * HEAD_DIM
            k = qkv[first : first + window, k_at : k_at + HEAD_DIM]
            v = qkv[first : first + window, v_at : v_at + HEAD_DIM]
            scores = lax.dot_general(
                q, k, (((1,), (1,)), ((), ())), preferred_element_type=F32
            ) * HEAD_DIM ** (-0.5)
            scores = scores + mask
            weights = jnp.exp(scores - jnp.max(scores, axis=1, keepdims=True))
            total = jnp.sum(weights, axis=1, keepdims=True)
            weights = weights / total
            high = weights.astype(BF16)
            low = (weights - high.astype(F32)).astype(BF16)
            result = jnp.dot(high, v, preferred_element_type=F32)
            result = (result + jnp.dot(low, v, preferred_element_type=F32)).astype(BF16)
            for h in range(group):
                at = (g * group + h) * HEAD_DIM
                for sub in range(0, block, row_unit):
                    place = pl.multiple_of(row_places[(start + sub) // row_unit], row_unit)
                    attended[pl.ds(place, row_unit), at : at + HEAD_DIM] = result[
                        h * block + sub : h * block + sub + row_unit
                    ]
    product = jnp.dot(attended[...], w_out[...], preferred_element_type=F32)
    for i, out in enumerate(outs):
        out[...] = product[i * row_unit : (i + 1) * row_unit].astype(out.dtype)


def arrange_kernel(unit, offsets, *refs):
    blocks, (gain, out, square_ref) = refs[:-3], refs[-3:]
    inverse = 1.0 / gain[...]
    step = 0
    for block in blocks:
        for first in range(0, block.shape[0], unit):
            rows = block[first : first + unit, :]
            place = pl.multiple_of(offsets[step], unit)
            out[pl.ds(place, unit), :] = rows
            plain = rows.astype(F32) * inverse
            square = jnp.sum(plain * plain, axis=1, keepdims=True)
            square_ref[pl.ds(place, unit), :] = jnp.broadcast_to(square, (unit, LANES))
            step += 1


def gate_up_kernel(squares, x, *refs):
    weights, (keep, send) = refs[: -2 - squares], refs[-2:]
    half = keep.shape[1]
    count = len(weights) // 2
    base = 2 * pl.program_id(0) if squares else 0
    for i in range(2):
        w = jnp.concatenate([w[0] for w in weights[i * count : (i + 1) * count]], axis=0)
        part = jnp.dot(x[...], w, preferred_element_type=F32)
        keep[base + i] = part[:half]
        send[base + i] = part[half:].astype(BF16)
    if squares:

        @pl.when(pl.program_id(0) == 0)
        def _():
            group = keep.shape[0] - 1
            keep[group] = jnp.zeros(keep.shape[1:], F32)
            send[group] = jnp.zeros(send.shape[1:], BF16)
            total = refs[-3][...]
            lane = lax.broadcasted_iota(jnp.int32, (half, LANES), 1)
            keep[group, :, :LANES] = jnp.where(lane < LANES // 2, total[:half], 0.0)
            send[group, :, :LANES] = split_square(total[half:])


def halve_kernel(squares, keep, recv, kept, send):
    half = kept.shape[1]
    body = keep.shape[0] - squares
    kept[...] = keep[:, :half, :] + recv[:, :half, :].astype(F32)
    send[:body] = (keep[:body, half:, :] + recv[:body, half:, :].astype(F32)).astype(BF16)
    if squares:
        total = keep[body, half:, :LANES] + recv[body, half:, :LANES].astype(F32)
        send[body] = jnp.zeros(send.shape[1:], BF16)
        send[body, :, :LANES] = split_square(join_square(total))


def hidden_kernel(squares, keep, recv, *refs):
    if squares:
        hidden, scale_ref = refs
        group = keep.shape[0] - 1
        total = keep[group, :, :LANES] + recv[group, :, :LANES].astype(F32)
        scale_ref[...] = lax.rsqrt(join_square(total) / D + EPSILON)
    else:
        scale_ref, hidden = refs
    scale = scale_ref[:, :1]
    width = keep.shape[2]
    for i in range(keep.shape[0] // 2):
        gate = (keep[2 * i] + recv[2 * i].astype(F32)) * scale
        up = (keep[2 * i + 1] + recv[2 * i + 1].astype(F32)) * scale
        hidden[:, i * width : (i + 1) * width] = (
            gate / (1.0 + jnp.exp(-gate)) * up
        ).astype(BF16)


def join_kernel(first, second, out):
    rows = first.shape[0]
    out[:rows] = first[...]
    out[rows:] = second[...]


def pack_kernel(*refs):
    parts, out = refs[:-1], refs[-1]
    for i, part in enumerate(parts):
        out[i] = part[...]


def output_kernel(stream, gain, *refs):
    parts, out = refs[:-1], refs[-1]
    total = stream[...].astype(F32)
    for part in parts:
        total = total + part[...].astype(F32)
    out[...] = (total * gain[...]).astype(BF16)


def down_kernel(sources, count, added, unit, rows, offsets, *refs):
    own, other, before = refs[:count], refs[count : 2 * count], refs[2 * count : 2 * count + added]
    outs, total = refs[-rows - 1 : -1], refs[-1]
    weights = refs[2 * count + added : -rows - 1]
    tile = len(weights) * weights[0].shape[1]
    for i, (which, at) in enumerate(sources):

        @pl.when(pl.program_id(0) == i)
        def _():
            hidden = jnp.concatenate(
                [own[which][:, at : at + tile], other[which][:, at : at + tile]], axis=0
            )
            w = jnp.concatenate([w[0] for w in weights], axis=0)
            part = jnp.dot(hidden, w, preferred_element_type=F32)
            if i > 0:
                part = part + total[...]
            elif added:
                part = part + before[0][...]
            total[...] = part

    @pl.when(pl.program_id(0) == len(sources) - 1)
    def _():
        step = 0
        for out in outs:
            for first in range(0, out.shape[0], unit):
                place = pl.multiple_of(offsets[step], unit)
                out[first : first + unit, :] = total[pl.ds(place, unit), :].astype(out.dtype)
                step += 1


def head_kernel(rows, first, col_index, row_places, *refs):
    own, other = refs[:rows], refs[rows : 2 * rows]
    gains, target, *weights = refs[2 * rows : -6]
    out, lhs, square, top, total, picked = refs[-6:]
    step = pl.program_id(0)
    chips, unit, width = own[0].shape

    @pl.when(step == 0)
    def _():
        inverse = 1.0 / gains[...]
        for i in range(rows):
            place = pl.multiple_of(row_places[i], unit)
            sums = jnp.zeros((unit, width), F32)
            for core, arrays in enumerate((own, other)):
                for j in range(chips):
                    feature = pl.multiple_of(col_index[2 * j + core] * width, LANES)
                    values = arrays[i][j]
                    lhs[pl.ds(place, unit), pl.ds(feature, width)] = values
                    plain = values.astype(F32) * inverse[2 * j + core : 2 * j + core + 1, :]
                    sums += plain * plain
            square[pl.ds(place, unit), :] = jnp.sum(sums, axis=1, keepdims=True)
        top[...] = jnp.full_like(top, MASKED)
        total[...] = jnp.zeros_like(total)
        picked[...] = jnp.zeros_like(picked)

    depth = weights[0].shape[0]
    logits = jnp.dot(lhs[:, :depth], weights[0][...], preferred_element_type=F32)
    for i in range(1, len(weights)):
        logits += jnp.dot(
            lhs[:, i * depth : (i + 1) * depth], weights[i][...], preferred_element_type=F32
        )
    logits = logits * lax.rsqrt(square[...] / D + EPSILON)
    lane = lax.broadcasted_iota(jnp.int32, logits.shape, 1)
    lane = lane + (step + first) * logits.shape[1]
    hit = jnp.where(lane == target[...], logits, 0.0)
    picked[...] += jnp.sum(hit, axis=1, keepdims=True)
    new_top = jnp.maximum(top[...], jnp.max(logits, axis=1, keepdims=True))
    total[...] = total[...] * jnp.exp(top[...] - new_top) + jnp.sum(
        jnp.exp(logits - new_top), axis=1, keepdims=True
    )
    top[...] = new_top

    @pl.when(step == pl.num_programs(0) - 1)
    def _():
        place = lax.broadcasted_iota(jnp.int32, out.shape, 1)
        out[...] = jnp.where(
            place == 0, top[...], jnp.where(place == 1, total[...], picked[...])
        )


def hold(arrays, token):
    def kernel(*refs):
        del refs

    count = len(arrays)
    results = pl.pallas_call(
        kernel,
        out_shape=[jax.ShapeDtypeStruct(array.shape, array.dtype) for array in arrays]
        + [jax.ShapeDtypeStruct((8, LANES), F32)],
        in_specs=[ANY] * (count + 1),
        out_specs=[ANY] * (count + 1),
        input_output_aliases={i: i for i in range(count)},
        compiler_params=params(16),
        cost_estimate=cost(0, 0),
        name="hold",
    )(*arrays, token[0])
    token[:] = [results[-1]]
    return results[:-1]


def per_device(
    residual,
    attn_gain,
    w_query,
    w_key,
    w_value,
    w_out,
    mlp_gain,
    w_gate,
    w_up,
    w_down,
    final_gain,
    w_head,
    seq_lengths,
    targets,
):
    row_count = lax.axis_size("row")
    col_count = lax.axis_size("col")
    chips = col_count // 2
    row_index = lax.axis_index("row")
    col_index = lax.axis_index("col")
    core = col_index % 2
    chip = col_index // 2
    row_tokens, features = residual.shape
    tokens = row_tokens * row_count
    col_tokens = tokens // col_count
    quarter = tokens // 4
    heads = w_query.shape[1] // HEAD_DIM
    kv_heads = w_key.shape[1] // HEAD_DIM
    qkv_width = w_query.shape[1] + 2 * w_key.shape[1]
    rotated = w_query.shape[1] + w_key.shape[1]
    ff_local = w_gate.shape[2]
    vocab_local = w_head.shape[1]

    row_range = jnp.arange(row_count, dtype=jnp.int32)
    col_range = jnp.arange(col_count, dtype=jnp.int32)
    row_rel = row_range ^ row_index
    col_rel = col_range ^ col_index

    token_index = jnp.arange(tokens, dtype=jnp.int32)
    segment, positions = sequence_layout(seq_lengths, token_index)
    block = min(64, tokens)
    window = min(tokens, block + LONGEST)
    first_key = jnp.maximum(0, (token_index // block + 1) * block - window)
    key_index = first_key[:, None] + jnp.arange(window, dtype=jnp.int32)[None, :]
    key_segment, _ = sequence_layout(seq_lengths, key_index.reshape(-1))
    allowed = (key_segment.reshape(tokens, window) == segment[:, None]) & (
        key_index <= token_index[:, None]
    )
    bias = jnp.where(allowed, 0.0, MASKED).astype(F32)
    own_positions = lax.dynamic_slice_in_dim(positions, col_index * col_tokens, col_tokens)
    exponent = jnp.arange(HEAD_DIM // 2, dtype=F32) * 2.0 / HEAD_DIM
    angles = own_positions[:, None] * (ROPE_BASE ** (-exponent))[None, :]
    cosine, sine = jnp.cos(angles), jnp.sin(angles)
    cosine = jnp.concatenate([cosine, cosine], axis=1)
    sine = jnp.concatenate([-sine, sine], axis=1)

    blocks = [residual] + [row_xor(residual, j) for j in range(1, row_count)]
    shape = jax.ShapeDtypeStruct

    per_row = row_tokens // col_tokens
    col_block = (row_rel[:, None] * per_row + jnp.arange(per_row, dtype=jnp.int32)).reshape(-1)
    relative = col_block ^ col_index
    offsets = ((relative & 1) * chips + (relative >> 1)) * col_tokens
    half = tokens // 2
    wide = qkv_width + LANES
    keep, send = pl.pallas_call(
        functools.partial(qkv_kernel, col_tokens, row_count),
        out_shape=[shape((half, wide), F32), shape((half, wide), BF16)],
        in_specs=[SMEM] + [VMEM] * (row_count + 4),
        out_specs=[VMEM] * 2,
        scratch_shapes=[pltpu.VMEM((tokens, features), BF16), pltpu.VMEM((tokens, LANES), F32)],
        compiler_params=params(56),
        cost_estimate=cost(
            2 * tokens * features * qkv_width, 2 * qkv_width * (features + tokens)
        ),
        name="qkv_partial",
    )(offsets, *blocks, attn_gain[None, :], w_query, w_key, w_value)
    received = col_xor(send, 1)
    parts = pl.pallas_call(
        core_add_kernel,
        out_shape=[shape((col_tokens, wide), F32 if i == 0 else BF16) for i in range(chips)],
        in_specs=[VMEM] * 2,
        out_specs=[VMEM] * chips,
        compiler_params=params(16),
        cost_estimate=cost(half * qkv_width, 6 * half * qkv_width),
        name="qkv_core_add",
    )(keep, received)
    parts = [parts[0]] + [col_xor(parts[j], 2 * j) for j in range(1, chips)]
    mine = pl.pallas_call(
        functools.partial(rope_kernel, rotated, chips),
        out_shape=shape((col_tokens, qkv_width), BF16),
        in_specs=[VMEM] * (chips + 2),
        out_specs=VMEM,
        compiler_params=params(16),
        cost_estimate=cost(8 * col_tokens * qkv_width, 2 * tokens * qkv_width),
        name="qkv_rope",
    )(*parts, cosine, sine)
    pieces = [mine] + [col_xor(mine, 2 * j) for j in range(1, chips)]
    pieces = pieces + [col_xor(piece, 1) for piece in pieces]
    piece_index = [2 * j for j in range(chips)] + [2 * j + 1 for j in range(chips)]
    places = (jnp.array(piece_index, jnp.int32) ^ col_index) * col_tokens

    projected = pl.pallas_call(
        functools.partial(attention_kernel, heads, kv_heads, col_count, block),
        out_shape=[
            shape((row_tokens, features), F32 if i == 0 else BF16) for i in range(row_count)
        ],
        in_specs=[SMEM] * 2 + [VMEM] * (col_count + 2),
        out_specs=[VMEM] * row_count,
        scratch_shapes=[
            pltpu.VMEM((tokens, qkv_width), BF16),
            pltpu.VMEM((tokens, heads * HEAD_DIM), BF16),
        ],
        compiler_params=params(32),
        cost_estimate=cost(
            2 * tokens * heads * HEAD_DIM * features * 2, 2 * heads * HEAD_DIM * features * 2
        ),
        name="attention_out",
    )(places, row_rel * row_tokens, *pieces, bias, w_out)
    projected = [projected[0]] + [row_xor(projected[j], j) for j in range(1, row_count)]
    stream = residual.astype(F32) + tree_sum([p.astype(F32) for p in projected])
    scaled_stream = (stream * mlp_gain[None, :]).astype(BF16)

    levels = (col_count - 1).bit_length()
    blocks = [scaled_stream] + [row_xor(scaled_stream, j) for j in range(1, row_count)]
    position = sum(((relative >> level) & 1) << (levels - 1 - level) for level in range(levels))
    half_offsets = position * col_tokens
    token = [mlp_gain]
    mlp_in, squares = call(
        functools.partial(arrange_kernel, col_tokens),
        [half_offsets, *blocks, mlp_gain[None, :]],
        [SMEM] + [VMEM] * (row_count + 1),
        token,
        out_shape=[
            shape((tokens, features), BF16),
            shape((tokens, LANES), F32),
        ],
        out_specs=[VMEM] * 2,
        compiler_params=params(16),
        cost_estimate=cost(tokens * features, 4 * tokens * features),
        name="mlp_in",
    )

    divisible = ff_local % (3 * LANES) == 0
    tile = ff_local // 3 if divisible else ff_local
    tiles = ff_local // tile
    sub = tile // 3 if tile % (3 * LANES) == 0 else tile
    subs = tile // sub
    plan = [(0, 0, 1), (1, 0, 1)]
    if divisible:
        plan = [(0, 0, 1), (0, 1, 2), (1, 0, 2), (1, 2, 1)]
    last = levels - 1
    keeps, arrivals, hiddens = {}, {}, {}
    scale = []
    states = {}

    def gate_up(j):
        member, first, count = plan[j]
        first = first * subs
        squared = j == 0
        groups = 2 * count * subs + squared
        weights = [
            pl.BlockSpec((1, features // 2, sub), lambda i, q=q: (member, q, first + i))
            for q in range(2)
        ]
        whole = pl.BlockSpec((tokens, features), lambda i: (0, 0))
        if squared:
            out = pl.BlockSpec((groups, half, sub), lambda i: (0, 0, 0))
        else:
            out = pl.BlockSpec((2, half, sub), lambda i: (i, 0, 0))
        keep, send = call(
            functools.partial(gate_up_kernel, squared),
            [mlp_in, w_gate, w_gate, w_up, w_up] + [squares] * squared,
            [whole] + weights * 2 + [pl.BlockSpec((tokens, LANES), lambda i: (0, 0))] * squared,
            token,
            grid=(count * subs,),
            out_shape=[shape((groups, half, sub), F32), shape((groups, half, sub), BF16)],
            out_specs=[out] * 2,
            compiler_params=params(GATE_MIB),
            cost_estimate=cost(4 * tokens * features * tile * count, 4 * tile * count * features),
            name="gate_up",
        )
        keeps[j], arrivals[j] = keep, col_xor(send, 1)

    def halve(j, level):
        count = 1 if j == 0 else plan[j][2]
        keep = keeps[j]
        groups, rows, _ = keep.shape
        part = groups // count
        keeps[j], send = call(
            functools.partial(halve_kernel, j == 0),
            [keep, arrivals[j]],
            [pl.BlockSpec((part, rows, sub), lambda i: (i, 0, 0))] * 2,
            token,
            grid=(count,),
            out_shape=[
                shape((groups, rows // 2, sub), F32),
                shape((groups, rows // 2, sub), BF16),
            ],
            out_specs=[pl.BlockSpec((part, rows // 2, sub), lambda i: (i, 0, 0))] * 2,
            compiler_params=params(24),
            cost_estimate=cost(rows * sub * groups, 9 * rows * sub * groups),
            name="halve",
        )
        arrivals[j] = col_xor(send, 2 << level)

    def hidden_of(j):
        groups, rows, _ = keeps[j].shape
        squared = j == 0
        hidden_shape = shape((rows, groups // 2 * sub), BF16)
        operands = [keeps[j], arrivals[j]] + ([] if squared else scale)
        hidden, *extra = call(
            functools.partial(hidden_kernel, squared),
            operands,
            [VMEM] * len(operands),
            token,
            out_shape=[hidden_shape] + [shape((rows, LANES), F32)] * squared,
            out_specs=[VMEM] * (1 + squared),
            compiler_params=params(24),
            cost_estimate=cost(8 * rows * groups * sub, 6 * rows * groups * sub),
            name="hidden",
        )
        if squared:
            scale[:] = extra
        hiddens[j] = (hidden, col_xor(hidden, 1 << last))

    def join(j, level):
        first, second = hiddens[j]
        rows, width = first.shape
        (joined,) = call(
            join_kernel,
            [first, second],
            [VMEM] * 2,
            token,
            out_shape=[shape((2 * rows, width), BF16)],
            out_specs=[VMEM],
            compiler_params=params(16),
            cost_estimate=cost(rows * width, 8 * rows * width),
            name="join",
        )
        hiddens[j] = (joined, col_xor(joined, 1 << level))

    partial = {0: [], 1: []}
    summed = {0: [], 1: []}

    def down(member, early=False):
        which = [j for j in range(len(plan)) if plan[j][0] == member and j not in summed[member]]
        if early:
            which = which[:1]
            summed[member] = which
        own = [hiddens[j][0] for j in which]
        other = [hiddens[j][1] for j in which]
        sources = [(k, i * tile) for k, j in enumerate(which) for i in range(plan[j][2])]
        first = plan[which[0]][1]
        before = partial[member]
        count = len(which)
        rows = 0 if early else row_count
        sum_spec = pl.BlockSpec((tokens, features), lambda i: (0, 0))
        sum_shape = shape((tokens, features), F32)
        row_shapes = [
            shape((row_tokens, features), F32 if i == 0 else BF16) for i in range(row_count)
        ]
        parts = call(
            functools.partial(down_kernel, sources, count, len(before), col_tokens, rows),
            [half_offsets, *own, *other, *before] + [w_down] * 3,
            [SMEM]
            + [pl.BlockSpec(array.shape, lambda i: (0, 0)) for array in own + other]
            + [sum_spec] * len(before)
            + [
                pl.BlockSpec((1, tile // 3, features), lambda i, q=q: (member, 3 * (first + i) + q, 0))
                for q in range(3)
            ],
            token,
            grid=(len(sources),),
            out_shape=[sum_shape] if early else row_shapes,
            out_specs=[sum_spec]
            if early
            else [pl.BlockSpec((row_tokens, features), lambda i: (0, 0))] * row_count,
            scratch_shapes=[] if early else [pltpu.VMEM((tokens, features), F32)],
            compiler_params=params(DOWN_MIB),
            cost_estimate=cost(
                2 * tokens * features * ff_local, 2 * ff_local * (features + tokens)
            ),
            name="down",
        )
        if early:
            partial[member] = [parts[0]]
        else:
            states[member] = [parts[0]] + [row_xor(parts[j], j) for j in range(1, row_count)]

    def output(member):
        parts = states[member]
        (scaled,) = call(
            output_kernel,
            [stream, final_gain[None, :], *parts],
            [VMEM] * (2 + row_count),
            token,
            out_shape=[shape((row_tokens, features), BF16)],
            out_specs=[VMEM],
            compiler_params=params(16),
            cost_estimate=cost(8 * row_tokens * features, 16 * row_tokens * features),
            name="output",
        )
        states[member] = [scaled] + [col_xor(scaled, 2 * j) for j in range(1, chips)]

    def pack(member):
        (by_chip,) = call(
            pack_kernel,
            states[member],
            [VMEM] * chips,
            token,
            out_shape=[shape((chips, row_tokens, features), BF16)],
            out_specs=[VMEM],
            compiler_params=params(16),
            cost_estimate=cost(chips * row_tokens * features, 4 * chips * row_tokens * features),
            name="pack",
        )
        other = col_xor(by_chip, 1)
        states[member] = [by_chip, other] + [row_xor(by_chip, j) for j in range(1, row_count)]

    def forward(member):
        by_chip, other, *rows = states[member]
        rows = hold(rows, token)
        states[member] = [by_chip, *rows, other] + [col_xor(array, 1) for array in rows]

    vocab_start = (row_index * col_count + col_index) * vocab_local
    local_targets = (targets - vocab_start)[:, None]
    vocab_tile = 512 if vocab_local % 512 == 0 else vocab_local
    vocab_tiles = vocab_local // vocab_tile
    stats = {0: [], 1: []}

    gain_parts = [final_gain[None, :]]
    small = []

    def gather_gain(level):
        (part,) = hold(gain_parts[-1:], token)
        gain_parts.append(jnp.concatenate([part, col_xor(part, 1 << level)], axis=0))

    def ready():
        small[:] = hold([gain_parts[-1], local_targets, col_rel, row_rel * row_tokens], token)

    def head(member, first, count):
        gains, target, features_at, rows_at = small
        state = states[member]
        (result,) = call(
            functools.partial(head_kernel, row_count, first),
            [features_at, rows_at, *state, gains, target] + [w_head] * HEAD_BLOCKS,
            [SMEM] * 2
            + [pl.BlockSpec(state[0].shape, lambda i: (0, 0, 0))] * (2 * row_count)
            + [pl.BlockSpec(gains.shape, lambda i: (0, 0))]
            + [pl.BlockSpec((tokens, 1), lambda i: (0, 0))]
            + [
                pl.BlockSpec((D // HEAD_BLOCKS, vocab_tile), lambda i, q=q: (q, first + i))
                for q in range(HEAD_BLOCKS)
            ],
            token,
            grid=(count,),
            out_shape=[shape((tokens, LANES), F32)],
            out_specs=[pl.BlockSpec((tokens, LANES), lambda i: (0, 0))],
            scratch_shapes=[pltpu.VMEM((tokens, D), BF16)] + [pltpu.VMEM((tokens, 1), F32)] * 4,
            compiler_params=params(HEAD_MIB),
            cost_estimate=cost(
                2 * tokens * D * vocab_tile * count, 2 * D * vocab_tile * count
            ),
            name="head",
        )
        stats[member].append(result[:, :3].T)

    if divisible and levels == 3:
        schedule = [
            (gate_up, 0), (gate_up, 1), (halve, 0, 0), (gate_up, 2), (halve, 1, 0),
            (halve, 0, 1), (gate_up, 3), (halve, 2, 0), (hidden_of, 0), (halve, 1, 1),
            (join, 0, 1), (halve, 3, 0), (hidden_of, 1), (halve, 2, 1), (halve, 3, 1),
            (join, 1, 1), (gather_gain, 0), (hidden_of, 2), (join, 1, 0), (join, 0, 0),
            (gather_gain, 1), (hidden_of, 3), (join, 2, 1), (gather_gain, 2), (join, 3, 1),
            (ready,), (down, 0), (join, 2, 0), (down, 1, True), (join, 3, 0), (down, 1),
            (output, 0), (output, 1), (pack, 0), (pack, 1), (forward, 0),
            (head, 0, 0, vocab_tiles), (forward, 1), (head, 1, 0, vocab_tiles),
        ]
    else:
        schedule = []
        for j in range(len(plan)):
            schedule += [(gate_up, j)] + [(halve, j, level) for level in range(last)]
            schedule += [(hidden_of, j)] + [(join, j, level) for level in range(last - 1, -1, -1)]
        schedule += [(gather_gain, level) for level in range(levels)] + [(ready,)]
        schedule += [(down, 0), (output, 0), (down, 1), (output, 1), (pack, 0), (pack, 1)]
        schedule += [(forward, 0), (forward, 1), (head, 0, 0, vocab_tiles)]
        schedule += [(head, 1, 0, vocab_tiles)]
    for step, *arguments in schedule:
        step(*arguments)

    def combine(parts):
        top = functools.reduce(jnp.maximum, [p[0] for p in parts])
        total = tree_sum([p[1] * jnp.exp(p[0] - top) for p in parts])
        picked = tree_sum([p[2] for p in parts])
        return jnp.stack([top, total, picked])

    merged = combine(stats[0]) if len(stats[0]) > 1 else stats[0][0]
    merged = jnp.stack([merged, stats[1][0]], axis=1)
    for level in range(levels):
        merged = combine([merged, col_xor(merged, 1 << level)])
    for level in range((row_count - 1).bit_length()):
        merged = combine([merged, row_xor(merged, 1 << level)])
    logprob = merged[2] - (merged[0] + jnp.log(merged[1]))
    difference = logprob[0] - logprob[1]
    one_hot = (segment[:, None] == jnp.arange(SEQS, dtype=jnp.int32)[None, :]).astype(F32)
    seq_sums = jnp.dot(difference, one_hot, precision=lax.Precision.HIGHEST)
    return seq_sums / seq_lengths.astype(F32)


def solution(mesh):
    placed = (
        P("row", "col"),
        P("col"),
        P("col", "row"),
        P("col", "row"),
        P("col", "row"),
        P("row", "col"),
        P("col"),
        P(None, "col", "row"),
        P(None, "col", "row"),
        P(None, "row", "col"),
        P("col"),
        P(None, ("row", "col")),
        P(),
        P(),
    )
    return jax.shard_map(per_device, mesh=mesh, in_specs=placed, out_specs=P(), check_vma=False)
```
